32 devices in a mesh: shard: 8 (over z, y), rep: 4 (over x, core).
Axes of the slice: x: 2, y: 2, z: 4, core: 2. Of those that a mesh axis runs over, the one named last changes fastest.
Arguments:
- feature_table: bfloat16 [2048, 1024], P('shard'), may hold values from -8 to 8
- projection: bfloat16 [1024, 1024], replicated, may hold values from -0.1875 to 0.1875
- slot_owner: int32 [1024, 16, 1], P(('shard', 'rep')), may hold values from 0 to 7; in each aligned block of 512 rows (0 to 511, 512 to 1023, ..., all dimensions but the last counted through in order) at most 128 rows name the same one
- slot_row: int32 [1024, 16], P(('shard', 'rep')), may hold values from 0 to 255
- visits: int32 [1024, 13], P(('shard', 'rep')), may hold values from 1 to 32
- neg_row: int32 [512], P('shard'), may hold values from 0 to 255
Outputs:
- table_grad: float32 [2048, 1024], P('shard')
The draws below stay inside these ranges and needn't reach their ends.
Inputs may be any that keep to these rules, and one draw needn't show every extreme that they name: `slot_owner`: within the slots of one device's 32 queries (aligned blocks of 512 slots in order), no shard index is named more than 128 times, a bound that some block reaches. `neg_row`: negative j lies in the rows of shard index j // 64.
All inputs are finite; a program needn't handle non-finite values.
Results may differ from the reference program's by a relative error of at most 0.006.
Values may be sent and summed in bfloat16 or wider, within the bound.
A program may use at most 64 MiB of HBM per device.

```python
import math
import jax
import jax.numpy as jnp
import numpy as np
from jax import lax

F = 1024
E = 1024
ROWS_DEV = 256
Q_DEV = 32
SLOTS = 16
NEG = 512
NODES = 2048
QUERIES = 1024
CAP = 128
NEG_DEV = 64
N_SHARD = 8


group_total = 16


def draw_feature_table(key, part):
    base = jax.random.fold_in(key, 4111)
    keys = jax.random.split(base, 2)
    member = jnp.arange(NODES, dtype=jnp.int32) % group_total
    centres = jax.random.normal(keys[0], (group_total, F), jnp.float32)
    noise = jax.random.normal(keys[1], (NODES, F), jnp.float32)
    table = centres[member] + noise
    return jnp.clip(table, -8.0, 8.0).astype(jnp.bfloat16)


def draw_slot_row(key, part):
    base = jax.random.fold_in(key, 7237)
    keys = jax.random.split(base, 6)
    span = ROWS_DEV // group_total
    home = jax.random.randint(keys[0], (QUERIES, 1), 0, group_total)
    first = jax.random.randint(keys[1], (QUERIES, SLOTS), 0, span)
    second = jax.random.randint(keys[2], (QUERIES, SLOTS), 0, span)
    within = jnp.minimum(first, second)
    stray = jax.random.randint(keys[3], (QUERIES, SLOTS), 0, group_total)
    stays = jax.random.randint(keys[4], (QUERIES, SLOTS), 0, 4) > 0
    offset = jax.random.randint(keys[5], (QUERIES, 1), 1, group_total)
    slot_index = jnp.arange(SLOTS, dtype=jnp.int32)[None, :]
    member = jnp.where(slot_index < 2, home, jnp.where(slot_index == 2, (home + offset) % group_total, jnp.where(stays, home, stray)))
    return (within * group_total + member).astype(jnp.int32)


def plant(result, own_key, smallest, largest):
    extent = result.shape
    place = [jax.random.randint(jax.random.fold_in(own_key, axis), (), 0, extent[axis]) for axis in range(len(extent))]
    result = result.at[tuple(place)].set(smallest)
    longest = extent.index(max(extent))
    place[longest] = (place[longest] + 1) % extent[longest]
    return result.at[tuple(place)].set(largest)


def routed_block(rng, own, number, rows, number_of, top, bound, lean):
    ranking = jax.random.permutation(rng, number_of)
    packed, common = shares(number_of, rows * top, bound, lean, True), shares(number_of, rows * top, bound, lean, False)
    places = jnp.arange(number_of)

    def named(tallies, rotation):
        used = int((tallies > 0).sum())
        fixed = max(1, used // 4)
        passed = fixed + (places - fixed + rotation * (used - fixed)) % max(1, number_of - fixed)
        return jnp.zeros((number_of,), jnp.int32).at[ranking[jnp.where(places < fixed, places, passed)]].set(jnp.asarray(tallies, jnp.int32))

    tallies = jnp.where(number % 4 == 0, named(packed, number // 4), named(common, number - number // 4 - 1))
    mixed = jax.random.permutation(jax.random.fold_in(own, 3), number_of)
    giver, taker = mixed[0:number_of // 2 * 2:2], mixed[1:number_of // 2 * 2:2]
    room = jnp.minimum(tallies[giver] - 1, bound - tallies[taker]) // 2
    room = jnp.where((giver == ranking[0]) | (taker == ranking[0]) | (tallies[taker] == 0), 0, jnp.maximum(room, 0))
    passed = jax.random.randint(jax.random.fold_in(own, 4), (number_of // 2,), 0, 1 << 20) % (room + 1)
    tallies = tallies.at[giver].add(-passed).at[taker].add(passed)
    members = jnp.searchsorted(jnp.cumsum(tallies), jnp.arange(rows * top), side="right").astype(jnp.int32)
    table = members.reshape(top, rows).T
    table = table[jax.random.permutation(jax.random.fold_in(own, 1), rows)]
    rotation = jax.random.randint(jax.random.fold_in(own, 2), (rows, 1), 0, top)
    return jnp.take_along_axis(table, (jnp.arange(top)[None, :] + rotation) % top, axis=1)


def shares(amount, total, bound, lean, full):
    weights = [(1 << 20) // math.isqrt(grade ** lean) + 1 for grade in range(1, amount + 1)]
    largest = bound if full else min(bound, max(-(-total // amount), total * weights[0] // sum(weights)))
    least = 1 if total - largest >= amount - 1 else 0
    counts, surplus = [largest] + [least] * (amount - 1), total - largest - least * (amount - 1)
    while surplus > 0:
        candidates = [i for i in range(1, amount) if counts[i] < largest] or [i for i in range(1, amount) if counts[i] < bound]
        pool, left = sum([weights[i] for i in candidates]), surplus
        for i in candidates:
            extra = min(bound - counts[i], max(1, left * weights[i] // pool), surplus)
            counts[i] = counts[i] + extra
            surplus = surplus - extra
    return np.array(counts)


def bell_draw(key, dims, deviation, limit, kind=jnp.bfloat16):
    array = deviation * jax.random.normal(key, dims, jnp.float32)
    return jnp.clip(array, min=-limit, max=limit).astype(kind)


def setup_inputs(seed: int = 0) -> dict:
    splits = jax.random.split(jax.random.key(seed), 7)
    feature_table = draw_feature_table(jax.random.fold_in(splits[6], 71), 0)
    projection = bell_draw(splits[1], (F, E), F ** -0.5, 0.1875)
    slot_owner_keys = jax.random.split(jax.random.fold_in(splits[2], 1), QUERIES * SLOTS // (Q_DEV * SLOTS))
    slot_owner_turns = jax.random.permutation(jax.random.fold_in(splits[2], 3), QUERIES * SLOTS // (Q_DEV * SLOTS))
    slot_owner = jax.vmap(lambda own, number: routed_block(jax.random.fold_in(splits[2], 2), own, number, Q_DEV * SLOTS, N_SHARD, 1, CAP, 2))(slot_owner_keys, slot_owner_turns).reshape((QUERIES, SLOTS, 1))
    slot_row = draw_slot_row(jax.random.fold_in(splits[6], 71), 0)
    visits = plant(jax.random.randint(splits[4], (QUERIES, SLOTS - 3), 1, 33), jax.random.fold_in(splits[4], 1), 1, 32).astype(jnp.int32)
    neg_row = plant(jax.random.randint(splits[5], (NEG,), 0, ROWS_DEV), jax.random.fold_in(splits[5], 1), 0, ROWS_DEV - 1).astype(jnp.int32)
    return {"feature_table": feature_table, "projection": projection, "slot_owner": slot_owner, "slot_row": slot_row, "visits": visits, "neg_row": neg_row}


score_scale = 8.0
margin_value = 0.1
epsilon = 1e-06

def unit_rows(values):
    norms = jnp.sqrt(lax.optimization_barrier(jnp.sum(values * values, axis=-1, keepdims=True)) + epsilon)
    return (values / norms, norms)

def unit_back(grads, unit, norms):
    return (grads - unit * lax.optimization_barrier(jnp.sum(unit * grads, axis=-1, keepdims=True))) / norms

def silu_slope(preact):
    gate_value = jax.nn.sigmoid(preact)
    return gate_value * (1.0 + preact * (1.0 - gate_value))

def reference(feature_table, projection, slot_owner, slot_row, visits, neg_row):
    node_ids = (slot_owner[:, :, 0] * ROWS_DEV + slot_row).astype(jnp.int32)
    neg_ids = (jnp.arange(NEG, dtype=jnp.int32) // NEG_DEV * ROWS_DEV + neg_row).astype(jnp.int32)
    neg_pre = jnp.dot(feature_table[neg_ids], projection, preferred_element_type=jnp.float32)
    neg_unit, neg_norms = unit_rows(jax.nn.silu(neg_pre))
    neg_embed = neg_unit.astype(jnp.bfloat16)
    visit_float = visits.astype(jnp.float32)
    coefs = visit_float / lax.optimization_barrier(jnp.sum(visit_float, axis=1, keepdims=True))
    block = min(QUERIES, 256)
    block_count = QUERIES // block
    node_blocks = node_ids.reshape(block_count, block, SLOTS)
    coef_blocks = coefs.reshape(block_count, block, SLOTS - 3)

    def visit_block(carry, inputs):
        grad_table, neg_grad = carry
        block_nodes, block_coefs = inputs
        gathered = feature_table[block_nodes.reshape(-1)]
        preact = jnp.dot(gathered, projection, preferred_element_type=jnp.float32).reshape(block, SLOTS, E)
        active = jax.nn.silu(preact)
        hood = active[:, 0] + jnp.einsum('bk,bke->be', block_coefs, active[:, 3:])
        query_unit, query_norms = unit_rows(hood)
        query_embed = query_unit.astype(jnp.bfloat16)
        item_unit, item_norms = unit_rows(active[:, 1:3])
        item_embed = item_unit.astype(jnp.bfloat16)
        query_float = query_embed.astype(jnp.float32)
        item_float = item_embed.astype(jnp.float32)
        neg_scores = jnp.dot(query_embed, neg_embed.T, preferred_element_type=jnp.float32)
        pair_scores = jnp.einsum('be,bse->bs', query_float, item_float)
        positive = pair_scores[:, 0:1]
        neg_weight = (score_scale * jax.nn.sigmoid(score_scale * (neg_scores - positive + margin_value))).astype(jnp.bfloat16)
        hard_weight = (score_scale * jax.nn.sigmoid(score_scale * (pair_scores[:, 1:2] - positive + margin_value))).astype(jnp.bfloat16)
        hard_float = hard_weight.astype(jnp.float32)
        total_weight = lax.optimization_barrier(jnp.sum(neg_weight.astype(jnp.float32), axis=1, keepdims=True)) + hard_float
        query_grad = jnp.dot(neg_weight, neg_embed, preferred_element_type=jnp.float32) + hard_float * item_float[:, 1] - total_weight * item_float[:, 0]
        item_grad = jnp.stack([-total_weight * query_float, hard_float * query_float], axis=1)
        neg_grad = neg_grad + jnp.dot(neg_weight.T, query_embed, preferred_element_type=jnp.float32)
        hood_grad = unit_back(query_grad, query_unit, query_norms)
        item_back = unit_back(item_grad, item_unit, item_norms)
        active_grad = jnp.concatenate([hood_grad[:, None], item_back, block_coefs[:, :, None] * hood_grad[:, None]], axis=1)
        preact_grad = (active_grad * silu_slope(preact)).astype(jnp.bfloat16)
        row_grads = jnp.dot(preact_grad.reshape(block * SLOTS, E), projection.T, preferred_element_type=jnp.float32)
        grad_table = grad_table.at[block_nodes.reshape(-1)].add(row_grads)
        return ((grad_table, neg_grad), None)
    start = (jnp.zeros((NODES, F), jnp.float32), jnp.zeros((NEG, E), jnp.float32))
    (grad_table, neg_grad), unused = lax.scan(visit_block, start, (node_blocks, coef_blocks))
    neg_back = unit_back(neg_grad, neg_unit, neg_norms)
    neg_pre_grad = (neg_back * silu_slope(neg_pre)).astype(jnp.bfloat16)
    neg_rows = jnp.dot(neg_pre_grad, projection.T, preferred_element_type=jnp.float32)
    return grad_table.at[neg_ids].add(neg_rows)
```

```python
import jax
import jax.numpy as jnp
from jax import lax
from jax.sharding import PartitionSpec as P

score_scale = 8.0
margin_value = 0.1
epsilon = 1e-06


def unit_rows(values):
    norms = jnp.sqrt(jnp.sum(values * values, axis=-1, keepdims=True) + epsilon)
    return (values / norms, norms)


def unit_back(grads, unit, norms):
    return (grads - unit * jnp.sum(unit * grads, axis=-1, keepdims=True)) / norms


def silu_slope(preact):
    gate_value = jax.nn.sigmoid(preact)
    return gate_value * (1.0 + preact * (1.0 - gate_value))


def times_back(left, projection):
    return jnp.einsum("re,fe->rf", left, projection, preferred_element_type=jnp.float32)


def on_device(feature_table, projection, slot_owner, slot_row, visits, neg_row):
    shard_count = lax.axis_size("shard")
    query_count, slot_count = slot_row.shape
    row_count = query_count * slot_count
    capacity = 2 * row_count // shard_count
    feat_width = projection.shape[0]
    embed_width = projection.shape[1]
    owners = slot_owner.reshape(row_count)
    one_hot = (owners[:, None] == jnp.arange(shard_count, dtype=jnp.int32)[None, :]).astype(
        jnp.int32
    )
    earlier = jnp.cumsum(one_hot, axis=0) - one_hot
    slot_rank = jnp.sum(earlier * one_hot, axis=1)
    position = owners * capacity + slot_rank
    send_ids = (
        jnp.zeros((shard_count * capacity,), jnp.int32)
        .at[position]
        .set(slot_row.reshape(row_count))
    )
    send_ids = send_ids.reshape(shard_count, capacity)
    asked = lax.all_to_all(send_ids, "shard", split_axis=0, concat_axis=0, tiled=True)
    picked = feature_table[asked]
    fetched = lax.all_to_all(picked, "shard", split_axis=0, concat_axis=0, tiled=True)
    gathered = fetched.reshape(shard_count * capacity, feat_width)[position]
    neg_pre = jnp.dot(feature_table[neg_row], projection, preferred_element_type=jnp.float32)
    neg_unit, neg_norms = unit_rows(jax.nn.silu(neg_pre))
    neg_embed = lax.all_gather(neg_unit.astype(jnp.bfloat16), "shard", axis=0, tiled=True)
    visit_float = visits.astype(jnp.float32)
    coefs = visit_float / jnp.sum(visit_float, axis=1, keepdims=True)
    preact = jnp.dot(gathered, projection, preferred_element_type=jnp.float32).reshape(
        query_count, slot_count, embed_width
    )
    active = jax.nn.silu(preact)
    hood = active[:, 0] + jnp.einsum("bk,bke->be", coefs, active[:, 3:])
    query_unit, query_norms = unit_rows(hood)
    query_embed = query_unit.astype(jnp.bfloat16)
    item_unit, item_norms = unit_rows(active[:, 1:3])
    item_embed = item_unit.astype(jnp.bfloat16)
    query_float = query_embed.astype(jnp.float32)
    item_float = item_embed.astype(jnp.float32)
    neg_scores = jnp.einsum("be,ne->bn", query_embed, neg_embed, preferred_element_type=jnp.float32)
    pair_scores = jnp.sum(query_float[:, None, :] * item_float, axis=2)
    positive = pair_scores[:, 0:1]
    neg_weight = (
        score_scale * jax.nn.sigmoid(score_scale * (neg_scores - positive + margin_value))
    ).astype(jnp.bfloat16)
    hard_weight = (
        score_scale * jax.nn.sigmoid(score_scale * (pair_scores[:, 1:2] - positive + margin_value))
    ).astype(jnp.bfloat16)
    hard_float = hard_weight.astype(jnp.float32)
    total_weight = jnp.sum(neg_weight.astype(jnp.float32), axis=1, keepdims=True) + hard_float
    query_grad = (
        jnp.dot(neg_weight, neg_embed, preferred_element_type=jnp.float32)
        + hard_float * item_float[:, 1]
        - total_weight * item_float[:, 0]
    )
    item_grad = jnp.stack([-total_weight * query_float, hard_float * query_float], axis=1)
    neg_partial = jnp.einsum(
        "bn,be->ne", neg_weight, query_embed, preferred_element_type=jnp.float32
    )
    hood_grad = unit_back(query_grad, query_unit, query_norms)
    item_back = unit_back(item_grad, item_unit, item_norms)
    active_grad = jnp.concatenate(
        [hood_grad[:, None], item_back, coefs[:, :, None] * hood_grad[:, None]], axis=1
    )
    preact_grad = (
        (active_grad * silu_slope(preact)).astype(jnp.bfloat16).reshape(row_count, embed_width)
    )
    outgoing = (
        jnp.zeros((shard_count * capacity, embed_width), jnp.bfloat16).at[position].set(preact_grad)
    )
    incoming = lax.all_to_all(
        outgoing.reshape(shard_count, capacity, embed_width),
        "shard",
        split_axis=0,
        concat_axis=0,
        tiled=True,
    )
    contrib = times_back(incoming.reshape(shard_count * capacity, embed_width), projection)
    neg_sum = lax.psum_scatter(neg_partial, "shard", scatter_dimension=0, tiled=True)
    grad_local = (
        jnp.zeros((feature_table.shape[0], feat_width), jnp.float32)
        .at[asked.reshape(-1)]
        .add(contrib)
    )
    grad_local, neg_total = lax.psum((grad_local, neg_sum), "rep")
    neg_back = unit_back(neg_total, neg_unit, neg_norms)
    neg_pre_grad = (neg_back * silu_slope(neg_pre)).astype(jnp.bfloat16)
    neg_rows = times_back(neg_pre_grad, projection)
    return grad_local.at[neg_row].add(neg_rows)


def row_picks(info, slot_count, node_count):
    rows = info.shape[0]
    ids = info[:, :slot_count]
    visits = info[:, slot_count:]
    lane = lax.broadcasted_iota(jnp.int32, (rows, node_count), 1)
    singles = [(ids[:, s : s + 1] == lane).astype(jnp.bfloat16) for s in range(3)]
    spread = jnp.zeros((rows, node_count), jnp.float32)
    for k in range(slot_count - 3):
        count = visits[:, k : k + 1].astype(jnp.float32)
        spread = spread + jnp.where(ids[:, 3 + k : 4 + k] == lane, count, 0.0)
    return jnp.concatenate(singles + [spread.astype(jnp.bfloat16)], axis=0)


def column_split(feature_table, projection, slot_owner, slot_row, visits, neg_row):
    shard_count = lax.axis_size("shard")
    rep_count = lax.axis_size("rep")
    query_count, slot_count = slot_row.shape
    node_count = feature_table.shape[0]
    neg_count = neg_row.shape[0]
    embed_width = projection.shape[1]
    width = embed_width // shard_count
    group = query_count * shard_count
    held = node_count + neg_count
    f32, bf16 = jnp.float32, jnp.bfloat16
    node = slot_owner[:, :, 0] * node_count + slot_row
    info = lax.all_gather(jnp.concatenate([node, visits], axis=1), "shard", axis=0, tiled=True)
    neg_pick = (neg_row[:, None] == jnp.arange(node_count, dtype=jnp.int32)[None, :]).astype(bf16)
    neg_feat = jnp.dot(neg_pick, feature_table, preferred_element_type=f32).astype(bf16)
    pre = jnp.dot(
        jnp.concatenate([feature_table, neg_feat], axis=0), projection, preferred_element_type=f32
    )
    act = jax.nn.silu(pre)
    neg_unit, neg_norms = unit_rows(act[node_count:])
    rows = jnp.concatenate([act[:node_count], neg_unit], axis=0).astype(bf16)
    slices = lax.all_to_all(
        rows.reshape(held, shard_count, width).transpose(1, 0, 2), "shard", 0, 0, tiled=True
    )
    act_slice = slices[:, :node_count].reshape(shard_count * node_count, width)
    neg_slice = slices[:, node_count:].reshape(shard_count * neg_count, width)
    picks = row_picks(info, slot_count, shard_count * node_count)
    picked = jnp.dot(picks, act_slice, preferred_element_type=f32)
    total = jnp.sum(info[:, slot_count:].astype(f32), axis=1, keepdims=True)
    own, pos, hard, spread = [picked[i * group : (i + 1) * group] for i in range(4)]
    hood = own + spread / total
    partial = lax.dot_general(
        hood.astype(bf16), neg_slice, (((1,), (1,)), ((), ())), preferred_element_type=f32
    )
    stats = jnp.stack(
        [jnp.sum(a * b, axis=1) for a, b in ((hood, hood), (pos, pos), (hard, hard), (hood, pos), (hood, hard))],
        axis=1,
    )
    parts = lax.all_to_all(
        partial.astype(bf16).reshape(shard_count, query_count, -1), "shard", 0, 0, tiled=True
    )
    stats = lax.all_to_all(
        stats.reshape(shard_count, query_count, -1), "shard", 0, 0, tiled=True
    )
    weight, scalars = loss_weights(
        jnp.sum(parts.astype(f32), axis=0), jnp.sum(stats, axis=0)
    )
    weight = lax.all_gather(weight, "shard", axis=0, tiled=True)
    scalars = lax.all_gather(scalars, "shard", axis=0, tiled=True)
    grads, query_embed = query_side(hood, pos, hard, total, weight, scalars, neg_slice)
    node_part = lax.dot_general(
        picks, grads, (((0,), (0,)), ((), ())), preferred_element_type=f32
    )
    neg_part = lax.dot_general(
        weight, query_embed, (((0,), (0,)), ((), ())), preferred_element_type=f32
    )
    back = jnp.concatenate(
        [
            node_part.astype(bf16).reshape(shard_count, node_count, width),
            neg_part.astype(bf16).reshape(shard_count, neg_count, width),
        ],
        axis=1,
    )
    back = lax.all_to_all(back, "shard", 0, 0, tiled=True)
    back = back.transpose(1, 0, 2).reshape(rep_count, held // rep_count, embed_width)
    back = jnp.sum(lax.all_to_all(back, "rep", 0, 0, tiled=True).astype(f32), axis=0)
    back = lax.all_gather(back.astype(bf16), "rep", axis=0, tiled=True).astype(f32)
    neg_grad = unit_back(back[node_count:], neg_unit, neg_norms)
    neg_grad = (neg_grad * silu_slope(pre[node_count:])).astype(bf16)
    pre_grad = back[:node_count] * silu_slope(pre[:node_count])
    pre_grad = pre_grad + lax.dot_general(
        neg_pick, neg_grad, (((0,), (0,)), ((), ())), preferred_element_type=f32
    )
    return times_back(pre_grad.astype(bf16), projection)


def loss_weights(dots, stats):
    inverse = lax.rsqrt(stats[:, 0:3] + epsilon)
    scores = dots * inverse[:, 0:1]
    positive = stats[:, 3:4] * inverse[:, 0:1] * inverse[:, 1:2]
    hard = stats[:, 4:5] * inverse[:, 0:1] * inverse[:, 2:3]
    weight = score_scale * jax.nn.sigmoid(score_scale * (scores - positive + margin_value))
    weight = weight.astype(jnp.bfloat16)
    wide = weight.astype(jnp.float32)
    hard_weight = score_scale * jax.nn.sigmoid(score_scale * (hard - positive + margin_value))
    hard_weight = hard_weight.astype(jnp.bfloat16).astype(jnp.float32)
    total = jnp.sum(wide, axis=1, keepdims=True) + hard_weight
    along = jnp.sum(wide * scores, axis=1, keepdims=True) + hard_weight * hard - total * positive
    columns = [inverse, hard_weight, total, along, positive, hard]
    return weight, jnp.concatenate(columns, axis=1)


def query_side(hood, pos, hard, visit_total, weight, scalars, neg_slice):
    f32, bf16 = jnp.float32, jnp.bfloat16
    inv_q, inv_p, inv_h, hard_weight, total, along, pos_score, hard_score = [
        scalars[:, i : i + 1] for i in range(8)
    ]
    query_unit, pos_unit, hard_unit = hood * inv_q, pos * inv_p, hard * inv_h
    query_embed = query_unit.astype(bf16)
    query_float = query_embed.astype(f32)
    query_grad = (
        jnp.dot(weight, neg_slice, preferred_element_type=f32)
        + hard_weight * hard_unit.astype(bf16).astype(f32)
        - total * pos_unit.astype(bf16).astype(f32)
    )
    hood_grad = (query_grad - query_unit * along) * inv_q
    pos_grad = -total * (query_float - pos_unit * pos_score) * inv_p
    hard_grad = hard_weight * (query_float - hard_unit * hard_score) * inv_h
    grads = jnp.concatenate([hood_grad, pos_grad, hard_grad, hood_grad / visit_total], axis=0)
    return grads.astype(bf16), query_embed


def solution(mesh):
    def body(feature_table, projection, *rest):
        slice_width = projection.shape[1] // mesh.shape["shard"]
        whole = slice_width >= 128 and slice_width % 128 == 0
        form = column_split if whole else on_device
        return form(feature_table, projection, *rest)

    return jax.shard_map(
        body,
        mesh=mesh,
        in_specs=(
            P("shard", None),
            P(),
            P(("shard", "rep"), None, None),
            P(("shard", "rep"), None),
            P(("shard", "rep"), None),
            P("shard"),
        ),
        out_specs=P("shard", None),
        check_vma=False,
    )
```

```python
import functools

import jax
import jax.numpy as jnp
from jax import lax
from jax.experimental import pallas as pl
from jax.experimental.pallas import tpu as pltpu
from jax.sharding import PartitionSpec as P

MESH = pl.DeviceIdType.MESH

score_scale = 8.0
margin_value = 0.1
epsilon = 1e-06


def unit_rows(values):
    norms = jnp.sqrt(jnp.sum(values * values, axis=-1, keepdims=True) + epsilon)
    return (values / norms, norms)


def unit_back(grads, unit, norms):
    return (grads - unit * jnp.sum(unit * grads, axis=-1, keepdims=True)) / norms


def silu_slope(preact):
    gate_value = jax.nn.sigmoid(preact)
    return gate_value * (1.0 + preact * (1.0 - gate_value))


def times_back(left, projection):
    return jnp.einsum("re,fe->rf", left, projection, preferred_element_type=jnp.float32)


def on_device(feature_table, projection, slot_owner, slot_row, visits, neg_row):
    shard_count = lax.axis_size("shard")
    query_count, slot_count = slot_row.shape
    row_count = query_count * slot_count
    capacity = 2 * row_count // shard_count
    feat_width = projection.shape[0]
    embed_width = projection.shape[1]
    owners = slot_owner.reshape(row_count)
    one_hot = (owners[:, None] == jnp.arange(shard_count, dtype=jnp.int32)[None, :]).astype(
        jnp.int32
    )
    earlier = jnp.cumsum(one_hot, axis=0) - one_hot
    slot_rank = jnp.sum(earlier * one_hot, axis=1)
    position = owners * capacity + slot_rank
    send_ids = (
        jnp.zeros((shard_count * capacity,), jnp.int32)
        .at[position]
        .set(slot_row.reshape(row_count))
    )
    send_ids = send_ids.reshape(shard_count, capacity)
    asked = lax.all_to_all(send_ids, "shard", split_axis=0, concat_axis=0, tiled=True)
    picked = feature_table[asked]
    fetched = lax.all_to_all(picked, "shard", split_axis=0, concat_axis=0, tiled=True)
    gathered = fetched.reshape(shard_count * capacity, feat_width)[position]
    neg_pre = jnp.dot(feature_table[neg_row], projection, preferred_element_type=jnp.float32)
    neg_unit, neg_norms = unit_rows(jax.nn.silu(neg_pre))
    neg_embed = lax.all_gather(neg_unit.astype(jnp.bfloat16), "shard", axis=0, tiled=True)
    visit_float = visits.astype(jnp.float32)
    coefs = visit_float / jnp.sum(visit_float, axis=1, keepdims=True)
    preact = jnp.dot(gathered, projection, preferred_element_type=jnp.float32).reshape(
        query_count, slot_count, embed_width
    )
    active = jax.nn.silu(preact)
    hood = active[:, 0] + jnp.einsum("bk,bke->be", coefs, active[:, 3:])
    query_unit, query_norms = unit_rows(hood)
    query_embed = query_unit.astype(jnp.bfloat16)
    item_unit, item_norms = unit_rows(active[:, 1:3])
    item_embed = item_unit.astype(jnp.bfloat16)
    query_float = query_embed.astype(jnp.float32)
    item_float = item_embed.astype(jnp.float32)
    neg_scores = jnp.einsum("be,ne->bn", query_embed, neg_embed, preferred_element_type=jnp.float32)
    pair_scores = jnp.sum(query_float[:, None, :] * item_float, axis=2)
    positive = pair_scores[:, 0:1]
    neg_weight = (
        score_scale * jax.nn.sigmoid(score_scale * (neg_scores - positive + margin_value))
    ).astype(jnp.bfloat16)
    hard_weight = (
        score_scale * jax.nn.sigmoid(score_scale * (pair_scores[:, 1:2] - positive + margin_value))
    ).astype(jnp.bfloat16)
    hard_float = hard_weight.astype(jnp.float32)
    total_weight = jnp.sum(neg_weight.astype(jnp.float32), axis=1, keepdims=True) + hard_float
    query_grad = (
        jnp.dot(neg_weight, neg_embed, preferred_element_type=jnp.float32)
        + hard_float * item_float[:, 1]
        - total_weight * item_float[:, 0]
    )
    item_grad = jnp.stack([-total_weight * query_float, hard_float * query_float], axis=1)
    neg_partial = jnp.einsum(
        "bn,be->ne", neg_weight, query_embed, preferred_element_type=jnp.float32
    )
    hood_grad = unit_back(query_grad, query_unit, query_norms)
    item_back = unit_back(item_grad, item_unit, item_norms)
    active_grad = jnp.concatenate(
        [hood_grad[:, None], item_back, coefs[:, :, None] * hood_grad[:, None]], axis=1
    )
    preact_grad = (
        (active_grad * silu_slope(preact)).astype(jnp.bfloat16).reshape(row_count, embed_width)
    )
    outgoing = (
        jnp.zeros((shard_count * capacity, embed_width), jnp.bfloat16).at[position].set(preact_grad)
    )
    incoming = lax.all_to_all(
        outgoing.reshape(shard_count, capacity, embed_width),
        "shard",
        split_axis=0,
        concat_axis=0,
        tiled=True,
    )
    contrib = times_back(incoming.reshape(shard_count * capacity, embed_width), projection)
    neg_sum = lax.psum_scatter(neg_partial, "shard", scatter_dimension=0, tiled=True)
    grad_local = (
        jnp.zeros((feature_table.shape[0], feat_width), jnp.float32)
        .at[asked.reshape(-1)]
        .add(contrib)
    )
    grad_local, neg_total = lax.psum((grad_local, neg_sum), "rep")
    neg_back = unit_back(neg_total, neg_unit, neg_norms)
    neg_pre_grad = (neg_back * silu_slope(neg_pre)).astype(jnp.bfloat16)
    neg_rows = times_back(neg_pre_grad, projection)
    return grad_local.at[neg_row].add(neg_rows)


def dot(left, right, left_dim=1, right_dim=0):
    return lax.dot_general(
        left, right, (((left_dim,), (right_dim,)), ((), ())), preferred_element_type=jnp.float32
    )


def lanes_of(columns, width):
    rows = columns[0].shape[0]
    lane = lax.broadcasted_iota(jnp.int32, (rows, width), 1)
    result = jnp.zeros((rows, width), jnp.float32)
    for place, column in enumerate(columns):
        result = jnp.where(lane == place, column, result)
    return result


def loss_weights(dots, stats):
    inverse = lax.rsqrt(stats[:, 0:3] + epsilon)
    inv_q, inv_p, inv_h = inverse[:, 0:1], inverse[:, 1:2], inverse[:, 2:3]
    scores = dots * inv_q
    positive = stats[:, 3:4] * inv_q * inv_p
    hard = stats[:, 4:5] * inv_q * inv_h
    weight = score_scale * jax.nn.sigmoid(score_scale * (scores - positive + margin_value))
    weight = weight.astype(jnp.bfloat16)
    wide = weight.astype(jnp.float32)
    hard_weight = score_scale * jax.nn.sigmoid(score_scale * (hard - positive + margin_value))
    hard_weight = hard_weight.astype(jnp.bfloat16).astype(jnp.float32)
    total = jnp.sum(wide, axis=1, keepdims=True) + hard_weight
    along = jnp.sum(wide * scores, axis=1, keepdims=True) + hard_weight * hard - total * positive
    return weight, [inv_q, inv_p, inv_h, hard_weight, total, along, positive, hard]


def query_side(hood, pos, hard, visit_total, weight, scalars, neg_slice):
    f32, bf16 = jnp.float32, jnp.bfloat16
    inv_q, inv_p, inv_h, hard_weight, total, along, pos_score, hard_score = [
        scalars[:, i : i + 1] for i in range(8)
    ]
    query_unit, pos_unit, hard_unit = hood * inv_q, pos * inv_p, hard * inv_h
    query_float = query_unit.astype(bf16).astype(f32)
    query_grad = (
        dot(weight, neg_slice)
        + hard_weight * hard_unit.astype(bf16).astype(f32)
        - total * pos_unit.astype(bf16).astype(f32)
    )
    hood_grad = (query_grad - query_unit * along) * inv_q
    pos_grad = -total * (query_float - pos_unit * pos_score) * inv_p
    hard_grad = hard_weight * (query_float - hard_unit * hard_score) * inv_h
    return [hood_grad, pos_grad, hard_grad, hood_grad / visit_total], query_float


def kernel(
    sizes,
    table,
    projection,
    info,
    neg_column,
    neg_line,
    out,
    feats,
    pre,
    act,
    info_all,
    rows,
    slices,
    picks,
    picked,
    partial,
    parts,
    stats,
    stats_all,
    weight_all,
    scalar_all,
    flipped,
    back,
    core_in,
    across,
    across_in,
    turned,
    landed,
    pre_grad,
    send_sem,
    recv_sem,
):
    shards, slot_count, node_count, neg_count, query_count = sizes
    f32, bf16 = jnp.float32, jnp.bfloat16
    width = slices.shape[3]
    embed_width = projection.shape[1]
    node_part, neg_part = node_count // 4, neg_count // 4
    part = node_part + neg_part
    group = query_count * shards
    me, rep = lax.axis_index("shard"), lax.axis_index("rep")
    x, core = rep // 2, rep % 2
    mine, half = 2 * core + x, 2 * core
    crossed = 2 * core + 1 - x
    x_peer = (me, (1 - x) * 2 + core)
    core_peer = (me, x * 2 + 1 - core)
    peers = [lax.rem(me + k, shards) for k in range(shards)]
    sources = [lax.rem(me + shards - k, shards) for k in range(shards)]
    sent = []

    def send(source, target, sem, device):
        copy = pltpu.make_async_remote_copy(
            src_ref=source,
            dst_ref=target,
            send_sem=send_sem.at[sem],
            recv_sem=recv_sem.at[sem],
            device_id=device,
            device_id_type=MESH,
        )
        copy.start()
        sent.append(copy)
        return copy

    barrier = pltpu.get_barrier_semaphore()
    for k in range(1, shards):
        pl.semaphore_signal(barrier, inc=1, device_id=(peers[k], rep), device_id_type=MESH)
    for device in (x_peer, core_peer):
        pl.semaphore_signal(barrier, inc=1, device_id=device, device_id_type=MESH)

    neg_pick = (
        lax.broadcasted_iota(jnp.int32, (neg_count, node_count), 1) == neg_column[...]
    ).astype(bf16)
    neg_feat = dot(neg_pick, table[...]).astype(bf16)
    for b in range(4):
        feats[b * part : b * part + node_part] = table[b * node_part : (b + 1) * node_part]
        feats[b * part + node_part : (b + 1) * part] = neg_feat[b * neg_part : (b + 1) * neg_part]
    tile = 2 * width

    def embed_tile(t, squares):
        columns = pl.ds(pl.multiple_of(t * tile, tile), tile)
        values = dot(feats[...], projection[:, columns])
        pre[:, :, columns] = values.reshape(4, part, tile)
        values = values * jax.nn.sigmoid(values)
        act[:, :, columns] = values.reshape(4, part, tile)
        return squares + jnp.sum(values * values, axis=1, keepdims=True)

    squares = lax.fori_loop(
        0, embed_width // tile, embed_tile, jnp.zeros((4 * part, 1), f32)
    ).reshape(4, part, 1)
    place = lax.broadcasted_iota(jnp.int32, (4, part, 1), 1)
    scale = jnp.where(place >= node_part, lax.rsqrt(squares + epsilon), 1.0)

    pl.semaphore_wait(barrier, shards + 1)

    own_rows = pl.ds(pl.multiple_of(me * query_count, query_count), query_count)
    info_copies = [
        send(info, info_all.at[own_rows], k, (peers[k], rep)) for k in range(1, shards)
    ]
    info_all[own_rows] = info[...]
    base = shards
    slice_copies = []
    for k in list(range(1, shards)) + [0]:
        columns = pl.ds(pl.multiple_of(peers[k] * width, width), width)
        values = (act[:, :, columns] * scale).astype(bf16)
        if k:
            rows[k] = values
            slice_copies.append(
                send(
                    rows.at[k, pl.ds(half, 2)],
                    slices.at[me, pl.ds(half, 2)],
                    base + k,
                    (peers[k], rep),
                )
            )
        else:
            slices[me] = values

    for copy in info_copies:
        copy.wait_recv()
    block = 16

    def pick_rows(step, carry):
        start = pl.multiple_of(step * block, block)
        ids = info_all[pl.ds(start, block)]
        lane = lax.broadcasted_iota(jnp.int32, (block, shards * node_count), 1)
        for s in range(3):
            picks[s, pl.ds(start, block)] = (
                jnp.where(lane == ids[:, s : s + 1], 1.0, 0.0).astype(bf16)
            )
        counts = ids.astype(f32)
        spread = jnp.zeros(lane.shape, f32)
        for k in range(3, slot_count):
            spread = spread + jnp.where(
                lane == ids[:, k : k + 1], counts[:, slot_count + k - 3 : slot_count + k - 2], 0.0
            )
        picks[3, pl.ds(start, block)] = spread.astype(bf16)
        return carry

    lax.fori_loop(0, group // block, pick_rows, 0)

    base = 2 * shards
    swaps = []
    for k in range(1, shards):
        slice_copies[k - 1].wait_recv()
        piece = slices.at[sources[k], pl.ds(half, 2)]
        swaps.append(send(piece, piece, base + k, core_peer))
    for copy in swaps:
        copy.wait_recv()

    act_slice = slices[:, :, :node_part].reshape(shards * node_count, width)
    neg_slice = slices[:, :, node_part:].reshape(shards * neg_count, width)

    def pick_set(s, carry):
        picked[s] = dot(picks[s], act_slice)
        return carry

    lax.fori_loop(0, 4, pick_set, 0)
    counts = info_all[:, slot_count : 2 * slot_count - 3].astype(f32)
    visit_total = jnp.sum(counts, axis=1, keepdims=True)
    hood = picked[0] + picked[3] / visit_total
    pos, hard = picked[1], picked[2]
    partial[...] = dot(hood.astype(bf16), neg_slice, 1, 1).astype(bf16)
    pairs = ((hood, hood), (pos, pos), (hard, hard), (hood, pos), (hood, hard))
    stats[...] = lanes_of([jnp.sum(a * b, axis=1, keepdims=True) for a, b in pairs], width)
    base = 3 * shards
    copies = []
    for k in range(1, shards):
        there = pl.ds(pl.multiple_of(peers[k] * query_count, query_count), query_count)
        copies.append(send(stats.at[there], stats_all.at[k], base + k, (peers[k], rep)))
        copies.append(
            send(partial.at[there], parts.at[k], base + shards + k, (peers[k], rep))
        )
    dots = partial[own_rows].astype(f32)
    sums = stats[own_rows]
    for copy in copies:
        copy.wait_recv()
    for k in range(1, shards):
        dots = dots + parts[k].astype(f32)
        sums = sums + stats_all[k]
    weight, scalars = loss_weights(dots, sums)
    weight_all[own_rows] = weight
    scalar_all[own_rows] = lanes_of(scalars, width)
    base = 5 * shards
    copies = []
    for k in range(1, shards):
        there = (peers[k], rep)
        copies.append(send(scalar_all.at[own_rows], scalar_all.at[own_rows], base + k, there))
        copies.append(
            send(weight_all.at[own_rows], weight_all.at[own_rows], base + shards + k, there)
        )
    for copy in copies:
        copy.wait_recv()

    weight = weight_all[...]
    grads, query_float = query_side(hood, pos, hard, visit_total, weight, scalar_all[...], neg_slice)
    for s in range(4):
        flipped[:, s * group : (s + 1) * group] = jnp.transpose(grads[s]).astype(bf16)
    neg_grad = jnp.transpose(dot(jnp.transpose(query_float).astype(bf16), weight))
    back[:, :, node_part:] = neg_grad.reshape(shards, 4, neg_part, width)
    base = 7 * shards
    other = pl.ds(2 - half, 2)

    def node_block(s, carry):
        columns = pl.ds(pl.multiple_of(s * node_count, node_count), node_count)
        total = jnp.zeros((width, node_count), f32)
        for kind in range(4):
            total = total + dot(
                flipped[:, kind * group : (kind + 1) * group], picks[kind, :, columns]
            )
        back[s, :, :node_part] = jnp.transpose(total).reshape(4, node_part, width)
        return carry

    lax.fori_loop(0, shards, node_block, 0)
    send(back.at[:, other], core_in, base, core_peer).wait_recv()

    across[...] = (back[:, crossed] + core_in[:, 1 - x]).astype(bf16)
    copy = send(across, across_in, base + 1, x_peer)
    kept = back[:, mine] + core_in[:, x]
    copy.wait_recv()
    turned[...] = (kept + across_in[...].astype(f32)).astype(bf16)
    base = 8 * shards
    copies = [
        send(turned.at[peers[k]], landed.at[me], base + k, (peers[k], rep))
        for k in range(1, shards)
    ]
    landed[me] = turned[me]
    for copy in copies:
        copy.wait_recv()
    grad = jnp.concatenate([landed[s].astype(f32) for s in range(shards)], axis=1)
    own_pre = pre[mine]
    neg_unit = act[mine, node_part:]
    inverse = lax.rsqrt(jnp.sum(neg_unit * neg_unit, axis=1, keepdims=True) + epsilon)
    neg_unit = neg_unit * inverse
    neg_back = grad[node_part:]
    neg_back = neg_back - neg_unit * jnp.sum(neg_unit * neg_back, axis=1, keepdims=True)
    neg_back = neg_back * inverse
    slope = silu_slope(own_pre)
    pre_grad[mine, :node_part] = (grad[:node_part] * slope[:node_part]).astype(bf16)
    pre_grad[mine, node_part:] = (neg_back * slope[node_part:]).astype(bf16)
    base = 9 * shards
    first = send(pre_grad.at[mine], pre_grad.at[mine], base, x_peer)
    second = send(pre_grad.at[mine], pre_grad.at[mine], base + 1, core_peer)
    first.wait_recv()
    third = send(pre_grad.at[crossed], pre_grad.at[crossed], base + 2, core_peer)
    second.wait_recv()
    third.wait_recv()
    node_grad = pre_grad[:, :node_part].reshape(node_count, embed_width)
    neg_grad = pre_grad[:, node_part:].reshape(neg_count, embed_width)
    placed = (
        lax.broadcasted_iota(jnp.int32, (node_count, neg_count), 0) == neg_line[...]
    ).astype(bf16)
    out[...] = (node_grad.astype(f32) + dot(placed, neg_grad)).astype(bf16)
    for copy in sent:
        copy.wait_send()


def column_split(feature_table, projection, slot_owner, slot_row, visits, neg_row):
    shards = lax.axis_size("shard")
    query_count, slot_count = slot_row.shape
    node_count, feat_width = feature_table.shape
    neg_count = neg_row.shape[0]
    embed_width = projection.shape[1]
    width = embed_width // shards
    group = query_count * shards
    part = (node_count + neg_count) // 4
    f32, bf16 = jnp.float32, jnp.bfloat16
    node = slot_owner.reshape(query_count, slot_count) * node_count + slot_row
    info = jnp.concatenate([node, visits], axis=1)
    info = jnp.pad(info, ((0, 0), (0, width - info.shape[1])))
    sizes = (shards, slot_count, node_count, neg_count, query_count)
    sems = 9 * shards + 3
    vmem = pl.BlockSpec(memory_space=pltpu.VMEM)
    pre_grad = pl.pallas_call(
        functools.partial(kernel, sizes),
        out_shape=jax.ShapeDtypeStruct((node_count, embed_width), bf16),
        in_specs=[vmem] * 5,
        out_specs=vmem,
        scratch_shapes=[
            pltpu.VMEM((4 * part, feat_width), bf16),
            pltpu.VMEM((4, part, embed_width), f32),
            pltpu.VMEM((4, part, embed_width), f32),
            pltpu.VMEM((group, width), jnp.int32),
            pltpu.VMEM((shards, 4, part, width), bf16),
            pltpu.VMEM((shards, 4, part, width), bf16),
            pltpu.VMEM((4, group, shards * node_count), bf16),
            pltpu.VMEM((4, group, width), f32),
            pltpu.VMEM((group, shards * neg_count), bf16),
            pltpu.VMEM((shards, query_count, shards * neg_count), bf16),
            pltpu.VMEM((group, width), f32),
            pltpu.VMEM((shards, query_count, width), f32),
            pltpu.VMEM((group, shards * neg_count), bf16),
            pltpu.VMEM((group, width), f32),
            pltpu.VMEM((width, 4 * group), bf16),
            pltpu.VMEM((shards, 4, part, width), f32),
            pltpu.VMEM((shards, 2, part, width), f32),
            pltpu.VMEM((shards, part, width), bf16),
            pltpu.VMEM((shards, part, width), bf16),
            pltpu.VMEM((shards, part, width), bf16),
            pltpu.VMEM((shards, part, width), bf16),
            pltpu.VMEM((4, part, embed_width), bf16),
            pltpu.SemaphoreType.DMA((sems,)),
            pltpu.SemaphoreType.DMA((sems,)),
        ],
        compiler_params=pltpu.CompilerParams(
            collective_id=0, has_side_effects=True, vmem_limit_bytes=48 * 1024 * 1024
        ),
    )(feature_table, projection, info, neg_row.reshape(neg_count, 1), neg_row.reshape(1, neg_count))
    return times_back(pre_grad, projection)


def solution(mesh):
    shards, reps = mesh.shape["shard"], mesh.shape["rep"]

    def body(feature_table, projection, slot_owner, slot_row, visits, neg_row):
        width = projection.shape[1] // shards
        parts = (feature_table.shape[0], neg_row.shape[0], slot_row.shape[0] * 2)
        whole = width == 128 and reps == 4 and all(size % 64 == 0 for size in parts)
        form = column_split if whole else on_device
        return form(feature_table, projection, slot_owner, slot_row, visits, neg_row)

    return jax.shard_map(
        body,
        mesh=mesh,
        in_specs=(
            P("shard", None),
            P(),
            P(("shard", "rep"), None, None),
            P(("shard", "rep"), None),
            P(("shard", "rep"), None),
            P("shard"),
        ),
        out_specs=P("shard", None),
        check_vma=False,
    )
```

```python
import functools

import jax
import jax.numpy as jnp
from jax import lax
from jax.experimental import pallas as pl
from jax.experimental.pallas import tpu as pltpu
from jax.sharding import PartitionSpec as P

MESH = pl.DeviceIdType.MESH

score_scale = 8.0
margin_value = 0.1
epsilon = 1e-06


def unit_rows(values):
    norms = jnp.sqrt(jnp.sum(values * values, axis=-1, keepdims=True) + epsilon)
    return (values / norms, norms)


def unit_back(grads, unit, norms):
    return (grads - unit * jnp.sum(unit * grads, axis=-1, keepdims=True)) / norms


def silu_slope(preact):
    gate_value = jax.nn.sigmoid(preact)
    return gate_value * (1.0 + preact * (1.0 - gate_value))


def times_back(left, projection):
    return jnp.einsum("re,fe->rf", left, projection, preferred_element_type=jnp.float32)


def on_device(feature_table, projection, slot_owner, slot_row, visits, neg_row):
    shard_count = lax.axis_size("shard")
    query_count, slot_count = slot_row.shape
    row_count = query_count * slot_count
    capacity = 2 * row_count // shard_count
    feat_width = projection.shape[0]
    embed_width = projection.shape[1]
    owners = slot_owner.reshape(row_count)
    one_hot = (owners[:, None] == jnp.arange(shard_count, dtype=jnp.int32)[None, :]).astype(
        jnp.int32
    )
    earlier = jnp.cumsum(one_hot, axis=0) - one_hot
    slot_rank = jnp.sum(earlier * one_hot, axis=1)
    position = owners * capacity + slot_rank
    send_ids = (
        jnp.zeros((shard_count * capacity,), jnp.int32)
        .at[position]
        .set(slot_row.reshape(row_count))
    )
    send_ids = send_ids.reshape(shard_count, capacity)
    asked = lax.all_to_all(send_ids, "shard", split_axis=0, concat_axis=0, tiled=True)
    picked = feature_table[asked]
    fetched = lax.all_to_all(picked, "shard", split_axis=0, concat_axis=0, tiled=True)
    gathered = fetched.reshape(shard_count * capacity, feat_width)[position]
    neg_pre = jnp.dot(feature_table[neg_row], projection, preferred_element_type=jnp.float32)
    neg_unit, neg_norms = unit_rows(jax.nn.silu(neg_pre))
    neg_embed = lax.all_gather(neg_unit.astype(jnp.bfloat16), "shard", axis=0, tiled=True)
    visit_float = visits.astype(jnp.float32)
    coefs = visit_float / jnp.sum(visit_float, axis=1, keepdims=True)
    preact = jnp.dot(gathered, projection, preferred_element_type=jnp.float32).reshape(
        query_count, slot_count, embed_width
    )
    active = jax.nn.silu(preact)
    hood = active[:, 0] + jnp.einsum("bk,bke->be", coefs, active[:, 3:])
    query_unit, query_norms = unit_rows(hood)
    query_embed = query_unit.astype(jnp.bfloat16)
    item_unit, item_norms = unit_rows(active[:, 1:3])
    item_embed = item_unit.astype(jnp.bfloat16)
    query_float = query_embed.astype(jnp.float32)
    item_float = item_embed.astype(jnp.float32)
    neg_scores = jnp.einsum("be,ne->bn", query_embed, neg_embed, preferred_element_type=jnp.float32)
    pair_scores = jnp.sum(query_float[:, None, :] * item_float, axis=2)
    positive = pair_scores[:, 0:1]
    neg_weight = (
        score_scale * jax.nn.sigmoid(score_scale * (neg_scores - positive + margin_value))
    ).astype(jnp.bfloat16)
    hard_weight = (
        score_scale * jax.nn.sigmoid(score_scale * (pair_scores[:, 1:2] - positive + margin_value))
    ).astype(jnp.bfloat16)
    hard_float = hard_weight.astype(jnp.float32)
    total_weight = jnp.sum(neg_weight.astype(jnp.float32), axis=1, keepdims=True) + hard_float
    query_grad = (
        jnp.dot(neg_weight, neg_embed, preferred_element_type=jnp.float32)
        + hard_float * item_float[:, 1]
        - total_weight * item_float[:, 0]
    )
    item_grad = jnp.stack([-total_weight * query_float, hard_float * query_float], axis=1)
    neg_partial = jnp.einsum(
        "bn,be->ne", neg_weight, query_embed, preferred_element_type=jnp.float32
    )
    hood_grad = unit_back(query_grad, query_unit, query_norms)
    item_back = unit_back(item_grad, item_unit, item_norms)
    active_grad = jnp.concatenate(
        [hood_grad[:, None], item_back, coefs[:, :, None] * hood_grad[:, None]], axis=1
    )
    preact_grad = (
        (active_grad * silu_slope(preact)).astype(jnp.bfloat16).reshape(row_count, embed_width)
    )
    outgoing = (
        jnp.zeros((shard_count * capacity, embed_width), jnp.bfloat16).at[position].set(preact_grad)
    )
    incoming = lax.all_to_all(
        outgoing.reshape(shard_count, capacity, embed_width),
        "shard",
        split_axis=0,
        concat_axis=0,
        tiled=True,
    )
    contrib = times_back(incoming.reshape(shard_count * capacity, embed_width), projection)
    neg_sum = lax.psum_scatter(neg_partial, "shard", scatter_dimension=0, tiled=True)
    grad_local = (
        jnp.zeros((feature_table.shape[0], feat_width), jnp.float32)
        .at[asked.reshape(-1)]
        .add(contrib)
    )
    grad_local, neg_total = lax.psum((grad_local, neg_sum), "rep")
    neg_back = unit_back(neg_total, neg_unit, neg_norms)
    neg_pre_grad = (neg_back * silu_slope(neg_pre)).astype(jnp.bfloat16)
    neg_rows = times_back(neg_pre_grad, projection)
    return grad_local.at[neg_row].add(neg_rows)


def dot(left, right, left_dim=1, right_dim=0):
    return lax.dot_general(
        left, right, (((left_dim,), (right_dim,)), ((), ())), preferred_element_type=jnp.float32
    )


def lanes_of(columns, width):
    rows = columns[0].shape[0]
    lane = lax.broadcasted_iota(jnp.int32, (rows, width), 1)
    result = jnp.zeros((rows, width), jnp.float32)
    for place, column in enumerate(columns):
        result = jnp.where(lane == place, column, result)
    return result


def loss_weights(dots, stats):
    inverse = lax.rsqrt(stats[:, 0:3] + epsilon)
    inv_q, inv_p, inv_h = inverse[:, 0:1], inverse[:, 1:2], inverse[:, 2:3]
    scores = dots * inv_q
    positive = stats[:, 3:4] * inv_q * inv_p
    hard = stats[:, 4:5] * inv_q * inv_h
    weight = score_scale * jax.nn.sigmoid(score_scale * (scores - positive + margin_value))
    weight = weight.astype(jnp.bfloat16)
    wide = weight.astype(jnp.float32)
    hard_weight = score_scale * jax.nn.sigmoid(score_scale * (hard - positive + margin_value))
    hard_weight = hard_weight.astype(jnp.bfloat16).astype(jnp.float32)
    total = jnp.sum(wide, axis=1, keepdims=True) + hard_weight
    along = jnp.sum(wide * scores, axis=1, keepdims=True) + hard_weight * hard - total * positive
    return weight, [inv_q, inv_p, inv_h, hard_weight, total, along, positive, hard]


def item_side(hood, pos, hard, scalars):
    f32, bf16 = jnp.float32, jnp.bfloat16
    inv_q, inv_p, inv_h, hard_weight, total, along, pos_score, hard_score = [
        scalars[:, i : i + 1] for i in range(8)
    ]
    query_unit, pos_unit, hard_unit = hood * inv_q, pos * inv_p, hard * inv_h
    query_float = query_unit.astype(bf16).astype(f32)
    known_grad = hard_weight * hard_unit.astype(bf16).astype(
        f32
    ) - total * pos_unit.astype(bf16).astype(f32)
    pos_grad = -total * (query_float - pos_unit * pos_score) * inv_p
    hard_grad = hard_weight * (query_float - hard_unit * hard_score) * inv_h
    return query_unit, query_float, known_grad, pos_grad, hard_grad


def kernel(
    sizes,
    table_hbm,
    projection_hbm,
    owner_line,
    row_line,
    visit_line,
    neg_line,
    out,
    table,
    projection,
    lines,
    info,
    slope,
    early,
    feats,
    pre,
    act,
    info_all,
    rows,
    slices,
    picks,
    picked,
    partial,
    parts,
    stats,
    stats_all,
    weight_all,
    scalar_all,
    flipped,
    back,
    core_in,
    across,
    across_in,
    turned,
    landed,
    pre_grad,
    send_sem,
    recv_sem,
    local_sem,
):
    shards, slot_count, node_count, neg_count, query_count = sizes
    f32, bf16 = jnp.float32, jnp.bfloat16
    width = slices.shape[3]
    embed_width = projection_hbm.shape[1]
    node_part, neg_part = node_count // 4, neg_count // 4
    part = node_part + neg_part
    group = query_count * shards
    me, rep = lax.axis_index("shard"), lax.axis_index("rep")
    x, core = rep // 2, rep % 2
    mine, half = 2 * core + x, 2 * core
    crossed = 2 * core + 1 - x
    x_peer = (me, (1 - x) * 2 + core)
    core_peer = (me, x * 2 + 1 - core)
    peers = [lax.rem(me + k, shards) for k in range(shards)]
    sources = [lax.rem(me + shards - k, shards) for k in range(shards)]
    sent = []
    tile = 2 * width
    tiles = embed_width // tile
    loads = [pltpu.make_async_copy(table_hbm, table, local_sem.at[tiles])]
    for t in range(tiles):
        columns = pl.ds(t * tile, tile)
        loads.append(
            pltpu.make_async_copy(
                projection_hbm.at[:, columns], projection.at[t], local_sem.at[t]
            )
        )
    for load in loads:
        load.start()

    def send(source, target, sem, device):
        copy = pltpu.make_async_remote_copy(
            src_ref=source,
            dst_ref=target,
            send_sem=send_sem.at[sem],
            recv_sem=recv_sem.at[sem],
            device_id=device,
            device_id_type=MESH,
        )
        copy.start()
        sent.append(copy)
        return copy

    barrier = pltpu.get_barrier_semaphore()
    for k in range(1, shards):
        pl.semaphore_signal(barrier, inc=1, device_id=(peers[k], rep), device_id_type=MESH)
    for device in (x_peer, core_peer):
        pl.semaphore_signal(barrier, inc=1, device_id=device, device_id_type=MESH)

    lines[...] = jnp.zeros(lines.shape, f32)
    lines[0:slot_count, 0:query_count] = (
        owner_line[...] * node_count + row_line[...]
    ).astype(f32)
    lines[slot_count : 2 * slot_count - 3, 0:query_count] = visit_line[...].astype(f32)
    lines[2 * slot_count : 2 * slot_count + 1, 0:neg_count] = neg_line[...].astype(f32)
    columns = jnp.transpose(lines[...])
    info[...] = columns[0:query_count]
    neg_column = columns[0:neg_count, 2 * slot_count : 2 * slot_count + 1].astype(jnp.int32)
    neg_pick = (
        lax.broadcasted_iota(jnp.int32, (neg_count, node_count), 1) == neg_column
    ).astype(bf16)
    loads[0].wait()
    neg_feat = dot(neg_pick, table[...]).astype(bf16)
    for b in range(4):
        feats[b * part : b * part + node_part] = table[b * node_part : (b + 1) * node_part]
        feats[b * part + node_part : (b + 1) * part] = neg_feat[b * neg_part : (b + 1) * neg_part]
    squares = jnp.zeros((4 * part, 1), f32)
    for t in range(tiles):
        loads[1 + t].wait()
        values = dot(feats[...], projection[t])
        pre[:, :, t * tile : (t + 1) * tile] = values.reshape(4, part, tile)
        values = values * jax.nn.sigmoid(values)
        act[:, :, t * tile : (t + 1) * tile] = values.reshape(4, part, tile)
        squares = squares + jnp.sum(values * values, axis=1, keepdims=True)
    squares = squares.reshape(4, part, 1)
    place = lax.broadcasted_iota(jnp.int32, (4, part, 1), 1)
    scale = jnp.where(place >= node_part, lax.rsqrt(squares + epsilon), 1.0)

    pl.semaphore_wait(barrier, shards + 1)

    own_rows = pl.ds(pl.multiple_of(me * query_count, query_count), query_count)
    info_copies = [
        send(info, info_all.at[own_rows], k, (peers[k], rep)) for k in range(1, shards)
    ]
    info_all[own_rows] = info[...]
    base = shards
    slice_copies = []
    for k in list(range(1, shards)) + [0]:
        columns = pl.ds(pl.multiple_of(peers[k] * width, width), width)
        values = (act[:, :, columns] * scale).astype(bf16)
        if k:
            rows[k] = values
            slice_copies.append(
                send(
                    rows.at[k, pl.ds(half, 2)],
                    slices.at[me, pl.ds(half, 2)],
                    base + k,
                    (peers[k], rep),
                )
            )
        else:
            slices[me] = values

    for copy in info_copies:
        copy.wait_recv()
    block = 16

    def pick_rows(step, carry):
        start = pl.multiple_of(step * block, block)
        ids = info_all[pl.ds(start, block)]
        lane = lax.broadcasted_iota(jnp.int32, (block, shards * node_count), 1).astype(f32)
        for s in range(3):
            picks[s, pl.ds(start, block)] = (
                jnp.where(lane == ids[:, s : s + 1], 1.0, 0.0).astype(bf16)
            )
        counts = ids
        spread = jnp.zeros(lane.shape, f32)
        for k in range(3, slot_count):
            spread = spread + jnp.where(
                lane == ids[:, k : k + 1], counts[:, slot_count + k - 3 : slot_count + k - 2], 0.0
            )
        picks[3, pl.ds(start, block)] = spread.astype(bf16)
        return carry

    lax.fori_loop(0, group // block, pick_rows, 0)

    def gather_from(k, first=False):
        source = sources[k]
        columns = pl.ds(pl.multiple_of(source * node_count, node_count), node_count)
        values = slices[source, :, :node_part].reshape(node_count, width)
        for kind in range(4):
            part_sum = dot(picks[kind, :, columns], values)
            picked[kind] = part_sum if first else picked[kind] + part_sum

    base = 2 * shards
    swaps = []
    gather_from(0, True)
    for k in range(1, shards):
        slice_copies[k - 1].wait_recv()
        piece = slices.at[sources[k], pl.ds(half, 2)]
        swaps.append(send(piece, piece, base + k, core_peer))
        if k > 1:
            swaps[k - 2].wait_recv()
            gather_from(k - 1)
    swaps[shards - 2].wait_recv()
    gather_from(shards - 1)
    neg_slice = slices[:, :, node_part:].reshape(shards * neg_count, width)
    counts = info_all[:, slot_count : 2 * slot_count - 3]
    visit_total = jnp.sum(counts, axis=1, keepdims=True)
    hood = picked[0] + picked[3] / visit_total
    pos, hard = picked[1], picked[2]
    partial[...] = dot(hood.astype(bf16), neg_slice, 1, 1).astype(bf16)
    pairs = ((hood, hood), (pos, pos), (hard, hard), (hood, pos), (hood, hard))
    stats[...] = lanes_of([jnp.sum(a * b, axis=1, keepdims=True) for a, b in pairs], width)
    base = 3 * shards
    copies = []
    for k in range(1, shards):
        there = pl.ds(pl.multiple_of(peers[k] * query_count, query_count), query_count)
        copies.append(send(stats.at[there], stats_all.at[k], base + k, (peers[k], rep)))
        copies.append(
            send(partial.at[there], parts.at[k], base + shards + k, (peers[k], rep))
        )
    slope[...] = silu_slope(pre[mine])
    neg_unit = act[mine, node_part:]
    inverse = lax.rsqrt(jnp.sum(neg_unit * neg_unit, axis=1, keepdims=True) + epsilon)
    neg_unit = neg_unit * inverse
    dots = partial[own_rows].astype(f32)
    sums = stats[own_rows]
    for copy in copies:
        copy.wait_recv()
    for k in range(1, shards):
        dots = dots + parts[k].astype(f32)
        sums = sums + stats_all[k]
    weight, scalars = loss_weights(dots, sums)
    weight_all[own_rows] = weight
    scalar_all[own_rows] = lanes_of(scalars, width)
    base = 5 * shards
    copies = [
        send(scalar_all.at[own_rows], scalar_all.at[own_rows], base + k, (peers[k], rep))
        for k in range(1, shards)
    ]
    weight_copies = [
        send(weight_all.at[own_rows], weight_all.at[own_rows], base + shards + k, (peers[k], rep))
        for k in range(1, shards)
    ]
    for copy in copies:
        copy.wait_recv()
    scalars = scalar_all[...]
    side = item_side(hood, pos, hard, scalars)
    query_unit, query_float, known_grad, pos_grad, hard_grad = side
    flipped[:, 0:group] = jnp.transpose(pos_grad).astype(bf16)
    flipped[:, group : 2 * group] = jnp.transpose(hard_grad).astype(bf16)
    query_flipped = jnp.transpose(query_float).astype(bf16)

    def early_block(s, carry):
        columns = pl.ds(pl.multiple_of(s * node_count, node_count), node_count)
        early[s] = dot(flipped[:, 0:group], picks[1, :, columns]) + dot(
            flipped[:, group : 2 * group], picks[2, :, columns]
        )
        return carry

    lax.fori_loop(0, shards, early_block, 0)
    for copy in weight_copies:
        copy.wait_recv()

    weight = weight_all[...]
    along, inv_q = scalars[:, 5:6], scalars[:, 0:1]
    hood_grad = (dot(weight, neg_slice) + known_grad - query_unit * along) * inv_q
    flipped[:, 2 * group : 3 * group] = jnp.transpose(hood_grad).astype(bf16)
    flipped[:, 3 * group :] = jnp.transpose(hood_grad / visit_total).astype(bf16)
    neg_grad = jnp.transpose(dot(query_flipped, weight))
    back[:, :, node_part:] = neg_grad.reshape(shards, 4, neg_part, width)
    other = pl.ds(2 - half, 2)
    order = list(range(1, shards)) + [0]
    core_copies, x_copies, row_copies = {}, {}, {}

    def to_core(k):
        s = peers[k]
        columns = pl.ds(pl.multiple_of(s * node_count, node_count), node_count)
        total = early[s] + dot(flipped[:, 2 * group : 3 * group], picks[0, :, columns])
        total = total + dot(flipped[:, 3 * group :], picks[3, :, columns])
        back[s, :, :node_part] = jnp.transpose(total).reshape(4, node_part, width)
        core_copies[k] = send(back.at[s, other], core_in.at[s], 7 * shards + k, core_peer)

    def to_x(k):
        s = peers[k]
        core_copies[k].wait_recv()
        across[s] = (back[s, crossed] + core_in[s, 1 - x]).astype(bf16)
        x_copies[k] = send(across.at[s], across_in.at[s], 8 * shards + k, x_peer)

    def to_holder(k):
        s = peers[k]
        x_copies[k].wait_recv()
        total = back[s, mine] + core_in[s, x] + across_in[s].astype(f32)
        if k:
            turned[k] = total.astype(bf16)
            row_copies[k] = send(turned.at[k], landed.at[me], 9 * shards + k, (s, rep))
        else:
            landed[me] = total.astype(bf16)

    lag = 3
    for step in range(shards + lag):
        if step < shards:
            to_core(order[step])
        if step >= lag:
            to_x(order[step - lag])
    for k in order:
        to_holder(k)

    home = [0] + list(range(1, shards))
    to_x_peer, to_core_peer, passed = [], [], []
    for k in home:
        if k:
            row_copies[k].wait_recv()
        s = sources[k]
        columns = pl.ds(pl.multiple_of(s * width, width), width)
        values = landed[s, :node_part].astype(f32) * slope[:node_part, columns]
        pre_grad[s, mine, :node_part] = values.astype(bf16)
        piece = pre_grad.at[s, mine, pl.ds(0, node_part)]
        to_x_peer.append(send(piece, piece, 10 * shards + k, x_peer))
        to_core_peer.append(send(piece, piece, 11 * shards + k, core_peer))
    neg_back = jnp.concatenate(
        [landed[s, node_part:].astype(f32) for s in range(shards)], axis=1
    )
    neg_back = neg_back - neg_unit * jnp.sum(neg_unit * neg_back, axis=1, keepdims=True)
    neg_back = (neg_back * inverse * slope[node_part:]).astype(bf16)
    for s in range(shards):
        pre_grad[s, mine, node_part:] = neg_back[:, s * width : (s + 1) * width]
    piece = pre_grad.at[:, mine, pl.ds(node_part, neg_part)]
    last = 13 * shards
    to_x_peer.append(send(piece, piece, last, x_peer))
    to_core_peer.append(send(piece, piece, last + 1, core_peer))
    for k in home:
        to_x_peer[k].wait_recv()
        piece = pre_grad.at[sources[k], crossed, pl.ds(0, node_part)]
        passed.append(send(piece, piece, 12 * shards + k, core_peer))
    to_x_peer[shards].wait_recv()
    piece = pre_grad.at[:, crossed, pl.ds(node_part, neg_part)]
    passed.append(send(piece, piece, last + 2, core_peer))
    placed = (
        lax.broadcasted_iota(jnp.int32, (node_count, neg_count), 0) == neg_line[...]
    ).astype(bf16)
    for copy in to_core_peer + passed:
        copy.wait_recv()
    for s in range(shards):
        node_grad = pre_grad[s, :, :node_part].reshape(node_count, width).astype(f32)
        neg_grad = pre_grad[s, :, node_part:].reshape(neg_count, width)
        out[:, s * width : (s + 1) * width] = (node_grad + dot(placed, neg_grad)).astype(bf16)
    for copy in sent:
        copy.wait_send()


def column_split(feature_table, projection, slot_owner, slot_row, visits, neg_row):
    shards = lax.axis_size("shard")
    query_count, slot_count = slot_row.shape
    node_count, feat_width = feature_table.shape
    neg_count = neg_row.shape[0]
    embed_width = projection.shape[1]
    width = embed_width // shards
    group = query_count * shards
    part = (node_count + neg_count) // 4
    f32, bf16 = jnp.float32, jnp.bfloat16
    owner_line = jnp.transpose(slot_owner, (1, 2, 0)).reshape(slot_count, query_count)
    sizes = (shards, slot_count, node_count, neg_count, query_count)
    sems = 13 * shards + 3
    tiles = embed_width // (2 * width)
    hbm = pl.BlockSpec(memory_space=pl.ANY)
    vmem = pl.BlockSpec(memory_space=pltpu.VMEM)
    pre_grad = pl.pallas_call(
        functools.partial(kernel, sizes),
        out_shape=jax.ShapeDtypeStruct((node_count, embed_width), bf16),
        in_specs=[hbm] * 2 + [vmem] * 4,
        out_specs=vmem,
        scratch_shapes=[
            pltpu.VMEM((node_count, feat_width), bf16),
            pltpu.VMEM((tiles, feat_width, 2 * width), bf16),
            pltpu.VMEM((128, 128), f32),
            pltpu.VMEM((query_count, width), f32),
            pltpu.VMEM((part, embed_width), f32),
            pltpu.VMEM((shards, width, node_count), f32),
            pltpu.VMEM((4 * part, feat_width), bf16),
            pltpu.VMEM((4, part, embed_width), f32),
            pltpu.VMEM((4, part, embed_width), f32),
            pltpu.VMEM((group, width), f32),
            pltpu.VMEM((shards, 4, part, width), bf16),
            pltpu.VMEM((shards, 4, part, width), bf16),
            pltpu.VMEM((4, group, shards * node_count), bf16),
            pltpu.VMEM((4, group, width), f32),
            pltpu.VMEM((group, shards * neg_count), bf16),
            pltpu.VMEM((shards, query_count, shards * neg_count), bf16),
            pltpu.VMEM((group, width), f32),
            pltpu.VMEM((shards, query_count, width), f32),
            pltpu.VMEM((group, shards * neg_count), bf16),
            pltpu.VMEM((group, width), f32),
            pltpu.VMEM((width, 4 * group), bf16),
            pltpu.VMEM((shards, 4, part, width), f32),
            pltpu.VMEM((shards, 2, part, width), f32),
            pltpu.VMEM((shards, part, width), bf16),
            pltpu.VMEM((shards, part, width), bf16),
            pltpu.VMEM((shards, part, width), bf16),
            pltpu.VMEM((shards, part, width), bf16),
            pltpu.VMEM((shards, 4, part, width), bf16),
            pltpu.SemaphoreType.DMA((sems,)),
            pltpu.SemaphoreType.DMA((sems,)),
            pltpu.SemaphoreType.DMA((tiles + 1,)),
        ],
        compiler_params=pltpu.CompilerParams(
            collective_id=0, has_side_effects=True, vmem_limit_bytes=60 * 1024 * 1024
        ),
    )(
        feature_table,
        projection,
        owner_line,
        jnp.transpose(slot_row),
        jnp.transpose(visits),
        neg_row.reshape(1, neg_count),
    )
    return times_back(pre_grad, projection)


def solution(mesh):
    shards, reps = mesh.shape["shard"], mesh.shape["rep"]

    def body(feature_table, projection, slot_owner, slot_row, visits, neg_row):
        width = projection.shape[1] // shards
        parts = (feature_table.shape[0], neg_row.shape[0], slot_row.shape[0] * 2)
        small = slot_row.shape[0] <= 128 and neg_row.shape[0] <= 128 and slot_row.shape[1] <= 32
        whole = width == 128 and reps == 4 and small and all(size % 64 == 0 for size in parts)
        form = column_split if whole else on_device
        return form(feature_table, projection, slot_owner, slot_row, visits, neg_row)

    return jax.shard_map(
        body,
        mesh=mesh,
        in_specs=(
            P("shard", None),
            P(),
            P(("shard", "rep"), None, None),
            P(("shard", "rep"), None),
            P(("shard", "rep"), None),
            P("shard"),
        ),
        out_specs=P("shard", None),
        check_vma=False,
    )
```

```python
import functools

import jax
import jax.numpy as jnp
from jax import lax
from jax.experimental import pallas as pl
from jax.experimental.pallas import tpu as pltpu
from jax.sharding import PartitionSpec as P

MESH = pl.DeviceIdType.MESH

score_scale = 8.0
margin_value = 0.1
epsilon = 1e-06


def unit_rows(values):
    norms = jnp.sqrt(jnp.sum(values * values, axis=-1, keepdims=True) + epsilon)
    return (values / norms, norms)


def unit_back(grads, unit, norms):
    return (grads - unit * jnp.sum(unit * grads, axis=-1, keepdims=True)) / norms


def silu_slope(preact):
    gate_value = jax.nn.sigmoid(preact)
    return gate_value * (1.0 + preact * (1.0 - gate_value))


def times_back(left, projection):
    return jnp.einsum("re,fe->rf", left, projection, preferred_element_type=jnp.float32)


def on_device(feature_table, projection, slot_owner, slot_row, visits, neg_row):
    shard_count = lax.axis_size("shard")
    query_count, slot_count = slot_row.shape
    row_count = query_count * slot_count
    capacity = 2 * row_count // shard_count
    feat_width = projection.shape[0]
    embed_width = projection.shape[1]
    owners = slot_owner.reshape(row_count)
    one_hot = (owners[:, None] == jnp.arange(shard_count, dtype=jnp.int32)[None, :]).astype(
        jnp.int32
    )
    earlier = jnp.cumsum(one_hot, axis=0) - one_hot
    slot_rank = jnp.sum(earlier * one_hot, axis=1)
    position = owners * capacity + slot_rank
    send_ids = (
        jnp.zeros((shard_count * capacity,), jnp.int32)
        .at[position]
        .set(slot_row.reshape(row_count))
    )
    send_ids = send_ids.reshape(shard_count, capacity)
    asked = lax.all_to_all(send_ids, "shard", split_axis=0, concat_axis=0, tiled=True)
    picked = feature_table[asked]
    fetched = lax.all_to_all(picked, "shard", split_axis=0, concat_axis=0, tiled=True)
    gathered = fetched.reshape(shard_count * capacity, feat_width)[position]
    neg_pre = jnp.dot(feature_table[neg_row], projection, preferred_element_type=jnp.float32)
    neg_unit, neg_norms = unit_rows(jax.nn.silu(neg_pre))
    neg_embed = lax.all_gather(neg_unit.astype(jnp.bfloat16), "shard", axis=0, tiled=True)
    visit_float = visits.astype(jnp.float32)
    coefs = visit_float / jnp.sum(visit_float, axis=1, keepdims=True)
    preact = jnp.dot(gathered, projection, preferred_element_type=jnp.float32).reshape(
        query_count, slot_count, embed_width
    )
    active = jax.nn.silu(preact)
    hood = active[:, 0] + jnp.einsum("bk,bke->be", coefs, active[:, 3:])
    query_unit, query_norms = unit_rows(hood)
    query_embed = query_unit.astype(jnp.bfloat16)
    item_unit, item_norms = unit_rows(active[:, 1:3])
    item_embed = item_unit.astype(jnp.bfloat16)
    query_float = query_embed.astype(jnp.float32)
    item_float = item_embed.astype(jnp.float32)
    neg_scores = jnp.einsum("be,ne->bn", query_embed, neg_embed, preferred_element_type=jnp.float32)
    pair_scores = jnp.sum(query_float[:, None, :] * item_float, axis=2)
    positive = pair_scores[:, 0:1]
    neg_weight = (
        score_scale * jax.nn.sigmoid(score_scale * (neg_scores - positive + margin_value))
    ).astype(jnp.bfloat16)
    hard_weight = (
        score_scale * jax.nn.sigmoid(score_scale * (pair_scores[:, 1:2] - positive + margin_value))
    ).astype(jnp.bfloat16)
    hard_float = hard_weight.astype(jnp.float32)
    total_weight = jnp.sum(neg_weight.astype(jnp.float32), axis=1, keepdims=True) + hard_float
    query_grad = (
        jnp.dot(neg_weight, neg_embed, preferred_element_type=jnp.float32)
        + hard_float * item_float[:, 1]
        - total_weight * item_float[:, 0]
    )
    item_grad = jnp.stack([-total_weight * query_float, hard_float * query_float], axis=1)
    neg_partial = jnp.einsum(
        "bn,be->ne", neg_weight, query_embed, preferred_element_type=jnp.float32
    )
    hood_grad = unit_back(query_grad, query_unit, query_norms)
    item_back = unit_back(item_grad, item_unit, item_norms)
    active_grad = jnp.concatenate(
        [hood_grad[:, None], item_back, coefs[:, :, None] * hood_grad[:, None]], axis=1
    )
    preact_grad = (
        (active_grad * silu_slope(preact)).astype(jnp.bfloat16).reshape(row_count, embed_width)
    )
    outgoing = (
        jnp.zeros((shard_count * capacity, embed_width), jnp.bfloat16).at[position].set(preact_grad)
    )
    incoming = lax.all_to_all(
        outgoing.reshape(shard_count, capacity, embed_width),
        "shard",
        split_axis=0,
        concat_axis=0,
        tiled=True,
    )
    contrib = times_back(incoming.reshape(shard_count * capacity, embed_width), projection)
    neg_sum = lax.psum_scatter(neg_partial, "shard", scatter_dimension=0, tiled=True)
    grad_local = (
        jnp.zeros((feature_table.shape[0], feat_width), jnp.float32)
        .at[asked.reshape(-1)]
        .add(contrib)
    )
    grad_local, neg_total = lax.psum((grad_local, neg_sum), "rep")
    neg_back = unit_back(neg_total, neg_unit, neg_norms)
    neg_pre_grad = (neg_back * silu_slope(neg_pre)).astype(jnp.bfloat16)
    neg_rows = times_back(neg_pre_grad, projection)
    return grad_local.at[neg_row].add(neg_rows)


def dot(left, right, left_dim=1, right_dim=0):
    return lax.dot_general(
        left, right, (((left_dim,), (right_dim,)), ((), ())), preferred_element_type=jnp.float32
    )


def lanes_of(columns, width):
    rows = columns[0].shape[0]
    lane = lax.broadcasted_iota(jnp.int32, (rows, width), 1)
    result = jnp.zeros((rows, width), jnp.float32)
    for place, column in enumerate(columns):
        result = jnp.where(lane == place, column, result)
    return result


def loss_weights(dots, stats):
    inverse = lax.rsqrt(stats[:, 0:3] + epsilon)
    inv_q, inv_p, inv_h = inverse[:, 0:1], inverse[:, 1:2], inverse[:, 2:3]
    scores = dots * inv_q
    positive = stats[:, 3:4] * inv_q * inv_p
    hard = stats[:, 4:5] * inv_q * inv_h
    weight = score_scale * jax.nn.sigmoid(score_scale * (scores - positive + margin_value))
    weight = weight.astype(jnp.bfloat16)
    wide = weight.astype(jnp.float32)
    hard_weight = score_scale * jax.nn.sigmoid(score_scale * (hard - positive + margin_value))
    hard_weight = hard_weight.astype(jnp.bfloat16).astype(jnp.float32)
    total = jnp.sum(wide, axis=1, keepdims=True) + hard_weight
    along = jnp.sum(wide * scores, axis=1, keepdims=True) + hard_weight * hard - total * positive
    return weight, [inv_q, inv_p, inv_h, hard_weight, total, along, positive, hard]


def item_side(hood, pos, hard, scalars):
    f32, bf16 = jnp.float32, jnp.bfloat16
    inv_q, inv_p, inv_h, hard_weight, total, along, pos_score, hard_score = [
        scalars[:, i : i + 1] for i in range(8)
    ]
    query_unit, pos_unit, hard_unit = hood * inv_q, pos * inv_p, hard * inv_h
    query_float = query_unit.astype(bf16).astype(f32)
    known_grad = hard_weight * hard_unit.astype(bf16).astype(
        f32
    ) - total * pos_unit.astype(bf16).astype(f32)
    pos_grad = -total * (query_float - pos_unit * pos_score) * inv_p
    hard_grad = hard_weight * (query_float - hard_unit * hard_score) * inv_h
    return query_unit, query_float, known_grad, pos_grad, hard_grad


def kernel(
    sizes,
    table_hbm,
    projection_hbm,
    owner_line,
    row_line,
    visit_line,
    neg_line,
    out,
    table,
    projection,
    lines,
    info,
    slope,
    early,
    summed,
    feats,
    pre,
    act,
    info_all,
    rows,
    slices,
    picks,
    picked,
    partial,
    parts,
    stats,
    stats_all,
    weight_all,
    scalar_all,
    flipped,
    back,
    core_in,
    across,
    across_in,
    turned,
    landed,
    pre_grad,
    send_sem,
    recv_sem,
    local_sem,
):
    shards, slot_count, node_count, neg_count, query_count = sizes
    f32, bf16 = jnp.float32, jnp.bfloat16
    width = slices.shape[3]
    embed_width = projection_hbm.shape[1]
    node_part, neg_part = node_count // 4, neg_count // 4
    part = node_part + neg_part
    group = query_count * shards
    me, rep = lax.axis_index("shard"), lax.axis_index("rep")
    x, core = rep // 2, rep % 2
    mine, half = 2 * core + x, 2 * core
    crossed = 2 * core + 1 - x
    x_peer = (me, (1 - x) * 2 + core)
    core_peer = (me, x * 2 + 1 - core)
    peers = [lax.rem(me + k, shards) for k in range(shards)]
    sources = [lax.rem(me + shards - k, shards) for k in range(shards)]
    sent = []
    tile = 2 * width
    tiles = embed_width // tile
    loads = [pltpu.make_async_copy(table_hbm, table, local_sem.at[tiles])]
    for t in range(tiles):
        columns = pl.ds(t * tile, tile)
        loads.append(
            pltpu.make_async_copy(
                projection_hbm.at[:, columns], projection.at[t], local_sem.at[t]
            )
        )
    for load in loads:
        load.start()

    def send(source, target, device):
        sem = len(sent)
        copy = pltpu.make_async_remote_copy(
            src_ref=source,
            dst_ref=target,
            send_sem=send_sem.at[sem],
            recv_sem=recv_sem.at[sem],
            device_id=device,
            device_id_type=MESH,
        )
        copy.start()
        sent.append(copy)
        return copy

    barrier = pltpu.get_barrier_semaphore()
    for k in range(1, shards):
        pl.semaphore_signal(barrier, inc=1, device_id=(peers[k], rep), device_id_type=MESH)
    for device in (x_peer, core_peer):
        pl.semaphore_signal(barrier, inc=1, device_id=device, device_id_type=MESH)

    lines[...] = jnp.zeros(lines.shape, f32)
    lines[0:slot_count, 0:query_count] = (
        owner_line[...] * node_count + row_line[...]
    ).astype(f32)
    lines[slot_count : 2 * slot_count - 3, 0:query_count] = visit_line[...].astype(f32)
    lines[2 * slot_count : 2 * slot_count + 1, 0:neg_count] = neg_line[...].astype(f32)
    columns = jnp.transpose(lines[...])
    info[...] = columns[0:query_count]
    neg_column = columns[0:neg_count, 2 * slot_count : 2 * slot_count + 1].astype(jnp.int32)
    neg_pick = (
        lax.broadcasted_iota(jnp.int32, (neg_count, node_count), 1) == neg_column
    ).astype(bf16)
    loads[0].wait()
    neg_feat = dot(neg_pick, table[...]).astype(bf16)
    for b in range(4):
        feats[b * part : b * part + node_part] = table[b * node_part : (b + 1) * node_part]
        feats[b * part + node_part : (b + 1) * part] = neg_feat[b * neg_part : (b + 1) * neg_part]
    squares = jnp.zeros((4 * part, 1), f32)
    for t in range(tiles):
        loads[1 + t].wait()
        values = dot(feats[...], projection[t])
        pre[:, :, t * tile : (t + 1) * tile] = values.reshape(4, part, tile)
        values = values * jax.nn.sigmoid(values)
        act[:, :, t * tile : (t + 1) * tile] = values.reshape(4, part, tile)
        squares = squares + jnp.sum(values * values, axis=1, keepdims=True)
    squares = squares.reshape(4, part, 1)
    place = lax.broadcasted_iota(jnp.int32, (4, part, 1), 1)
    scale = jnp.where(place >= node_part, lax.rsqrt(squares + epsilon), 1.0)

    pl.semaphore_wait(barrier, shards + 1)

    own_rows = pl.ds(pl.multiple_of(me * query_count, query_count), query_count)
    info_copies = [
        send(info, info_all.at[own_rows], (peers[k], rep)) for k in range(1, shards)
    ]
    info_all[own_rows] = info[...]
    base = shards
    slice_copies = []
    for k in list(range(1, shards)) + [0]:
        columns = pl.ds(pl.multiple_of(peers[k] * width, width), width)
        values = (act[:, :, columns] * scale).astype(bf16)
        if k:
            rows[k] = values
            slice_copies.append(
                send(rows.at[k, mine], slices.at[me, mine], (peers[k], rep))
            )
        else:
            slices[me] = values

    for copy in info_copies:
        copy.wait_recv()
    block = 16

    def pick_rows(step, carry):
        start = pl.multiple_of(step * block, block)
        ids = info_all[pl.ds(start, block)]
        lane = lax.broadcasted_iota(jnp.int32, (block, shards * node_count), 1).astype(f32)
        for s in range(3):
            picks[s, pl.ds(start, block)] = (
                jnp.where(lane == ids[:, s : s + 1], 1.0, 0.0).astype(bf16)
            )
        counts = ids
        spread = jnp.zeros(lane.shape, f32)
        for k in range(3, slot_count):
            spread = spread + jnp.where(
                lane == ids[:, k : k + 1], counts[:, slot_count + k - 3 : slot_count + k - 2], 0.0
            )
        picks[3, pl.ds(start, block)] = spread.astype(bf16)
        return carry

    over_x, over_core, twice = {}, {}, {}

    def pass_on(k):
        slice_copies[k - 1].wait_recv()
        piece = slices.at[sources[k], mine]
        over_x[k] = send(piece, piece, x_peer)
        over_core[k] = send(piece, piece, core_peer)

    def pass_twice(k):
        over_x[k].wait_recv()
        piece = slices.at[sources[k], crossed]
        twice[k] = send(piece, piece, core_peer)

    def gather_from(k):
        source = sources[k]
        if k:
            over_core[k].wait_recv()
            twice[k].wait_recv()
        columns = pl.ds(pl.multiple_of(source * node_count, node_count), node_count)
        values = slices[source, :, :node_part].reshape(node_count, width)
        for kind in range(4):
            part_sum = dot(picks[kind, :, columns], values)
            picked[kind] = picked[kind] + part_sum if k else part_sum

    steps = group // block
    last = shards - 1
    lax.fori_loop(0, steps // 2, pick_rows, 0)
    for k in range(1, shards // 2):
        pass_on(k)
    lax.fori_loop(steps // 2, steps - steps // 4, pick_rows, 0)
    for k in range(shards // 2, shards):
        pass_on(k)
        pass_twice(k - shards // 2 + 1)
    lax.fori_loop(steps - steps // 4, steps, pick_rows, 0)
    for k in range(shards):
        if k + shards // 2 < last:
            pass_twice(k + shards // 2 + 1)
        gather_from(k)
    neg_slice = slices[:, :, node_part:].reshape(shards * neg_count, width)
    counts = info_all[:, slot_count : 2 * slot_count - 3]
    visit_total = jnp.sum(counts, axis=1, keepdims=True)
    hood = picked[0] + picked[3] / visit_total
    pos, hard = picked[1], picked[2]
    partial[...] = dot(hood.astype(bf16), neg_slice, 1, 1).astype(bf16)
    pairs = ((hood, hood), (pos, pos), (hard, hard), (hood, pos), (hood, hard))
    part_rows = query_count // 2

    def half_rows(owner, h):
        start = owner * query_count + h * part_rows
        return pl.ds(pl.multiple_of(start, part_rows), part_rows)

    def send_half(h):
        there = pl.ds(h * part_rows, part_rows)
        return [
            send(partial.at[half_rows(peers[k], h)], parts.at[k, there], (peers[k], rep))
            for k in range(1, shards)
        ]

    score_copies = [send_half(0)]
    stats[...] = lanes_of([jnp.sum(a * b, axis=1, keepdims=True) for a, b in pairs], width)
    stat_copies = []
    for k in range(1, shards):
        there = pl.ds(pl.multiple_of(peers[k] * query_count, query_count), query_count)
        stat_copies.append(send(stats.at[there], stats_all.at[k], (peers[k], rep)))
    score_copies.append(send_half(1))
    slope[...] = silu_slope(pre[mine])
    neg_unit = act[mine, node_part:]
    inverse = lax.rsqrt(jnp.sum(neg_unit * neg_unit, axis=1, keepdims=True) + epsilon)
    neg_unit = neg_unit * inverse
    sums = stats[own_rows]
    for copy in stat_copies:
        copy.wait_recv()
    for k in range(1, shards):
        sums = sums + stats_all[k]
    weight_copies, copies = [], []
    for h in range(2):
        there = half_rows(me, h)
        dots = partial[there].astype(f32)
        for copy in score_copies[h]:
            copy.wait_recv()
        held = slice(h * part_rows, (h + 1) * part_rows)
        for k in range(1, shards):
            dots = dots + parts[k, held].astype(f32)
        weight, scalars = loss_weights(dots, sums[held])
        weight_all[there] = weight
        scalar_all[there] = lanes_of(scalars, width)
        if h:
            copies = [
                send(scalar_all.at[own_rows], scalar_all.at[own_rows], (peers[k], rep))
                for k in range(1, shards)
            ]
        for k in range(1, shards):
            weight_copies.append(
                send(weight_all.at[there], weight_all.at[there], (peers[k], rep))
            )
    for copy in copies:
        copy.wait_recv()
    scalars = scalar_all[...]
    side = item_side(hood, pos, hard, scalars)
    query_unit, query_float, known_grad, pos_grad, hard_grad = side
    flipped[:, 0:group] = jnp.transpose(pos_grad).astype(bf16)
    flipped[:, group : 2 * group] = jnp.transpose(hard_grad).astype(bf16)
    query_flipped = jnp.transpose(query_float).astype(bf16)

    def early_block(s, carry):
        columns = pl.ds(pl.multiple_of(s * node_count, node_count), node_count)
        early[s] = dot(flipped[:, 0:group], picks[1, :, columns]) + dot(
            flipped[:, group : 2 * group], picks[2, :, columns]
        )
        return carry

    lax.fori_loop(0, shards, early_block, 0)
    for copy in weight_copies:
        copy.wait_recv()

    weight = weight_all[...]
    along, inv_q = scalars[:, 5:6], scalars[:, 0:1]
    hood_grad = (dot(weight, neg_slice) + known_grad - query_unit * along) * inv_q
    flipped[:, 2 * group : 3 * group] = jnp.transpose(hood_grad).astype(bf16)
    flipped[:, 3 * group :] = jnp.transpose(hood_grad / visit_total).astype(bf16)
    neg_grad = jnp.transpose(dot(query_flipped, weight))
    back[:, :, node_part:] = neg_grad.reshape(shards, 4, neg_part, width)
    other = pl.ds(2 - half, 2)
    order = list(range(1, shards)) + [0]
    core_copies, x_copies, row_copies = {}, {}, {}

    def to_core(k):
        s = peers[k]
        columns = pl.ds(pl.multiple_of(s * node_count, node_count), node_count)
        total = early[s] + dot(flipped[:, 2 * group : 3 * group], picks[0, :, columns])
        total = total + dot(flipped[:, 3 * group :], picks[3, :, columns])
        back[s, :, :node_part] = jnp.transpose(total).reshape(4, node_part, width)
        core_copies[k] = send(back.at[s, other], core_in.at[s], core_peer)

    def to_x(k):
        s = peers[k]
        core_copies[k].wait_recv()
        across[s] = (back[s, crossed] + core_in[s, 1 - x]).astype(bf16)
        x_copies[k] = send(across.at[s], across_in.at[s], x_peer)

    def to_holder(k):
        s = peers[k]
        x_copies[k].wait_recv()
        total = back[s, mine] + core_in[s, x] + across_in[s].astype(f32)
        if k:
            turned[k] = total.astype(bf16)
            row_copies[k] = send(turned.at[k], landed.at[me], (s, rep))
        else:
            landed[me] = total.astype(bf16)

    lag = 3
    for step in range(shards + lag):
        if step < shards:
            to_core(order[step])
        if step >= lag:
            to_x(order[step - lag])
    for k in order:
        to_holder(k)

    home = [0] + list(range(1, shards))
    to_x_peer, to_core_peer, passed = [], [], []
    for k in home:
        if k:
            row_copies[k].wait_recv()
        s = sources[k]
        columns = pl.ds(pl.multiple_of(s * width, width), width)
        values = landed[s, :node_part].astype(f32) * slope[:node_part, columns]
        pre_grad[s, mine, :node_part] = values.astype(bf16)
        piece = pre_grad.at[s, mine, pl.ds(0, node_part)]
        to_x_peer.append(send(piece, piece, x_peer))
        to_core_peer.append(send(piece, piece, core_peer))
    neg_back = jnp.concatenate(
        [landed[s, node_part:].astype(f32) for s in range(shards)], axis=1
    )
    neg_back = neg_back - neg_unit * jnp.sum(neg_unit * neg_back, axis=1, keepdims=True)
    neg_back = (neg_back * inverse * slope[node_part:]).astype(bf16)
    for s in range(shards):
        pre_grad[s, mine, node_part:] = neg_back[:, s * width : (s + 1) * width]
    piece = pre_grad.at[:, mine, pl.ds(node_part, neg_part)]
    to_x_peer.append(send(piece, piece, x_peer))
    to_core_peer.append(send(piece, piece, core_peer))
    for k in home:
        to_x_peer[k].wait_recv()
        piece = pre_grad.at[sources[k], crossed, pl.ds(0, node_part)]
        passed.append(send(piece, piece, core_peer))
    to_x_peer[shards].wait_recv()
    piece = pre_grad.at[:, crossed, pl.ds(node_part, neg_part)]
    passed.append(send(piece, piece, core_peer))
    placed = (
        lax.broadcasted_iota(jnp.int32, (node_count, neg_count), 0) == neg_line[...]
    ).astype(bf16)
    for copy in to_core_peer + passed:
        copy.wait_recv()
    node_grad = jnp.concatenate(
        [pre_grad[s, :, :node_part].reshape(node_count, width) for s in range(shards)], axis=1
    )
    neg_grad = jnp.concatenate(
        [pre_grad[s, :, node_part:].reshape(neg_count, width) for s in range(shards)], axis=1
    )
    summed[...] = (node_grad.astype(f32) + dot(placed, neg_grad)).astype(bf16)
    feat_tile = out.shape[1] // 4

    def out_tile(f, carry):
        columns = pl.ds(pl.multiple_of(f * feat_tile, feat_tile), feat_tile)
        total = dot(summed[:, 0:tile], projection[0, columns], 1, 1)
        for t in range(1, tiles):
            total = total + dot(
                summed[:, t * tile : (t + 1) * tile], projection[t, columns], 1, 1
            )
        out[:, columns] = total
        return carry

    lax.fori_loop(0, 4, out_tile, 0)
    for copy in sent:
        copy.wait_send()


def column_split(feature_table, projection, slot_owner, slot_row, visits, neg_row):
    shards = lax.axis_size("shard")
    query_count, slot_count = slot_row.shape
    node_count, feat_width = feature_table.shape
    neg_count = neg_row.shape[0]
    embed_width = projection.shape[1]
    width = embed_width // shards
    group = query_count * shards
    part = (node_count + neg_count) // 4
    f32, bf16 = jnp.float32, jnp.bfloat16
    owner_line = jnp.transpose(slot_owner, (1, 2, 0)).reshape(slot_count, query_count)
    sizes = (shards, slot_count, node_count, neg_count, query_count)
    sems = 18 * shards
    tiles = embed_width // (2 * width)
    hbm = pl.BlockSpec(memory_space=pl.ANY)
    vmem = pl.BlockSpec(memory_space=pltpu.VMEM)
    return pl.pallas_call(
        functools.partial(kernel, sizes),
        out_shape=jax.ShapeDtypeStruct((node_count, feat_width), f32),
        in_specs=[hbm] * 2 + [vmem] * 4,
        out_specs=vmem,
        scratch_shapes=[
            pltpu.VMEM((node_count, feat_width), bf16),
            pltpu.VMEM((tiles, feat_width, 2 * width), bf16),
            pltpu.VMEM((128, 128), f32),
            pltpu.VMEM((query_count, width), f32),
            pltpu.VMEM((part, embed_width), f32),
            pltpu.VMEM((shards, width, node_count), f32),
            pltpu.VMEM((node_count, embed_width), bf16),
            pltpu.VMEM((4 * part, feat_width), bf16),
            pltpu.VMEM((4, part, embed_width), f32),
            pltpu.VMEM((4, part, embed_width), f32),
            pltpu.VMEM((group, width), f32),
            pltpu.VMEM((shards, 4, part, width), bf16),
            pltpu.VMEM((shards, 4, part, width), bf16),
            pltpu.VMEM((4, group, shards * node_count), bf16),
            pltpu.VMEM((4, group, width), f32),
            pltpu.VMEM((group, shards * neg_count), bf16),
            pltpu.VMEM((shards, query_count, shards * neg_count), bf16),
            pltpu.VMEM((group, width), f32),
            pltpu.VMEM((shards, query_count, width), f32),
            pltpu.VMEM((group, shards * neg_count), bf16),
            pltpu.VMEM((group, width), f32),
            pltpu.VMEM((width, 4 * group), bf16),
            pltpu.VMEM((shards, 4, part, width), f32),
            pltpu.VMEM((shards, 2, part, width), f32),
            pltpu.VMEM((shards, part, width), bf16),
            pltpu.VMEM((shards, part, width), bf16),
            pltpu.VMEM((shards, part, width), bf16),
            pltpu.VMEM((shards, part, width), bf16),
            pltpu.VMEM((shards, 4, part, width), bf16),
            pltpu.SemaphoreType.DMA((sems,)),
            pltpu.SemaphoreType.DMA((sems,)),
            pltpu.SemaphoreType.DMA((tiles + 1,)),
        ],
        compiler_params=pltpu.CompilerParams(
            collective_id=0, has_side_effects=True, vmem_limit_bytes=60 * 1024 * 1024
        ),
    )(
        feature_table,
        projection,
        owner_line,
        jnp.transpose(slot_row),
        jnp.transpose(visits),
        neg_row.reshape(1, neg_count),
    )


def solution(mesh):
    shards, reps = mesh.shape["shard"], mesh.shape["rep"]

    def body(feature_table, projection, slot_owner, slot_row, visits, neg_row):
        width = projection.shape[1] // shards
        parts = (feature_table.shape[0], neg_row.shape[0], slot_row.shape[0] * 2)
        small = slot_row.shape[0] <= 128 and neg_row.shape[0] <= 128 and slot_row.shape[1] <= 32
        whole = width == 128 and reps == 4 and small and all(size % 64 == 0 for size in parts)
        form = column_split if whole else on_device
        return form(feature_table, projection, slot_owner, slot_row, visits, neg_row)

    return jax.shard_map(
        body,
        mesh=mesh,
        in_specs=(
            P("shard", None),
            P(),
            P(("shard", "rep"), None, None),
            P(("shard", "rep"), None),
            P(("shard", "rep"), None),
            P("shard"),
        ),
        out_specs=P("shard", None),
        check_vma=False,
    )
```

```python
import functools

import jax
import jax.numpy as jnp
from jax import lax
from jax.experimental import pallas as pl
from jax.experimental.pallas import tpu as pltpu
from jax.sharding import PartitionSpec as P

MESH = pl.DeviceIdType.MESH

score_scale = 8.0
margin_value = 0.1
epsilon = 1e-06


def unit_rows(values):
    norms = jnp.sqrt(jnp.sum(values * values, axis=-1, keepdims=True) + epsilon)
    return (values / norms, norms)


def unit_back(grads, unit, norms):
    return (grads - unit * jnp.sum(unit * grads, axis=-1, keepdims=True)) / norms


def silu_slope(preact):
    gate_value = jax.nn.sigmoid(preact)
    return gate_value * (1.0 + preact * (1.0 - gate_value))


def times_back(left, projection):
    return jnp.einsum("re,fe->rf", left, projection, preferred_element_type=jnp.float32)


def on_device(feature_table, projection, slot_owner, slot_row, visits, neg_row):
    shard_count = lax.axis_size("shard")
    query_count, slot_count = slot_row.shape
    row_count = query_count * slot_count
    capacity = 2 * row_count // shard_count
    feat_width = projection.shape[0]
    embed_width = projection.shape[1]
    owners = slot_owner.reshape(row_count)
    one_hot = (owners[:, None] == jnp.arange(shard_count, dtype=jnp.int32)[None, :]).astype(
        jnp.int32
    )
    earlier = jnp.cumsum(one_hot, axis=0) - one_hot
    slot_rank = jnp.sum(earlier * one_hot, axis=1)
    position = owners * capacity + slot_rank
    send_ids = (
        jnp.zeros((shard_count * capacity,), jnp.int32)
        .at[position]
        .set(slot_row.reshape(row_count))
    )
    send_ids = send_ids.reshape(shard_count, capacity)
    asked = lax.all_to_all(send_ids, "shard", split_axis=0, concat_axis=0, tiled=True)
    picked = feature_table[asked]
    fetched = lax.all_to_all(picked, "shard", split_axis=0, concat_axis=0, tiled=True)
    gathered = fetched.reshape(shard_count * capacity, feat_width)[position]
    neg_pre = jnp.dot(feature_table[neg_row], projection, preferred_element_type=jnp.float32)
    neg_unit, neg_norms = unit_rows(jax.nn.silu(neg_pre))
    neg_embed = lax.all_gather(neg_unit.astype(jnp.bfloat16), "shard", axis=0, tiled=True)
    visit_float = visits.astype(jnp.float32)
    coefs = visit_float / jnp.sum(visit_float, axis=1, keepdims=True)
    preact = jnp.dot(gathered, projection, preferred_element_type=jnp.float32).reshape(
        query_count, slot_count, embed_width
    )
    active = jax.nn.silu(preact)
    hood = active[:, 0] + jnp.einsum("bk,bke->be", coefs, active[:, 3:])
    query_unit, query_norms = unit_rows(hood)
    query_embed = query_unit.astype(jnp.bfloat16)
    item_unit, item_norms = unit_rows(active[:, 1:3])
    item_embed = item_unit.astype(jnp.bfloat16)
    query_float = query_embed.astype(jnp.float32)
    item_float = item_embed.astype(jnp.float32)
    neg_scores = jnp.einsum("be,ne->bn", query_embed, neg_embed, preferred_element_type=jnp.float32)
    pair_scores = jnp.sum(query_float[:, None, :] * item_float, axis=2)
    positive = pair_scores[:, 0:1]
    neg_weight = (
        score_scale * jax.nn.sigmoid(score_scale * (neg_scores - positive + margin_value))
    ).astype(jnp.bfloat16)
    hard_weight = (
        score_scale * jax.nn.sigmoid(score_scale * (pair_scores[:, 1:2] - positive + margin_value))
    ).astype(jnp.bfloat16)
    hard_float = hard_weight.astype(jnp.float32)
    total_weight = jnp.sum(neg_weight.astype(jnp.float32), axis=1, keepdims=True) + hard_float
    query_grad = (
        jnp.dot(neg_weight, neg_embed, preferred_element_type=jnp.float32)
        + hard_float * item_float[:, 1]
        - total_weight * item_float[:, 0]
    )
    item_grad = jnp.stack([-total_weight * query_float, hard_float * query_float], axis=1)
    neg_partial = jnp.einsum(
        "bn,be->ne", neg_weight, query_embed, preferred_element_type=jnp.float32
    )
    hood_grad = unit_back(query_grad, query_unit, query_norms)
    item_back = unit_back(item_grad, item_unit, item_norms)
    active_grad = jnp.concatenate(
        [hood_grad[:, None], item_back, coefs[:, :, None] * hood_grad[:, None]], axis=1
    )
    preact_grad = (
        (active_grad * silu_slope(preact)).astype(jnp.bfloat16).reshape(row_count, embed_width)
    )
    outgoing = (
        jnp.zeros((shard_count * capacity, embed_width), jnp.bfloat16).at[position].set(preact_grad)
    )
    incoming = lax.all_to_all(
        outgoing.reshape(shard_count, capacity, embed_width),
        "shard",
        split_axis=0,
        concat_axis=0,
        tiled=True,
    )
    contrib = times_back(incoming.reshape(shard_count * capacity, embed_width), projection)
    neg_sum = lax.psum_scatter(neg_partial, "shard", scatter_dimension=0, tiled=True)
    grad_local = (
        jnp.zeros((feature_table.shape[0], feat_width), jnp.float32)
        .at[asked.reshape(-1)]
        .add(contrib)
    )
    grad_local, neg_total = lax.psum((grad_local, neg_sum), "rep")
    neg_back = unit_back(neg_total, neg_unit, neg_norms)
    neg_pre_grad = (neg_back * silu_slope(neg_pre)).astype(jnp.bfloat16)
    neg_rows = times_back(neg_pre_grad, projection)
    return grad_local.at[neg_row].add(neg_rows)


def dot(left, right, left_dim=1, right_dim=0):
    return lax.dot_general(
        left, right, (((left_dim,), (right_dim,)), ((), ())), preferred_element_type=jnp.float32
    )


def lanes_of(columns, width):
    rows = columns[0].shape[0]
    lane = lax.broadcasted_iota(jnp.int32, (rows, width), 1)
    result = jnp.zeros((rows, width), jnp.float32)
    for place, column in enumerate(columns):
        result = jnp.where(lane == place, column, result)
    return result


def loss_weights(dots, stats):
    inverse = lax.rsqrt(stats[:, 0:3] + epsilon)
    inv_q, inv_p, inv_h = inverse[:, 0:1], inverse[:, 1:2], inverse[:, 2:3]
    scores = dots * inv_q
    positive = stats[:, 3:4] * inv_q * inv_p
    hard = stats[:, 4:5] * inv_q * inv_h
    weight = score_scale * jax.nn.sigmoid(score_scale * (scores - positive + margin_value))
    weight = weight.astype(jnp.bfloat16)
    wide = weight.astype(jnp.float32)
    hard_weight = score_scale * jax.nn.sigmoid(score_scale * (hard - positive + margin_value))
    hard_weight = hard_weight.astype(jnp.bfloat16).astype(jnp.float32)
    total = jnp.sum(wide, axis=1, keepdims=True) + hard_weight
    along = jnp.sum(wide * scores, axis=1, keepdims=True) + hard_weight * hard - total * positive
    return weight, [inv_q, inv_p, inv_h, hard_weight, total, along, positive, hard]


def item_side(hood, pos, hard, scalars):
    f32, bf16 = jnp.float32, jnp.bfloat16
    inv_q, inv_p, inv_h, hard_weight, total, along, pos_score, hard_score = [
        scalars[:, i : i + 1] for i in range(8)
    ]
    query_unit, pos_unit, hard_unit = hood * inv_q, pos * inv_p, hard * inv_h
    query_float = query_unit.astype(bf16).astype(f32)
    known_grad = hard_weight * hard_unit.astype(bf16).astype(
        f32
    ) - total * pos_unit.astype(bf16).astype(f32)
    pos_grad = -total * (query_float - pos_unit * pos_score) * inv_p
    hard_grad = hard_weight * (query_float - hard_unit * hard_score) * inv_h
    return query_unit, query_float, known_grad, pos_grad, hard_grad


def kernel(
    sizes,
    table_hbm,
    projection_hbm,
    owner_line,
    row_line,
    visit_line,
    neg_line,
    out,
    table,
    projection,
    lines,
    info,
    slope,
    early,
    summed,
    feats,
    pre,
    act,
    info_all,
    rows,
    slices,
    picks,
    picked,
    partial,
    parts,
    stats,
    stats_all,
    weight_all,
    scalar_all,
    flipped,
    back,
    core_in,
    across,
    across_in,
    turned,
    landed,
    pre_grad,
    send_sem,
    recv_sem,
    local_sem,
):
    shards, slot_count, node_count, neg_count, query_count = sizes
    f32, bf16 = jnp.float32, jnp.bfloat16
    width = slices.shape[3]
    embed_width = projection_hbm.shape[1]
    node_part, neg_part = node_count // 4, neg_count // 4
    part = node_part + neg_part
    group = query_count * shards
    me, rep = lax.axis_index("shard"), lax.axis_index("rep")
    x, core = rep // 2, rep % 2
    mine, half = 2 * core + x, 2 * core
    crossed = 2 * core + 1 - x
    x_peer = (me, (1 - x) * 2 + core)
    core_peer = (me, x * 2 + 1 - core)
    peers = [lax.rem(me + k, shards) for k in range(shards)]
    sources = [lax.rem(me + shards - k, shards) for k in range(shards)]
    sent = []
    tile = 2 * width
    tiles = embed_width // tile
    loads = [pltpu.make_async_copy(table_hbm, table, local_sem.at[tiles])]
    for t in range(tiles):
        columns = pl.ds(t * tile, tile)
        loads.append(
            pltpu.make_async_copy(
                projection_hbm.at[:, columns], projection.at[t], local_sem.at[t]
            )
        )
    for load in loads:
        load.start()

    def send(source, target, device):
        sem = len(sent)
        copy = pltpu.make_async_remote_copy(
            src_ref=source,
            dst_ref=target,
            send_sem=send_sem.at[sem],
            recv_sem=recv_sem.at[sem],
            device_id=device,
            device_id_type=MESH,
        )
        copy.start()
        sent.append(copy)
        return copy

    barrier = pltpu.get_barrier_semaphore()
    for k in range(1, shards):
        pl.semaphore_signal(barrier, inc=1, device_id=(peers[k], rep), device_id_type=MESH)
    for device in (x_peer, core_peer):
        pl.semaphore_signal(barrier, inc=1, device_id=device, device_id_type=MESH)

    lines[...] = jnp.zeros(lines.shape, f32)
    lines[0:slot_count, 0:query_count] = owner_line[...].astype(f32)
    lines[slot_count : 2 * slot_count, 0:query_count] = row_line[...].astype(f32)
    lines[2 * slot_count : 3 * slot_count - 3, 0:query_count] = visit_line[...].astype(f32)
    lines[3 * slot_count : 3 * slot_count + 1, 0:neg_count] = neg_line[...].astype(f32)
    columns = jnp.transpose(lines[...])
    info[...] = columns[0:query_count]
    neg_column = columns[0:neg_count, 3 * slot_count : 3 * slot_count + 1].astype(jnp.int32)
    neg_pick = (
        lax.broadcasted_iota(jnp.int32, (neg_count, node_count), 1) == neg_column
    ).astype(bf16)
    loads[0].wait()
    neg_feat = dot(neg_pick, table[...]).astype(bf16)
    for b in range(4):
        feats[b * part : b * part + node_part] = table[b * node_part : (b + 1) * node_part]
        feats[b * part + node_part : (b + 1) * part] = neg_feat[b * neg_part : (b + 1) * neg_part]
    pl.semaphore_wait(barrier, shards + 1)

    own_rows = pl.ds(pl.multiple_of(me * query_count, query_count), query_count)
    info_copies = [
        send(info, info_all.at[own_rows], (peers[k], rep)) for k in range(1, shards)
    ]
    info_all[own_rows] = info[...]
    base = shards
    squares = jnp.zeros((4 * part, 1), f32)
    for t in range(tiles):
        loads[1 + t].wait()
        values = dot(feats[...], projection[t])
        pre[:, :, t * tile : (t + 1) * tile] = values.reshape(4, part, tile)
        values = values * jax.nn.sigmoid(values)
        act[:, :, t * tile : (t + 1) * tile] = values.reshape(4, part, tile)
        squares = squares + jnp.sum(values * values, axis=1, keepdims=True)
    squares = squares.reshape(4, part, 1)
    place = lax.broadcasted_iota(jnp.int32, (4, part, 1), 1)
    scale = jnp.where(place >= node_part, lax.rsqrt(squares + epsilon), 1.0)

    slice_copies = []
    for k in list(range(1, shards)) + [0]:
        columns = pl.ds(pl.multiple_of(peers[k] * width, width), width)
        values = (act[:, :, columns] * scale).astype(bf16)
        if k:
            rows[k] = values
            slice_copies.append(
                send(rows.at[k, mine], slices.at[me, mine], (peers[k], rep))
            )
        else:
            slices[me] = values

    for copy in info_copies:
        copy.wait_recv()
    block = 16

    chunks = node_count // width
    zero = jnp.zeros((block, width), bf16)
    lane = lax.broadcasted_iota(jnp.int32, (block, width), 1)
    lanes = [(lane + c * width).astype(f32).astype(bf16) for c in range(chunks)]

    def pick_rows(step, carry):
        here = pl.ds(pl.multiple_of(step * block, block), block)
        ids = info_all[here]

        def wide(column):
            return jnp.broadcast_to(ids[:, column : column + 1], (block, width)).astype(bf16)

        def hits(slot, amount):
            owner, row = wide(slot), wide(slot_count + slot)
            found = [row == place for place in lanes]
            for shard in range(shards):
                held = jnp.where(owner == jnp.asarray(shard, bf16), amount, zero)
                for c in range(chunks):
                    yield shard * chunks + c, jnp.where(found[c], held, zero)

        for slot in range(3):
            for place, value in hits(slot, jnp.ones((block, width), bf16)):
                picks[slot, here, place * width : (place + 1) * width] = value
        spread = [zero] * (shards * chunks)
        for slot in range(3, slot_count):
            for place, value in hits(slot, wide(2 * slot_count + slot - 3)):
                spread[place] = spread[place] + value
        for place, value in enumerate(spread):
            picks[3, here, place * width : (place + 1) * width] = value
        return carry

    over_x, over_core, twice = {}, {}, {}

    def pass_on(k):
        slice_copies[k - 1].wait_recv()
        piece = slices.at[sources[k], mine]
        over_x[k] = send(piece, piece, x_peer)
        over_core[k] = send(piece, piece, core_peer)

    def pass_twice(k):
        over_x[k].wait_recv()
        piece = slices.at[sources[k], crossed]
        twice[k] = send(piece, piece, core_peer)

    def gather_from(k):
        source = sources[k]
        if k:
            over_core[k].wait_recv()
            twice[k].wait_recv()
        columns = pl.ds(pl.multiple_of(source * node_count, node_count), node_count)
        values = slices[source, :, :node_part].reshape(node_count, width)
        for kind in range(4):
            part_sum = dot(picks[kind, :, columns], values)
            picked[kind] = picked[kind] + part_sum if k else part_sum

    steps = group // block
    last = shards - 1
    lax.fori_loop(0, steps // 2, pick_rows, 0)
    for k in range(1, shards // 2):
        pass_on(k)
    lax.fori_loop(steps // 2, steps - steps // 4, pick_rows, 0)
    for k in range(shards // 2, shards):
        pass_on(k)
        pass_twice(k - shards // 2 + 1)
    lax.fori_loop(steps - steps // 4, steps, pick_rows, 0)
    for k in range(shards):
        if k + shards // 2 < last:
            pass_twice(k + shards // 2 + 1)
        gather_from(k)
    neg_slice = slices[:, :, node_part:].reshape(shards * neg_count, width)
    counts = info_all[:, 2 * slot_count : 3 * slot_count - 3]
    visit_total = jnp.sum(counts, axis=1, keepdims=True)
    hood = picked[0] + picked[3] / visit_total
    pos, hard = picked[1], picked[2]
    partial[...] = dot(hood.astype(bf16), neg_slice, 1, 1).astype(bf16)
    pairs = ((hood, hood), (pos, pos), (hard, hard), (hood, pos), (hood, hard))
    part_rows = query_count // 2

    def half_rows(owner, h):
        start = owner * query_count + h * part_rows
        return pl.ds(pl.multiple_of(start, part_rows), part_rows)

    def send_half(h):
        there = pl.ds(h * part_rows, part_rows)
        return [
            send(partial.at[half_rows(peers[k], h)], parts.at[k, there], (peers[k], rep))
            for k in range(1, shards)
        ]

    score_copies = [send_half(0)]
    stats[...] = lanes_of([jnp.sum(a * b, axis=1, keepdims=True) for a, b in pairs], width)
    stat_copies = []
    for k in range(1, shards):
        there = pl.ds(pl.multiple_of(peers[k] * query_count, query_count), query_count)
        stat_copies.append(send(stats.at[there], stats_all.at[k], (peers[k], rep)))
    score_copies.append(send_half(1))
    slope[...] = silu_slope(pre[mine])
    neg_unit = act[mine, node_part:]
    inverse = lax.rsqrt(jnp.sum(neg_unit * neg_unit, axis=1, keepdims=True) + epsilon)
    neg_unit = neg_unit * inverse
    sums = stats[own_rows]
    for copy in stat_copies:
        copy.wait_recv()
    for k in range(1, shards):
        sums = sums + stats_all[k]
    weight_copies, copies = [], []
    for h in range(2):
        there = half_rows(me, h)
        dots = partial[there].astype(f32)
        for copy in score_copies[h]:
            copy.wait_recv()
        held = slice(h * part_rows, (h + 1) * part_rows)
        for k in range(1, shards):
            dots = dots + parts[k, held].astype(f32)
        weight, scalars = loss_weights(dots, sums[held])
        weight_all[there] = weight
        scalar_all[there] = lanes_of(scalars, width)
        if h:
            copies = [
                send(scalar_all.at[own_rows], scalar_all.at[own_rows], (peers[k], rep))
                for k in range(1, shards)
            ]
        for k in range(1, shards):
            weight_copies.append(
                send(weight_all.at[there], weight_all.at[there], (peers[k], rep))
            )
    for copy in copies:
        copy.wait_recv()
    scalars = scalar_all[...]
    side = item_side(hood, pos, hard, scalars)
    query_unit, query_float, known_grad, pos_grad, hard_grad = side
    flipped[:, 0:group] = jnp.transpose(pos_grad).astype(bf16)
    flipped[:, group : 2 * group] = jnp.transpose(hard_grad).astype(bf16)
    query_flipped = jnp.transpose(query_float).astype(bf16)

    def early_block(s, carry):
        columns = pl.ds(pl.multiple_of(s * node_count, node_count), node_count)
        early[s] = dot(flipped[:, 0:group], picks[1, :, columns]) + dot(
            flipped[:, group : 2 * group], picks[2, :, columns]
        )
        return carry

    lax.fori_loop(0, shards, early_block, 0)
    for copy in weight_copies:
        copy.wait_recv()

    weight = weight_all[...]
    along, inv_q = scalars[:, 5:6], scalars[:, 0:1]
    hood_grad = (dot(weight, neg_slice) + known_grad - query_unit * along) * inv_q
    flipped[:, 2 * group : 3 * group] = jnp.transpose(hood_grad).astype(bf16)
    flipped[:, 3 * group :] = jnp.transpose(hood_grad / visit_total).astype(bf16)
    neg_grad = jnp.transpose(dot(query_flipped, weight))
    back[:, :, node_part:] = neg_grad.reshape(shards, 4, neg_part, width)
    other = pl.ds(2 - half, 2)
    order = list(range(1, shards)) + [0]
    core_copies, x_copies, row_copies = {}, {}, {}

    def to_core(k):
        s = peers[k]
        columns = pl.ds(pl.multiple_of(s * node_count, node_count), node_count)
        total = early[s] + dot(flipped[:, 2 * group : 3 * group], picks[0, :, columns])
        total = total + dot(flipped[:, 3 * group :], picks[3, :, columns])
        back[s, :, :node_part] = jnp.transpose(total).reshape(4, node_part, width)
        core_copies[k] = send(back.at[s, other], core_in.at[s], core_peer)

    def to_x(k):
        s = peers[k]
        core_copies[k].wait_recv()
        across[s] = (back[s, crossed] + core_in[s, 1 - x]).astype(bf16)
        x_copies[k] = send(across.at[s], across_in.at[s], x_peer)

    def to_holder(k):
        s = peers[k]
        x_copies[k].wait_recv()
        total = back[s, mine] + core_in[s, x] + across_in[s].astype(f32)
        if k:
            turned[k] = total.astype(bf16)
            row_copies[k] = send(turned.at[k], landed.at[me], (s, rep))
        else:
            landed[me] = total.astype(bf16)

    lag = 3
    for step in range(shards + lag):
        if step < shards:
            to_core(order[step])
        if step >= lag:
            to_x(order[step - lag])
    for k in order:
        to_holder(k)

    home = [0] + list(range(1, shards))
    to_x_peer, to_core_peer, passed = [], [], []
    for k in home:
        if k:
            row_copies[k].wait_recv()
        s = sources[k]
        columns = pl.ds(pl.multiple_of(s * width, width), width)
        values = landed[s, :node_part].astype(f32) * slope[:node_part, columns]
        pre_grad[s, mine, :node_part] = values.astype(bf16)
        piece = pre_grad.at[s, mine, pl.ds(0, node_part)]
        to_x_peer.append(send(piece, piece, x_peer))
        to_core_peer.append(send(piece, piece, core_peer))
    neg_back = jnp.concatenate(
        [landed[s, node_part:].astype(f32) for s in range(shards)], axis=1
    )
    neg_back = neg_back - neg_unit * jnp.sum(neg_unit * neg_back, axis=1, keepdims=True)
    neg_back = (neg_back * inverse * slope[node_part:]).astype(bf16)
    for s in range(shards):
        pre_grad[s, mine, node_part:] = neg_back[:, s * width : (s + 1) * width]
    piece = pre_grad.at[:, mine, pl.ds(node_part, neg_part)]
    to_x_peer.append(send(piece, piece, x_peer))
    to_core_peer.append(send(piece, piece, core_peer))
    for k in home:
        to_x_peer[k].wait_recv()
        piece = pre_grad.at[sources[k], crossed, pl.ds(0, node_part)]
        passed.append(send(piece, piece, core_peer))
    to_x_peer[shards].wait_recv()
    piece = pre_grad.at[:, crossed, pl.ds(node_part, neg_part)]
    passed.append(send(piece, piece, core_peer))
    placed = (
        lax.broadcasted_iota(jnp.int32, (node_count, neg_count), 0) == neg_line[...]
    ).astype(bf16)
    for copy in to_core_peer + passed:
        copy.wait_recv()
    node_grad = jnp.concatenate(
        [pre_grad[s, :, :node_part].reshape(node_count, width) for s in range(shards)], axis=1
    )
    neg_grad = jnp.concatenate(
        [pre_grad[s, :, node_part:].reshape(neg_count, width) for s in range(shards)], axis=1
    )
    summed[...] = (node_grad.astype(f32) + dot(placed, neg_grad)).astype(bf16)
    feat_tile = out.shape[1] // 4

    def out_tile(f, carry):
        columns = pl.ds(pl.multiple_of(f * feat_tile, feat_tile), feat_tile)
        total = dot(summed[:, 0:tile], projection[0, columns], 1, 1)
        for t in range(1, tiles):
            total = total + dot(
                summed[:, t * tile : (t + 1) * tile], projection[t, columns], 1, 1
            )
        out[:, columns] = total
        return carry

    lax.fori_loop(0, 4, out_tile, 0)
    for copy in sent:
        copy.wait_send()


def column_split(feature_table, projection, slot_owner, slot_row, visits, neg_row):
    shards = lax.axis_size("shard")
    query_count, slot_count = slot_row.shape
    node_count, feat_width = feature_table.shape
    neg_count = neg_row.shape[0]
    embed_width = projection.shape[1]
    width = embed_width // shards
    group = query_count * shards
    part = (node_count + neg_count) // 4
    f32, bf16 = jnp.float32, jnp.bfloat16
    owner_line = jnp.transpose(slot_owner, (1, 2, 0)).reshape(slot_count, query_count)
    sizes = (shards, slot_count, node_count, neg_count, query_count)
    sems = 18 * shards
    tiles = embed_width // (2 * width)
    hbm = pl.BlockSpec(memory_space=pl.ANY)
    vmem = pl.BlockSpec(memory_space=pltpu.VMEM)
    return pl.pallas_call(
        functools.partial(kernel, sizes),
        out_shape=jax.ShapeDtypeStruct((node_count, feat_width), f32),
        in_specs=[hbm] * 2 + [vmem] * 4,
        out_specs=vmem,
        scratch_shapes=[
            pltpu.VMEM((node_count, feat_width), bf16),
            pltpu.VMEM((tiles, feat_width, 2 * width), bf16),
            pltpu.VMEM((128, 128), f32),
            pltpu.VMEM((query_count, width), f32),
            pltpu.VMEM((part, embed_width), f32),
            pltpu.VMEM((shards, width, node_count), f32),
            pltpu.VMEM((node_count, embed_width), bf16),
            pltpu.VMEM((4 * part, feat_width), bf16),
            pltpu.VMEM((4, part, embed_width), f32),
            pltpu.VMEM((4, part, embed_width), f32),
            pltpu.VMEM((group, width), f32),
            pltpu.VMEM((shards, 4, part, width), bf16),
            pltpu.VMEM((shards, 4, part, width), bf16),
            pltpu.VMEM((4, group, shards * node_count), bf16),
            pltpu.VMEM((4, group, width), f32),
            pltpu.VMEM((group, shards * neg_count), bf16),
            pltpu.VMEM((shards, query_count, shards * neg_count), bf16),
            pltpu.VMEM((group, width), f32),
            pltpu.VMEM((shards, query_count, width), f32),
            pltpu.VMEM((group, shards * neg_count), bf16),
            pltpu.VMEM((group, width), f32),
            pltpu.VMEM((width, 4 * group), bf16),
            pltpu.VMEM((shards, 4, part, width), f32),
            pltpu.VMEM((shards, 2, part, width), f32),
            pltpu.VMEM((shards, part, width), bf16),
            pltpu.VMEM((shards, part, width), bf16),
            pltpu.VMEM((shards, part, width), bf16),
            pltpu.VMEM((shards, part, width), bf16),
            pltpu.VMEM((shards, 4, part, width), bf16),
            pltpu.SemaphoreType.DMA((sems,)),
            pltpu.SemaphoreType.DMA((sems,)),
            pltpu.SemaphoreType.DMA((tiles + 1,)),
        ],
        compiler_params=pltpu.CompilerParams(
            collective_id=0, has_side_effects=True, vmem_limit_bytes=60 * 1024 * 1024
        ),
    )(
        feature_table,
        projection,
        owner_line,
        jnp.transpose(slot_row),
        jnp.transpose(visits),
        neg_row.reshape(1, neg_count),
    )


def solution(mesh):
    shards, reps = mesh.shape["shard"], mesh.shape["rep"]

    def body(feature_table, projection, slot_owner, slot_row, visits, neg_row):
        width = projection.shape[1] // shards
        parts = (feature_table.shape[0], neg_row.shape[0], slot_row.shape[0] * 2)
        small = slot_row.shape[0] <= 128 and neg_row.shape[0] <= 128 and slot_row.shape[1] <= 40
        small = small and feature_table.shape[0] in (width, 2 * width)
        whole = width == 128 and reps == 4 and small and all(size % 64 == 0 for size in parts)
        form = column_split if whole else on_device
        return form(feature_table, projection, slot_owner, slot_row, visits, neg_row)

    return jax.shard_map(
        body,
        mesh=mesh,
        in_specs=(
            P("shard", None),
            P(),
            P(("shard", "rep"), None, None),
            P(("shard", "rep"), None),
            P(("shard", "rep"), None),
            P("shard"),
        ),
        out_specs=P("shard", None),
        check_vma=False,
    )
```

```python
import functools

import jax
import jax.numpy as jnp
from jax import lax
from jax.experimental import pallas as pl
from jax.experimental.pallas import tpu as pltpu
from jax.sharding import PartitionSpec as P

MESH = pl.DeviceIdType.MESH

score_scale = 8.0
margin_value = 0.1
epsilon = 1e-06


def unit_rows(values):
    norms = jnp.sqrt(jnp.sum(values * values, axis=-1, keepdims=True) + epsilon)
    return (values / norms, norms)


def unit_back(grads, unit, norms):
    return (grads - unit * jnp.sum(unit * grads, axis=-1, keepdims=True)) / norms


def silu_slope(preact):
    gate_value = jax.nn.sigmoid(preact)
    return gate_value * (1.0 + preact * (1.0 - gate_value))


def times_back(left, projection):
    return jnp.einsum("re,fe->rf", left, projection, preferred_element_type=jnp.float32)


def on_device(feature_table, projection, slot_owner, slot_row, visits, neg_row):
    shard_count = lax.axis_size("shard")
    query_count, slot_count = slot_row.shape
    row_count = query_count * slot_count
    capacity = 2 * row_count // shard_count
    feat_width = projection.shape[0]
    embed_width = projection.shape[1]
    owners = slot_owner.reshape(row_count)
    one_hot = (owners[:, None] == jnp.arange(shard_count, dtype=jnp.int32)[None, :]).astype(
        jnp.int32
    )
    earlier = jnp.cumsum(one_hot, axis=0) - one_hot
    slot_rank = jnp.sum(earlier * one_hot, axis=1)
    position = owners * capacity + slot_rank
    send_ids = (
        jnp.zeros((shard_count * capacity,), jnp.int32)
        .at[position]
        .set(slot_row.reshape(row_count))
    )
    send_ids = send_ids.reshape(shard_count, capacity)
    asked = lax.all_to_all(send_ids, "shard", split_axis=0, concat_axis=0, tiled=True)
    picked = feature_table[asked]
    fetched = lax.all_to_all(picked, "shard", split_axis=0, concat_axis=0, tiled=True)
    gathered = fetched.reshape(shard_count * capacity, feat_width)[position]
    neg_pre = jnp.dot(feature_table[neg_row], projection, preferred_element_type=jnp.float32)
    neg_unit, neg_norms = unit_rows(jax.nn.silu(neg_pre))
    neg_embed = lax.all_gather(neg_unit.astype(jnp.bfloat16), "shard", axis=0, tiled=True)
    visit_float = visits.astype(jnp.float32)
    coefs = visit_float / jnp.sum(visit_float, axis=1, keepdims=True)
    preact = jnp.dot(gathered, projection, preferred_element_type=jnp.float32).reshape(
        query_count, slot_count, embed_width
    )
    active = jax.nn.silu(preact)
    hood = active[:, 0] + jnp.einsum("bk,bke->be", coefs, active[:, 3:])
    query_unit, query_norms = unit_rows(hood)
    query_embed = query_unit.astype(jnp.bfloat16)
    item_unit, item_norms = unit_rows(active[:, 1:3])
    item_embed = item_unit.astype(jnp.bfloat16)
    query_float = query_embed.astype(jnp.float32)
    item_float = item_embed.astype(jnp.float32)
    neg_scores = jnp.einsum("be,ne->bn", query_embed, neg_embed, preferred_element_type=jnp.float32)
    pair_scores = jnp.sum(query_float[:, None, :] * item_float, axis=2)
    positive = pair_scores[:, 0:1]
    neg_weight = (
        score_scale * jax.nn.sigmoid(score_scale * (neg_scores - positive + margin_value))
    ).astype(jnp.bfloat16)
    hard_weight = (
        score_scale * jax.nn.sigmoid(score_scale * (pair_scores[:, 1:2] - positive + margin_value))
    ).astype(jnp.bfloat16)
    hard_float = hard_weight.astype(jnp.float32)
    total_weight = jnp.sum(neg_weight.astype(jnp.float32), axis=1, keepdims=True) + hard_float
    query_grad = (
        jnp.dot(neg_weight, neg_embed, preferred_element_type=jnp.float32)
        + hard_float * item_float[:, 1]
        - total_weight * item_float[:, 0]
    )
    item_grad = jnp.stack([-total_weight * query_float, hard_float * query_float], axis=1)
    neg_partial = jnp.einsum(
        "bn,be->ne", neg_weight, query_embed, preferred_element_type=jnp.float32
    )
    hood_grad = unit_back(query_grad, query_unit, query_norms)
    item_back = unit_back(item_grad, item_unit, item_norms)
    active_grad = jnp.concatenate(
        [hood_grad[:, None], item_back, coefs[:, :, None] * hood_grad[:, None]], axis=1
    )
    preact_grad = (
        (active_grad * silu_slope(preact)).astype(jnp.bfloat16).reshape(row_count, embed_width)
    )
    outgoing = (
        jnp.zeros((shard_count * capacity, embed_width), jnp.bfloat16).at[position].set(preact_grad)
    )
    incoming = lax.all_to_all(
        outgoing.reshape(shard_count, capacity, embed_width),
        "shard",
        split_axis=0,
        concat_axis=0,
        tiled=True,
    )
    contrib = times_back(incoming.reshape(shard_count * capacity, embed_width), projection)
    neg_sum = lax.psum_scatter(neg_partial, "shard", scatter_dimension=0, tiled=True)
    grad_local = (
        jnp.zeros((feature_table.shape[0], feat_width), jnp.float32)
        .at[asked.reshape(-1)]
        .add(contrib)
    )
    grad_local, neg_total = lax.psum((grad_local, neg_sum), "rep")
    neg_back = unit_back(neg_total, neg_unit, neg_norms)
    neg_pre_grad = (neg_back * silu_slope(neg_pre)).astype(jnp.bfloat16)
    neg_rows = times_back(neg_pre_grad, projection)
    return grad_local.at[neg_row].add(neg_rows)


def dot(left, right, left_dim=1, right_dim=0):
    return lax.dot_general(
        left, right, (((left_dim,), (right_dim,)), ((), ())), preferred_element_type=jnp.float32
    )


def lanes_of(columns, width):
    rows = columns[0].shape[0]
    lane = lax.broadcasted_iota(jnp.int32, (rows, width), 1)
    result = jnp.zeros((rows, width), jnp.float32)
    for place, column in enumerate(columns):
        result = jnp.where(lane == place, column, result)
    return result


def loss_weights(dots, stats):
    inverse = lax.rsqrt(stats[:, 0:3] + epsilon)
    inv_q, inv_p, inv_h = inverse[:, 0:1], inverse[:, 1:2], inverse[:, 2:3]
    scores = dots * inv_q
    positive = stats[:, 3:4] * inv_q * inv_p
    hard = stats[:, 4:5] * inv_q * inv_h
    weight = score_scale * jax.nn.sigmoid(score_scale * (scores - positive + margin_value))
    weight = weight.astype(jnp.bfloat16)
    wide = weight.astype(jnp.float32)
    hard_weight = score_scale * jax.nn.sigmoid(score_scale * (hard - positive + margin_value))
    hard_weight = hard_weight.astype(jnp.bfloat16).astype(jnp.float32)
    total = jnp.sum(wide, axis=1, keepdims=True) + hard_weight
    along = jnp.sum(wide * scores, axis=1, keepdims=True) + hard_weight * hard - total * positive
    return weight, [inv_q, inv_p, inv_h, hard_weight, total, along, positive, hard]


def item_side(hood, pos, hard, scalars):
    f32, bf16 = jnp.float32, jnp.bfloat16
    inv_q, inv_p, inv_h, hard_weight, total, along, pos_score, hard_score = [
        scalars[:, i : i + 1] for i in range(8)
    ]
    query_unit, pos_unit, hard_unit = hood * inv_q, pos * inv_p, hard * inv_h
    query_float = query_unit.astype(bf16).astype(f32)
    known_grad = hard_weight * hard_unit.astype(bf16).astype(
        f32
    ) - total * pos_unit.astype(bf16).astype(f32)
    pos_grad = -total * (query_float - pos_unit * pos_score) * inv_p
    hard_grad = hard_weight * (query_float - hard_unit * hard_score) * inv_h
    return query_unit, query_float, known_grad, pos_grad, hard_grad


def kernel(
    sizes,
    table_hbm,
    projection_hbm,
    owner_line,
    row_line,
    visit_line,
    neg_line,
    out,
    table,
    projection,
    lines,
    info,
    slope,
    early,
    norms,
    norms_all,
    neg_all,
    feats,
    pre,
    act,
    info_all,
    rows,
    slices,
    picks,
    picked,
    partial,
    parts,
    stats,
    stats_all,
    weight_all,
    scalar_all,
    flipped,
    back,
    core_in,
    across,
    across_in,
    turned,
    landed,
    pre_grad,
    send_sem,
    recv_sem,
    local_sem,
):
    shards, slot_count, node_count, neg_count, query_count = sizes
    f32, bf16 = jnp.float32, jnp.bfloat16
    width = slices.shape[3]
    embed_width = projection_hbm.shape[1]
    node_part, neg_part = node_count // 4, neg_count // 4
    part = node_part + neg_part
    group = query_count * shards
    me, rep = lax.axis_index("shard"), lax.axis_index("rep")
    x, core = rep // 2, rep % 2
    mine, half = 2 * core + x, 2 * core
    crossed = 2 * core + 1 - x
    x_peer = (me, (1 - x) * 2 + core)
    core_peer = (me, x * 2 + 1 - core)
    peers = [lax.rem(me + k, shards) for k in range(shards)]
    sources = [lax.rem(me + shards - k, shards) for k in range(shards)]
    sent = []
    tile = 2 * width
    tiles = embed_width // tile
    loads = [pltpu.make_async_copy(table_hbm, table, local_sem.at[tiles])]
    for t in range(tiles):
        columns = pl.ds(t * tile, tile)
        loads.append(
            pltpu.make_async_copy(
                projection_hbm.at[:, columns], projection.at[t], local_sem.at[t]
            )
        )
    for load in loads:
        load.start()

    def send(source, target, device):
        sem = len(sent)
        copy = pltpu.make_async_remote_copy(
            src_ref=source,
            dst_ref=target,
            send_sem=send_sem.at[sem],
            recv_sem=recv_sem.at[sem],
            device_id=device,
            device_id_type=MESH,
        )
        copy.start()
        sent.append(copy)
        return copy

    drained = [0]

    def drain(count):
        for copy in sent[drained[0] : count]:
            copy.wait_send()
        drained[0] = count

    barrier = pltpu.get_barrier_semaphore()
    for k in range(1, shards):
        pl.semaphore_signal(barrier, inc=1, device_id=(peers[k], rep), device_id_type=MESH)
    for device in (x_peer, core_peer):
        pl.semaphore_signal(barrier, inc=1, device_id=device, device_id_type=MESH)

    lines[...] = jnp.zeros(lines.shape, f32)
    lines[0:slot_count, 0:query_count] = owner_line[...].astype(f32)
    lines[slot_count : 2 * slot_count, 0:query_count] = row_line[...].astype(f32)
    lines[2 * slot_count : 3 * slot_count - 3, 0:query_count] = visit_line[...].astype(f32)
    lines[3 * slot_count : 3 * slot_count + 1, 0:neg_count] = neg_line[...].astype(f32)
    columns = jnp.transpose(lines[...])
    info[...] = columns[0:query_count]
    neg_column = columns[0:neg_count, 3 * slot_count : 3 * slot_count + 1].astype(jnp.int32)
    neg_pick = (
        lax.broadcasted_iota(jnp.int32, (neg_count, node_count), 1) == neg_column
    ).astype(bf16)
    loads[0].wait()
    neg_feat = dot(neg_pick, table[...]).astype(bf16)
    for b in range(4):
        feats[b * part : b * part + node_part] = table[b * node_part : (b + 1) * node_part]
        feats[b * part + node_part : (b + 1) * part] = neg_feat[b * neg_part : (b + 1) * neg_part]
    pl.semaphore_wait(barrier, shards + 1)

    own_rows = pl.ds(pl.multiple_of(me * query_count, query_count), query_count)
    info_copies = [
        send(info, info_all.at[own_rows], (peers[k], rep)) for k in range(1, shards)
    ]
    info_all[own_rows] = info[...]
    base = shards
    squares = jnp.zeros((4 * part, 1), f32)
    for load in loads[1:]:
        load.wait()
    slice_copies = []
    for k in list(range(1, shards)) + [0]:
        columns = pl.ds(pl.multiple_of(peers[k] * width, width), width)
        within = pl.ds(pl.multiple_of(peers[k] % 2 * width, width), width)
        values = dot(feats[...], projection[peers[k] // 2, :, within])
        pre[:, :, columns] = values.reshape(4, part, width)
        values = values * jax.nn.sigmoid(values)
        squares = squares + jnp.sum(values * values, axis=1, keepdims=True)
        values = values.reshape(4, part, width)
        act[:, :, columns] = values
        if k:
            rows[k] = values.astype(bf16)
            slice_copies.append(send(rows.at[k, mine], slices.at[me, mine], (peers[k], rep)))
        else:
            slices[me] = values.astype(bf16)
    inverse = lax.rsqrt(squares.reshape(4, part, 1)[:, node_part:] + epsilon)
    inverse = inverse.reshape(neg_count, 1)
    if neg_count < 128:
        inverse = jnp.concatenate([inverse, jnp.zeros((128 - neg_count, 1), f32)], axis=0)
    inverse = jnp.transpose(jnp.broadcast_to(inverse, (128, 128)))
    norms[...] = inverse[0:8]
    norms_all[me] = inverse[0:8]
    norm_copies = [send(norms, norms_all.at[me], (peers[k], rep)) for k in range(1, shards)]

    for copy in info_copies:
        copy.wait_recv()
    block = 16

    chunks = node_count // width
    zero = jnp.zeros((block, width), bf16)
    lane = lax.broadcasted_iota(jnp.int32, (block, width), 1)
    lanes = [(lane + c * width).astype(f32).astype(bf16) for c in range(chunks)]

    def pick_rows(step, carry):
        here = pl.ds(pl.multiple_of(step * block, block), block)
        ids = info_all[here]

        def wide(column):
            return jnp.broadcast_to(ids[:, column : column + 1], (block, width)).astype(bf16)

        def hits(slot, amount):
            owner, row = wide(slot), wide(slot_count + slot)
            found = [row == place for place in lanes]
            for shard in range(shards):
                held = jnp.where(owner == jnp.asarray(shard, bf16), amount, zero)
                for c in range(chunks):
                    yield shard * chunks + c, jnp.where(found[c], held, zero)

        for slot in range(3):
            for place, value in hits(slot, jnp.ones((block, width), bf16)):
                picks[slot, here, place * width : (place + 1) * width] = value
        spread = [zero] * (shards * chunks)
        for slot in range(3, slot_count):
            for place, value in hits(slot, wide(2 * slot_count + slot - 3)):
                spread[place] = spread[place] + value
        for place, value in enumerate(spread):
            picks[3, here, place * width : (place + 1) * width] = value
        return carry

    over_x, over_core, twice = {}, {}, {}

    def pass_on(k):
        slice_copies[k - 1].wait_recv()
        piece = slices.at[sources[k], mine]
        over_x[k] = send(piece, piece, x_peer)
        over_core[k] = send(piece, piece, core_peer)

    def pass_twice(k):
        over_x[k].wait_recv()
        piece = slices.at[sources[k], crossed]
        twice[k] = send(piece, piece, core_peer)

    def gather_from(k):
        source = sources[k]
        if k:
            over_core[k].wait_recv()
            twice[k].wait_recv()
        columns = pl.ds(pl.multiple_of(source * node_count, node_count), node_count)
        values = slices[source, :, :node_part].reshape(node_count, width)
        for kind in range(4):
            part_sum = dot(picks[kind, :, columns], values)
            picked[kind] = picked[kind] + part_sum if k else part_sum

    steps = group // block
    last = shards - 1
    lax.fori_loop(0, steps // 2, pick_rows, 0)
    for k in range(1, shards // 2):
        pass_on(k)
    lax.fori_loop(steps // 2, steps - steps // 4, pick_rows, 0)
    for k in range(shards // 2, shards):
        pass_on(k)
        pass_twice(k - shards // 2 + 1)
    lax.fori_loop(steps - steps // 4, steps, pick_rows, 0)
    for k in range(shards):
        if k + shards // 2 < last:
            pass_twice(k + shards // 2 + 1)
        gather_from(k)
    for copy in norm_copies:
        copy.wait_recv()
    inverse = [norms_all[s, 0:1] for s in range(shards)]
    inverse = jnp.transpose(
        jnp.concatenate(inverse + [jnp.zeros((128 - shards, 128), f32)], axis=0)
    )
    for s in range(shards):
        values = slices[s, :, node_part:].reshape(neg_count, width).astype(f32)
        values = values * inverse[0:neg_count, s : s + 1]
        neg_all[s * neg_count : (s + 1) * neg_count] = values.astype(bf16)
    neg_slice = neg_all[...]
    counts = info_all[:, 2 * slot_count : 3 * slot_count - 3]
    visit_total = jnp.sum(counts, axis=1, keepdims=True)
    hood = picked[0] + picked[3] / visit_total
    pos, hard = picked[1], picked[2]
    partial[...] = dot(hood.astype(bf16), neg_slice, 1, 1).astype(bf16)
    pairs = ((hood, hood), (pos, pos), (hard, hard), (hood, pos), (hood, hard))
    part_rows = query_count // 2

    def half_rows(owner, h):
        start = owner * query_count + h * part_rows
        return pl.ds(pl.multiple_of(start, part_rows), part_rows)

    def send_half(h):
        there = pl.ds(h * part_rows, part_rows)
        return [
            send(partial.at[half_rows(peers[k], h)], parts.at[k, there], (peers[k], rep))
            for k in range(1, shards)
        ]

    score_copies = [send_half(0)]
    stats[...] = lanes_of([jnp.sum(a * b, axis=1, keepdims=True) for a, b in pairs], width)
    stat_copies = []
    for k in range(1, shards):
        there = pl.ds(pl.multiple_of(peers[k] * query_count, query_count), query_count)
        stat_copies.append(send(stats.at[there], stats_all.at[k], (peers[k], rep)))
    score_copies.append(send_half(1))
    slope[...] = silu_slope(pre[mine])
    neg_unit = act[mine, node_part:]
    inverse = lax.rsqrt(jnp.sum(neg_unit * neg_unit, axis=1, keepdims=True) + epsilon)
    neg_unit = neg_unit * inverse
    drain(len(sent) - 3 * (shards - 1))
    sums = stats[own_rows]
    for copy in stat_copies:
        copy.wait_recv()
    for k in range(1, shards):
        sums = sums + stats_all[k]
    weight_copies, copies = [], []
    for h in range(2):
        there = half_rows(me, h)
        dots = partial[there].astype(f32)
        for copy in score_copies[h]:
            copy.wait_recv()
        held = slice(h * part_rows, (h + 1) * part_rows)
        for k in range(1, shards):
            dots = dots + parts[k, held].astype(f32)
        weight, scalars = loss_weights(dots, sums[held])
        weight_all[there] = weight
        scalar_all[there] = lanes_of(scalars, width)
        if h:
            copies = [
                send(scalar_all.at[own_rows], scalar_all.at[own_rows], (peers[k], rep))
                for k in range(1, shards)
            ]
        for k in range(1, shards):
            weight_copies.append(
                send(weight_all.at[there], weight_all.at[there], (peers[k], rep))
            )
    for copy in copies:
        copy.wait_recv()
    scalars = scalar_all[...]
    side = item_side(hood, pos, hard, scalars)
    query_unit, query_float, known_grad, pos_grad, hard_grad = side
    flipped[:, 0:group] = jnp.transpose(pos_grad).astype(bf16)
    flipped[:, group : 2 * group] = jnp.transpose(hard_grad).astype(bf16)
    query_flipped = jnp.transpose(query_float).astype(bf16)

    def early_block(s, carry):
        columns = pl.ds(pl.multiple_of(s * node_count, node_count), node_count)
        early[s] = dot(flipped[:, 0:group], picks[1, :, columns]) + dot(
            flipped[:, group : 2 * group], picks[2, :, columns]
        )
        return carry

    lax.fori_loop(0, shards, early_block, 0)
    drain(len(sent) - 3 * (shards - 1))
    for copy in weight_copies:
        copy.wait_recv()

    weight = weight_all[...]
    along, inv_q = scalars[:, 5:6], scalars[:, 0:1]
    hood_grad = (dot(weight, neg_slice) + known_grad - query_unit * along) * inv_q
    flipped[:, 2 * group : 3 * group] = jnp.transpose(hood_grad).astype(bf16)
    flipped[:, 3 * group :] = jnp.transpose(hood_grad / visit_total).astype(bf16)
    neg_grad = jnp.transpose(dot(query_flipped, weight))
    back[:, :, node_part:] = neg_grad.reshape(shards, 4, neg_part, width)
    other = pl.ds(2 - half, 2)
    order = list(range(1, shards)) + [0]
    core_copies, x_copies, row_copies = {}, {}, {}

    def to_core(k):
        s = peers[k]
        columns = pl.ds(pl.multiple_of(s * node_count, node_count), node_count)
        total = early[s] + dot(flipped[:, 2 * group : 3 * group], picks[0, :, columns])
        total = total + dot(flipped[:, 3 * group :], picks[3, :, columns])
        back[s, :, :node_part] = jnp.transpose(total).reshape(4, node_part, width)
        core_copies[k] = send(back.at[s, other], core_in.at[s], core_peer)

    def to_x(k):
        s = peers[k]
        core_copies[k].wait_recv()
        across[s] = (back[s, crossed] + core_in[s, 1 - x]).astype(bf16)
        x_copies[k] = send(across.at[s], across_in.at[s], x_peer)

    def to_holder(k):
        s = peers[k]
        x_copies[k].wait_recv()
        total = back[s, mine] + core_in[s, x] + across_in[s].astype(f32)
        if k:
            turned[k] = total.astype(bf16)
            row_copies[k] = send(turned.at[k], landed.at[me], (s, rep))
        else:
            landed[me] = total.astype(bf16)

    lag = 3
    for step in range(shards + lag):
        if step < shards:
            to_core(order[step])
        if step >= lag:
            to_x(order[step - lag])
    for k in order:
        to_holder(k)

    home = [0] + list(range(1, shards))
    to_x_peer, to_core_peer, passed = [], [], []
    for k in home:
        if k:
            row_copies[k].wait_recv()
        s = sources[k]
        columns = pl.ds(pl.multiple_of(s * width, width), width)
        values = landed[s, :node_part].astype(f32) * slope[:node_part, columns]
        pre_grad[s, mine, :node_part] = values.astype(bf16)
        piece = pre_grad.at[s, mine, pl.ds(0, node_part)]
        to_x_peer.append(send(piece, piece, x_peer))
        to_core_peer.append(send(piece, piece, core_peer))
    neg_back = jnp.concatenate(
        [landed[s, node_part:].astype(f32) for s in range(shards)], axis=1
    )
    neg_back = neg_back - neg_unit * jnp.sum(neg_unit * neg_back, axis=1, keepdims=True)
    neg_back = (neg_back * inverse * slope[node_part:]).astype(bf16)
    for s in range(shards):
        pre_grad[s, mine, node_part:] = neg_back[:, s * width : (s + 1) * width]
    piece = pre_grad.at[:, mine, pl.ds(node_part, neg_part)]
    to_x_peer.append(send(piece, piece, x_peer))
    to_core_peer.append(send(piece, piece, core_peer))
    for k in home:
        to_x_peer[k].wait_recv()
        piece = pre_grad.at[sources[k], crossed, pl.ds(0, node_part)]
        passed.append(send(piece, piece, core_peer))
    to_x_peer[shards].wait_recv()
    piece = pre_grad.at[:, crossed, pl.ds(node_part, neg_part)]
    passed.append(send(piece, piece, core_peer))
    drain(len(sent) - len(to_x_peer + to_core_peer + passed))
    placed = (
        lax.broadcasted_iota(jnp.int32, (node_count, neg_count), 0) == neg_line[...]
    ).astype(bf16)
    for copy in to_core_peer + passed:
        copy.wait_recv()
    node_grad = jnp.concatenate(
        [pre_grad[s, :, :node_part].reshape(node_count, width) for s in range(shards)], axis=1
    )
    neg_grad = jnp.concatenate(
        [pre_grad[s, :, node_part:].reshape(neg_count, width) for s in range(shards)], axis=1
    )
    out[...] = (node_grad.astype(f32) + dot(placed, neg_grad)).astype(bf16)
    drain(len(sent))


def column_split(feature_table, projection, slot_owner, slot_row, visits, neg_row):
    shards = lax.axis_size("shard")
    query_count, slot_count = slot_row.shape
    node_count, feat_width = feature_table.shape
    neg_count = neg_row.shape[0]
    embed_width = projection.shape[1]
    width = embed_width // shards
    group = query_count * shards
    part = (node_count + neg_count) // 4
    f32, bf16 = jnp.float32, jnp.bfloat16
    owner_line = jnp.transpose(slot_owner, (1, 2, 0)).reshape(slot_count, query_count)
    sizes = (shards, slot_count, node_count, neg_count, query_count)
    sems = 19 * shards
    tiles = embed_width // (2 * width)
    hbm = pl.BlockSpec(memory_space=pl.ANY)
    vmem = pl.BlockSpec(memory_space=pltpu.VMEM)
    pre_grad = pl.pallas_call(
        functools.partial(kernel, sizes),
        out_shape=jax.ShapeDtypeStruct((node_count, embed_width), bf16),
        in_specs=[hbm] * 2 + [vmem] * 4,
        out_specs=vmem,
        scratch_shapes=[
            pltpu.VMEM((node_count, feat_width), bf16),
            pltpu.VMEM((tiles, feat_width, 2 * width), bf16),
            pltpu.VMEM((128, 128), f32),
            pltpu.VMEM((query_count, width), f32),
            pltpu.VMEM((part, embed_width), f32),
            pltpu.VMEM((shards, width, node_count), f32),
            pltpu.VMEM((8, 128), f32),
            pltpu.VMEM((shards, 8, 128), f32),
            pltpu.VMEM((shards * neg_count, width), bf16),
            pltpu.VMEM((4 * part, feat_width), bf16),
            pltpu.VMEM((4, part, embed_width), f32),
            pltpu.VMEM((4, part, embed_width), f32),
            pltpu.VMEM((group, width), f32),
            pltpu.VMEM((shards, 4, part, width), bf16),
            pltpu.VMEM((shards, 4, part, width), bf16),
            pltpu.VMEM((4, group, shards * node_count), bf16),
            pltpu.VMEM((4, group, width), f32),
            pltpu.VMEM((group, shards * neg_count), bf16),
            pltpu.VMEM((shards, query_count, shards * neg_count), bf16),
            pltpu.VMEM((group, width), f32),
            pltpu.VMEM((shards, query_count, width), f32),
            pltpu.VMEM((group, shards * neg_count), bf16),
            pltpu.VMEM((group, width), f32),
            pltpu.VMEM((width, 4 * group), bf16),
            pltpu.VMEM((shards, 4, part, width), f32),
            pltpu.VMEM((shards, 2, part, width), f32),
            pltpu.VMEM((shards, part, width), bf16),
            pltpu.VMEM((shards, part, width), bf16),
            pltpu.VMEM((shards, part, width), bf16),
            pltpu.VMEM((shards, part, width), bf16),
            pltpu.VMEM((shards, 4, part, width), bf16),
            pltpu.SemaphoreType.DMA((sems,)),
            pltpu.SemaphoreType.DMA((sems,)),
            pltpu.SemaphoreType.DMA((tiles + 1,)),
        ],
        compiler_params=pltpu.CompilerParams(
            collective_id=0, has_side_effects=True, vmem_limit_bytes=56 * 1024 * 1024
        ),
    )(
        feature_table,
        projection,
        owner_line,
        jnp.transpose(slot_row),
        jnp.transpose(visits),
        neg_row.reshape(1, neg_count),
    )
    return times_back(pre_grad, projection)


def solution(mesh):
    shards, reps = mesh.shape["shard"], mesh.shape["rep"]

    def body(feature_table, projection, slot_owner, slot_row, visits, neg_row):
        width = projection.shape[1] // shards
        parts = (feature_table.shape[0], neg_row.shape[0], slot_row.shape[0] * 2)
        small = slot_row.shape[0] <= 128 and neg_row.shape[0] <= 128 and slot_row.shape[1] <= 40
        small = small and shards <= 128 and feature_table.shape[0] in (width, 2 * width)
        whole = width == 128 and reps == 4 and small and all(size % 64 == 0 for size in parts)
        form = column_split if whole else on_device
        return form(feature_table, projection, slot_owner, slot_row, visits, neg_row)

    return jax.shard_map(
        body,
        mesh=mesh,
        in_specs=(
            P("shard", None),
            P(),
            P(("shard", "rep"), None, None),
            P(("shard", "rep"), None),
            P(("shard", "rep"), None),
            P("shard"),
        ),
        out_specs=P("shard", None),
        check_vma=False,
    )
```

```python
import functools

import jax
import jax.numpy as jnp
from jax import lax
from jax.experimental import pallas as pl
from jax.experimental.pallas import tpu as pltpu
from jax.sharding import PartitionSpec as P

MESH = pl.DeviceIdType.MESH

score_scale = 8.0
margin_value = 0.1
epsilon = 1e-06


def unit_rows(values):
    norms = jnp.sqrt(jnp.sum(values * values, axis=-1, keepdims=True) + epsilon)
    return (values / norms, norms)


def unit_back(grads, unit, norms):
    return (grads - unit * jnp.sum(unit * grads, axis=-1, keepdims=True)) / norms


def silu_slope(preact):
    gate_value = jax.nn.sigmoid(preact)
    return gate_value * (1.0 + preact * (1.0 - gate_value))


def times_back(left, projection):
    return jnp.einsum("re,fe->rf", left, projection, preferred_element_type=jnp.float32)


def on_device(feature_table, projection, slot_owner, slot_row, visits, neg_row):
    shard_count = lax.axis_size("shard")
    query_count, slot_count = slot_row.shape
    row_count = query_count * slot_count
    capacity = 2 * row_count // shard_count
    feat_width = projection.shape[0]
    embed_width = projection.shape[1]
    owners = slot_owner.reshape(row_count)
    one_hot = (owners[:, None] == jnp.arange(shard_count, dtype=jnp.int32)[None, :]).astype(
        jnp.int32
    )
    earlier = jnp.cumsum(one_hot, axis=0) - one_hot
    slot_rank = jnp.sum(earlier * one_hot, axis=1)
    position = owners * capacity + slot_rank
    send_ids = (
        jnp.zeros((shard_count * capacity,), jnp.int32)
        .at[position]
        .set(slot_row.reshape(row_count))
    )
    send_ids = send_ids.reshape(shard_count, capacity)
    asked = lax.all_to_all(send_ids, "shard", split_axis=0, concat_axis=0, tiled=True)
    picked = feature_table[asked]
    fetched = lax.all_to_all(picked, "shard", split_axis=0, concat_axis=0, tiled=True)
    gathered = fetched.reshape(shard_count * capacity, feat_width)[position]
    neg_pre = jnp.dot(feature_table[neg_row], projection, preferred_element_type=jnp.float32)
    neg_unit, neg_norms = unit_rows(jax.nn.silu(neg_pre))
    neg_embed = lax.all_gather(neg_unit.astype(jnp.bfloat16), "shard", axis=0, tiled=True)
    visit_float = visits.astype(jnp.float32)
    coefs = visit_float / jnp.sum(visit_float, axis=1, keepdims=True)
    preact = jnp.dot(gathered, projection, preferred_element_type=jnp.float32).reshape(
        query_count, slot_count, embed_width
    )
    active = jax.nn.silu(preact)
    hood = active[:, 0] + jnp.einsum("bk,bke->be", coefs, active[:, 3:])
    query_unit, query_norms = unit_rows(hood)
    query_embed = query_unit.astype(jnp.bfloat16)
    item_unit, item_norms = unit_rows(active[:, 1:3])
    item_embed = item_unit.astype(jnp.bfloat16)
    query_float = query_embed.astype(jnp.float32)
    item_float = item_embed.astype(jnp.float32)
    neg_scores = jnp.einsum("be,ne->bn", query_embed, neg_embed, preferred_element_type=jnp.float32)
    pair_scores = jnp.sum(query_float[:, None, :] * item_float, axis=2)
    positive = pair_scores[:, 0:1]
    neg_weight = (
        score_scale * jax.nn.sigmoid(score_scale * (neg_scores - positive + margin_value))
    ).astype(jnp.bfloat16)
    hard_weight = (
        score_scale * jax.nn.sigmoid(score_scale * (pair_scores[:, 1:2] - positive + margin_value))
    ).astype(jnp.bfloat16)
    hard_float = hard_weight.astype(jnp.float32)
    total_weight = jnp.sum(neg_weight.astype(jnp.float32), axis=1, keepdims=True) + hard_float
    query_grad = (
        jnp.dot(neg_weight, neg_embed, preferred_element_type=jnp.float32)
        + hard_float * item_float[:, 1]
        - total_weight * item_float[:, 0]
    )
    item_grad = jnp.stack([-total_weight * query_float, hard_float * query_float], axis=1)
    neg_partial = jnp.einsum(
        "bn,be->ne", neg_weight, query_embed, preferred_element_type=jnp.float32
    )
    hood_grad = unit_back(query_grad, query_unit, query_norms)
    item_back = unit_back(item_grad, item_unit, item_norms)
    active_grad = jnp.concatenate(
        [hood_grad[:, None], item_back, coefs[:, :, None] * hood_grad[:, None]], axis=1
    )
    preact_grad = (
        (active_grad * silu_slope(preact)).astype(jnp.bfloat16).reshape(row_count, embed_width)
    )
    outgoing = (
        jnp.zeros((shard_count * capacity, embed_width), jnp.bfloat16).at[position].set(preact_grad)
    )
    incoming = lax.all_to_all(
        outgoing.reshape(shard_count, capacity, embed_width),
        "shard",
        split_axis=0,
        concat_axis=0,
        tiled=True,
    )
    contrib = times_back(incoming.reshape(shard_count * capacity, embed_width), projection)
    neg_sum = lax.psum_scatter(neg_partial, "shard", scatter_dimension=0, tiled=True)
    grad_local = (
        jnp.zeros((feature_table.shape[0], feat_width), jnp.float32)
        .at[asked.reshape(-1)]
        .add(contrib)
    )
    grad_local, neg_total = lax.psum((grad_local, neg_sum), "rep")
    neg_back = unit_back(neg_total, neg_unit, neg_norms)
    neg_pre_grad = (neg_back * silu_slope(neg_pre)).astype(jnp.bfloat16)
    neg_rows = times_back(neg_pre_grad, projection)
    return grad_local.at[neg_row].add(neg_rows)


def dot(left, right, left_dim=1, right_dim=0):
    return lax.dot_general(
        left, right, (((left_dim,), (right_dim,)), ((), ())), preferred_element_type=jnp.float32
    )


def lanes_of(columns, width):
    rows = columns[0].shape[0]
    lane = lax.broadcasted_iota(jnp.int32, (rows, width), 1)
    result = jnp.zeros((rows, width), jnp.float32)
    for place, column in enumerate(columns):
        result = jnp.where(lane == place, column, result)
    return result


def loss_weights(dots, stats):
    inverse = lax.rsqrt(stats[:, 0:3] + epsilon)
    inv_q, inv_p, inv_h = inverse[:, 0:1], inverse[:, 1:2], inverse[:, 2:3]
    scores = dots * inv_q
    positive = stats[:, 3:4] * inv_q * inv_p
    hard = stats[:, 4:5] * inv_q * inv_h
    weight = score_scale * jax.nn.sigmoid(score_scale * (scores - positive + margin_value))
    weight = weight.astype(jnp.bfloat16)
    wide = weight.astype(jnp.float32)
    hard_weight = score_scale * jax.nn.sigmoid(score_scale * (hard - positive + margin_value))
    hard_weight = hard_weight.astype(jnp.bfloat16).astype(jnp.float32)
    total = jnp.sum(wide, axis=1, keepdims=True) + hard_weight
    along = jnp.sum(wide * scores, axis=1, keepdims=True) + hard_weight * hard - total * positive
    return weight, [inv_q, inv_p, inv_h, hard_weight, total, along, positive, hard]


def item_side(hood, pos, hard, scalars):
    f32, bf16 = jnp.float32, jnp.bfloat16
    inv_q, inv_p, inv_h, hard_weight, total, along, pos_score, hard_score = [
        scalars[:, i : i + 1] for i in range(8)
    ]
    query_unit, pos_unit, hard_unit = hood * inv_q, pos * inv_p, hard * inv_h
    query_float = query_unit.astype(bf16).astype(f32)
    known_grad = hard_weight * hard_unit.astype(bf16).astype(
        f32
    ) - total * pos_unit.astype(bf16).astype(f32)
    pos_grad = -total * (query_float - pos_unit * pos_score) * inv_p
    hard_grad = hard_weight * (query_float - hard_unit * hard_score) * inv_h
    return query_unit, query_float, known_grad, pos_grad, hard_grad


def kernel(
    sizes,
    table_hbm,
    projection_hbm,
    owner_line,
    row_line,
    visit_line,
    neg_line,
    out,
    table,
    projection,
    lines,
    info,
    slope,
    early,
    norms,
    norms_all,
    own_scalars,
    scalars_in,
    neg_all,
    feats,
    pre,
    act,
    info_all,
    rows,
    slices,
    picks,
    picked,
    partial,
    parts,
    stats,
    stats_all,
    weight_all,
    scalar_all,
    flipped,
    back,
    core_in,
    across,
    across_in,
    turned,
    landed,
    pre_grad,
    send_sem,
    recv_sem,
    local_sem,
):
    shards, slot_count, node_count, neg_count, query_count = sizes
    f32, bf16 = jnp.float32, jnp.bfloat16
    width = slices.shape[3]
    embed_width = projection_hbm.shape[1]
    node_part, neg_part = node_count // 4, neg_count // 4
    part = node_part + neg_part
    group = query_count * shards
    me, rep = lax.axis_index("shard"), lax.axis_index("rep")
    x, core = rep // 2, rep % 2
    mine, half = 2 * core + x, 2 * core
    crossed = 2 * core + 1 - x
    x_peer = (me, (1 - x) * 2 + core)
    core_peer = (me, x * 2 + 1 - core)
    peers = [lax.rem(me + k, shards) for k in range(shards)]
    sources = [lax.rem(me + shards - k, shards) for k in range(shards)]
    sent = []
    tile = 2 * width
    tiles = embed_width // tile
    loads = [pltpu.make_async_copy(table_hbm, table, local_sem.at[tiles])]
    for t in range(tiles):
        columns = pl.ds(t * tile, tile)
        loads.append(
            pltpu.make_async_copy(
                projection_hbm.at[:, columns], projection.at[t], local_sem.at[t]
            )
        )
    for load in loads:
        load.start()

    def send(source, target, device):
        sem = len(sent)
        copy = pltpu.make_async_remote_copy(
            src_ref=source,
            dst_ref=target,
            send_sem=send_sem.at[sem],
            recv_sem=recv_sem.at[sem],
            device_id=device,
            device_id_type=MESH,
        )
        copy.start()
        sent.append(copy)
        return copy

    drained = [0]

    def drain(count):
        for copy in sent[drained[0] : count]:
            copy.wait_send()
        drained[0] = count

    barrier = pltpu.get_barrier_semaphore()
    for k in range(1, shards):
        pl.semaphore_signal(barrier, inc=1, device_id=(peers[k], rep), device_id_type=MESH)
    for device in (x_peer, core_peer):
        pl.semaphore_signal(barrier, inc=1, device_id=device, device_id_type=MESH)

    lines[...] = jnp.zeros(lines.shape, f32)
    lines[0:slot_count, 0:query_count] = owner_line[...].astype(f32)
    lines[slot_count : 2 * slot_count, 0:query_count] = row_line[...].astype(f32)
    lines[2 * slot_count : 3 * slot_count - 3, 0:query_count] = visit_line[...].astype(f32)
    lines[3 * slot_count : 3 * slot_count + 1, 0:neg_count] = neg_line[...].astype(f32)
    columns = jnp.transpose(lines[...])
    info[...] = columns[0:query_count].astype(bf16)
    neg_column = columns[0:neg_count, 3 * slot_count : 3 * slot_count + 1].astype(jnp.int32)
    neg_pick = (
        lax.broadcasted_iota(jnp.int32, (neg_count, node_count), 1) == neg_column
    ).astype(bf16)
    loads[0].wait()
    neg_feat = dot(neg_pick, table[...]).astype(bf16)
    for b in range(4):
        feats[b * part : b * part + node_part] = table[b * node_part : (b + 1) * node_part]
        feats[b * part + node_part : (b + 1) * part] = neg_feat[b * neg_part : (b + 1) * neg_part]
    pl.semaphore_wait(barrier, shards + 1)

    own_rows = pl.ds(pl.multiple_of(me * query_count, query_count), query_count)
    info_copies = [
        send(info, info_all.at[own_rows], (peers[k], rep)) for k in range(1, shards)
    ]
    info_all[own_rows] = info[...]
    base = shards
    squares = jnp.zeros((4 * part, 1), f32)
    for load in loads[1:]:
        load.wait()
    slice_copies = []
    for k in list(range(1, shards)) + [0]:
        columns = pl.ds(pl.multiple_of(peers[k] * width, width), width)
        within = pl.ds(pl.multiple_of(peers[k] % 2 * width, width), width)
        values = dot(feats[...], projection[peers[k] // 2, :, within])
        pre[:, :, columns] = values.reshape(4, part, width)
        values = values * jax.nn.sigmoid(values)
        squares = squares + jnp.sum(values * values, axis=1, keepdims=True)
        values = values.reshape(4, part, width)
        act[:, :, columns] = values
        if k:
            rows[k] = values.astype(bf16)
            slice_copies.append(send(rows.at[k, mine], slices.at[me, mine], (peers[k], rep)))
        else:
            slices[me] = values.astype(bf16)
    inverse = lax.rsqrt(squares.reshape(4, part, 1)[:, node_part:] + epsilon)
    inverse = inverse.reshape(neg_count, 1)
    if neg_count < 128:
        inverse = jnp.concatenate([inverse, jnp.zeros((128 - neg_count, 1), f32)], axis=0)
    inverse = jnp.transpose(jnp.broadcast_to(inverse, (128, 128)))
    norms[...] = inverse[0:8]
    norms_all[me] = inverse[0:8]
    norm_copies = [send(norms, norms_all.at[me], (peers[k], rep)) for k in range(1, shards)]

    for copy in info_copies:
        copy.wait_recv()
    block = 16

    chunks = node_count // width
    zero = jnp.zeros((block, width), bf16)
    lane = lax.broadcasted_iota(jnp.int32, (block, width), 1)
    lanes = [(lane + c * width).astype(f32).astype(bf16) for c in range(chunks)]

    def pick_rows(step, carry):
        here = pl.ds(pl.multiple_of(step * block, block), block)
        ids = info_all[here].astype(f32)

        def wide(column):
            return jnp.broadcast_to(ids[:, column : column + 1], (block, width)).astype(bf16)

        def hits(slot, amount):
            owner, row = wide(slot), wide(slot_count + slot)
            found = [row == place for place in lanes]
            for shard in range(shards):
                held = jnp.where(owner == jnp.asarray(shard, bf16), amount, zero)
                for c in range(chunks):
                    yield shard * chunks + c, jnp.where(found[c], held, zero)

        for slot in range(3):
            for place, value in hits(slot, jnp.ones((block, width), bf16)):
                picks[slot, here, place * width : (place + 1) * width] = value
        spread = [zero] * (shards * chunks)
        for slot in range(3, slot_count):
            for place, value in hits(slot, wide(2 * slot_count + slot - 3)):
                spread[place] = spread[place] + value
        for place, value in enumerate(spread):
            picks[3, here, place * width : (place + 1) * width] = value
        return carry

    over_x, over_core, twice = {}, {}, {}

    def pass_on(k):
        slice_copies[k - 1].wait_recv()
        piece = slices.at[sources[k], mine]
        over_x[k] = send(piece, piece, x_peer)
        over_core[k] = send(piece, piece, core_peer)

    def pass_twice(k):
        over_x[k].wait_recv()
        piece = slices.at[sources[k], crossed]
        twice[k] = send(piece, piece, core_peer)

    def gather_from(k):
        source = sources[k]
        if k:
            over_core[k].wait_recv()
            twice[k].wait_recv()
        columns = pl.ds(pl.multiple_of(source * node_count, node_count), node_count)
        values = slices[source, :, :node_part].reshape(node_count, width)
        for kind in range(4):
            part_sum = dot(picks[kind, :, columns], values)
            picked[kind] = picked[kind] + part_sum if k else part_sum

    steps = group // block
    last = shards - 1
    lax.fori_loop(0, steps // 2, pick_rows, 0)
    for k in range(1, shards // 2):
        pass_on(k)
    lax.fori_loop(steps // 2, steps - steps // 4, pick_rows, 0)
    for k in range(shards // 2, shards):
        pass_on(k)
        pass_twice(k - shards // 2 + 1)
    lax.fori_loop(steps - steps // 4, steps, pick_rows, 0)
    for k in range(shards):
        if k + shards // 2 < last:
            pass_twice(k + shards // 2 + 1)
        gather_from(k)
    for copy in norm_copies:
        copy.wait_recv()
    inverse = [norms_all[s, 0:1] for s in range(shards)]
    inverse = jnp.transpose(
        jnp.concatenate(inverse + [jnp.zeros((128 - shards, 128), f32)], axis=0)
    )
    for s in range(shards):
        values = slices[s, :, node_part:].reshape(neg_count, width).astype(f32)
        values = values * inverse[0:neg_count, s : s + 1]
        neg_all[s * neg_count : (s + 1) * neg_count] = values.astype(bf16)
    neg_slice = neg_all[...]
    counts = info_all[...].astype(f32)[:, 2 * slot_count : 3 * slot_count - 3]
    visit_total = jnp.sum(counts, axis=1, keepdims=True)
    hood = picked[0] + picked[3] / visit_total
    pos, hard = picked[1], picked[2]
    partial[...] = dot(hood.astype(bf16), neg_slice, 1, 1).astype(bf16)
    pairs = ((hood, hood), (pos, pos), (hard, hard), (hood, pos), (hood, hard))
    part_rows = query_count // 2

    def half_rows(owner, h):
        start = owner * query_count + h * part_rows
        return pl.ds(pl.multiple_of(start, part_rows), part_rows)

    def send_half(h):
        there = pl.ds(h * part_rows, part_rows)
        return [
            send(partial.at[half_rows(peers[k], h)], parts.at[k, there], (peers[k], rep))
            for k in range(1, shards)
        ]

    score_copies = [send_half(0)]
    flat = jnp.transpose(
        lanes_of([jnp.sum(a * b, axis=1, keepdims=True) for a, b in pairs], width)
    )
    rest = jnp.zeros((8, 128 - query_count), f32)
    for s in range(shards):
        stats[s] = jnp.concatenate(
            [flat[0:8, s * query_count : (s + 1) * query_count], rest], axis=1
        )
    stat_copies = []
    for k in range(1, shards):
        stat_copies.append(send(stats.at[peers[k]], stats_all.at[k], (peers[k], rep)))
    score_copies.append(send_half(1))
    slope[...] = silu_slope(pre[mine])
    neg_unit = act[mine, node_part:]
    inverse = lax.rsqrt(jnp.sum(neg_unit * neg_unit, axis=1, keepdims=True) + epsilon)
    neg_unit = neg_unit * inverse
    drain(len(sent) - 3 * (shards - 1))
    sums = stats[me]
    for copy in stat_copies:
        copy.wait_recv()
    for k in range(1, shards):
        sums = sums + stats_all[k]
    sums = jnp.transpose(jnp.concatenate([sums, jnp.zeros((120, 128), f32)], axis=0))
    weight_copies, copies, halves = [], [], []
    for h in range(2):
        there = half_rows(me, h)
        dots = partial[there].astype(f32)
        for copy in score_copies[h]:
            copy.wait_recv()
        held = slice(h * part_rows, (h + 1) * part_rows)
        for k in range(1, shards):
            dots = dots + parts[k, held].astype(f32)
        weight, scalars = loss_weights(dots, sums[held])
        weight_all[there] = weight
        halves.append(lanes_of(scalars, 128))
        if h:
            rest = jnp.zeros((128 - query_count, 128), f32)
            flat = jnp.transpose(jnp.concatenate(halves + [rest], axis=0))
            own_scalars[...] = flat[0:8]
            scalars_in[me] = flat[0:8]
            copies = [
                send(own_scalars, scalars_in.at[me], (peers[k], rep)) for k in range(1, shards)
            ]
        for k in range(1, shards):
            weight_copies.append(
                send(weight_all.at[there], weight_all.at[there], (peers[k], rep))
            )
    for copy in copies:
        copy.wait_recv()
    flat = [scalars_in[s] for s in range(shards)]
    if shards < 16:
        flat.append(jnp.zeros((128 - 8 * shards, 128), f32))
    flat = jnp.transpose(jnp.concatenate(flat, axis=0))
    for s in range(shards):
        scalar_all[s * query_count : (s + 1) * query_count, 0:8] = flat[
            0:query_count, s * 8 : (s + 1) * 8
        ]
    scalars = scalar_all[:, 0:8]
    side = item_side(hood, pos, hard, scalars)
    query_unit, query_float, known_grad, pos_grad, hard_grad = side
    flipped[:, 0:group] = jnp.transpose(pos_grad).astype(bf16)
    flipped[:, group : 2 * group] = jnp.transpose(hard_grad).astype(bf16)
    query_flipped = jnp.transpose(query_float).astype(bf16)

    def early_block(s, carry):
        columns = pl.ds(pl.multiple_of(s * node_count, node_count), node_count)
        early[s] = dot(flipped[:, 0:group], picks[1, :, columns]) + dot(
            flipped[:, group : 2 * group], picks[2, :, columns]
        )
        return carry

    lax.fori_loop(0, shards, early_block, 0)
    drain(len(sent) - 3 * (shards - 1))
    for copy in weight_copies:
        copy.wait_recv()

    weight = weight_all[...]
    along, inv_q = scalars[:, 5:6], scalars[:, 0:1]
    hood_grad = (dot(weight, neg_slice) + known_grad - query_unit * along) * inv_q
    flipped[:, 2 * group : 3 * group] = jnp.transpose(hood_grad).astype(bf16)
    flipped[:, 3 * group :] = jnp.transpose(hood_grad / visit_total).astype(bf16)
    neg_grad = jnp.transpose(dot(query_flipped, weight))
    back[:, :, node_part:] = neg_grad.reshape(shards, 4, neg_part, width)
    other = pl.ds(2 - half, 2)
    order = list(range(1, shards)) + [0]
    core_copies, x_copies, row_copies = {}, {}, {}

    def to_core(k):
        s = peers[k]
        columns = pl.ds(pl.multiple_of(s * node_count, node_count), node_count)
        total = early[s] + dot(flipped[:, 2 * group : 3 * group], picks[0, :, columns])
        total = total + dot(flipped[:, 3 * group :], picks[3, :, columns])
        back[s, :, :node_part] = jnp.transpose(total).reshape(4, node_part, width)
        core_copies[k] = send(back.at[s, other], core_in.at[s], core_peer)

    def to_x(k):
        s = peers[k]
        core_copies[k].wait_recv()
        across[s] = (back[s, crossed] + core_in[s, 1 - x]).astype(bf16)
        x_copies[k] = send(across.at[s], across_in.at[s], x_peer)

    def to_holder(k):
        s = peers[k]
        x_copies[k].wait_recv()
        total = back[s, mine] + core_in[s, x] + across_in[s].astype(f32)
        if k:
            turned[k] = total.astype(bf16)
            row_copies[k] = send(turned.at[k], landed.at[me], (s, rep))
        else:
            landed[me] = total.astype(bf16)

    lag = 3
    for step in range(shards + lag):
        if step < shards:
            to_core(order[step])
        if step >= lag:
            to_x(order[step - lag])
    for k in order:
        to_holder(k)

    home = [0] + list(range(1, shards))
    to_x_peer, to_core_peer, passed = [], [], []
    for k in home:
        if k:
            row_copies[k].wait_recv()
        s = sources[k]
        columns = pl.ds(pl.multiple_of(s * width, width), width)
        values = landed[s, :node_part].astype(f32) * slope[:node_part, columns]
        pre_grad[s, mine, :node_part] = values.astype(bf16)
        piece = pre_grad.at[s, mine, pl.ds(0, node_part)]
        to_x_peer.append(send(piece, piece, x_peer))
        to_core_peer.append(send(piece, piece, core_peer))
    neg_back = jnp.concatenate(
        [landed[s, node_part:].astype(f32) for s in range(shards)], axis=1
    )
    neg_back = neg_back - neg_unit * jnp.sum(neg_unit * neg_back, axis=1, keepdims=True)
    neg_back = (neg_back * inverse * slope[node_part:]).astype(bf16)
    for s in range(shards):
        pre_grad[s, mine, node_part:] = neg_back[:, s * width : (s + 1) * width]
    piece = pre_grad.at[:, mine, pl.ds(node_part, neg_part)]
    to_x_peer.append(send(piece, piece, x_peer))
    to_core_peer.append(send(piece, piece, core_peer))
    for k in home:
        to_x_peer[k].wait_recv()
        piece = pre_grad.at[sources[k], crossed, pl.ds(0, node_part)]
        passed.append(send(piece, piece, core_peer))
    to_x_peer[shards].wait_recv()
    piece = pre_grad.at[:, crossed, pl.ds(node_part, neg_part)]
    passed.append(send(piece, piece, core_peer))
    drain(len(sent) - len(to_x_peer + to_core_peer + passed))
    placed = (
        lax.broadcasted_iota(jnp.int32, (node_count, neg_count), 0) == neg_line[...]
    ).astype(bf16)
    for copy in to_core_peer + passed:
        copy.wait_recv()
    node_grad = jnp.concatenate(
        [pre_grad[s, :, :node_part].reshape(node_count, width) for s in range(shards)], axis=1
    )
    neg_grad = jnp.concatenate(
        [pre_grad[s, :, node_part:].reshape(neg_count, width) for s in range(shards)], axis=1
    )
    out[...] = (node_grad.astype(f32) + dot(placed, neg_grad)).astype(bf16)
    drain(len(sent))


def column_split(feature_table, projection, slot_owner, slot_row, visits, neg_row):
    shards = lax.axis_size("shard")
    query_count, slot_count = slot_row.shape
    node_count, feat_width = feature_table.shape
    neg_count = neg_row.shape[0]
    embed_width = projection.shape[1]
    width = embed_width // shards
    group = query_count * shards
    part = (node_count + neg_count) // 4
    f32, bf16 = jnp.float32, jnp.bfloat16
    owner_line = jnp.transpose(slot_owner, (1, 2, 0)).reshape(slot_count, query_count)
    sizes = (shards, slot_count, node_count, neg_count, query_count)
    sems = 19 * shards
    tiles = embed_width // (2 * width)
    hbm = pl.BlockSpec(memory_space=pl.ANY)
    vmem = pl.BlockSpec(memory_space=pltpu.VMEM)
    pre_grad = pl.pallas_call(
        functools.partial(kernel, sizes),
        out_shape=jax.ShapeDtypeStruct((node_count, embed_width), bf16),
        in_specs=[hbm] * 2 + [vmem] * 4,
        out_specs=vmem,
        scratch_shapes=[
            pltpu.VMEM((node_count, feat_width), bf16),
            pltpu.VMEM((tiles, feat_width, 2 * width), bf16),
            pltpu.VMEM((128, 128), f32),
            pltpu.VMEM((query_count, width), bf16),
            pltpu.VMEM((part, embed_width), f32),
            pltpu.VMEM((shards, width, node_count), f32),
            pltpu.VMEM((8, 128), f32),
            pltpu.VMEM((shards, 8, 128), f32),
            pltpu.VMEM((8, 128), f32),
            pltpu.VMEM((shards, 8, 128), f32),
            pltpu.VMEM((shards * neg_count, width), bf16),
            pltpu.VMEM((4 * part, feat_width), bf16),
            pltpu.VMEM((4, part, embed_width), f32),
            pltpu.VMEM((4, part, embed_width), f32),
            pltpu.VMEM((group, width), bf16),
            pltpu.VMEM((shards, 4, part, width), bf16),
            pltpu.VMEM((shards, 4, part, width), bf16),
            pltpu.VMEM((4, group, shards * node_count), bf16),
            pltpu.VMEM((4, group, width), f32),
            pltpu.VMEM((group, shards * neg_count), bf16),
            pltpu.VMEM((shards, query_count, shards * neg_count), bf16),
            pltpu.VMEM((shards, 8, 128), f32),
            pltpu.VMEM((shards, 8, 128), f32),
            pltpu.VMEM((group, shards * neg_count), bf16),
            pltpu.VMEM((group, width), f32),
            pltpu.VMEM((width, 4 * group), bf16),
            pltpu.VMEM((shards, 4, part, width), f32),
            pltpu.VMEM((shards, 2, part, width), f32),
            pltpu.VMEM((shards, part, width), bf16),
            pltpu.VMEM((shards, part, width), bf16),
            pltpu.VMEM((shards, part, width), bf16),
            pltpu.VMEM((shards, part, width), bf16),
            pltpu.VMEM((shards, 4, part, width), bf16),
            pltpu.SemaphoreType.DMA((sems,)),
            pltpu.SemaphoreType.DMA((sems,)),
            pltpu.SemaphoreType.DMA((tiles + 1,)),
        ],
        compiler_params=pltpu.CompilerParams(
            collective_id=0, has_side_effects=True, vmem_limit_bytes=56 * 1024 * 1024
        ),
    )(
        feature_table,
        projection,
        owner_line,
        jnp.transpose(slot_row),
        jnp.transpose(visits),
        neg_row.reshape(1, neg_count),
    )
    return times_back(pre_grad, projection)


def solution(mesh):
    shards, reps = mesh.shape["shard"], mesh.shape["rep"]

    def body(feature_table, projection, slot_owner, slot_row, visits, neg_row):
        width = projection.shape[1] // shards
        parts = (feature_table.shape[0], neg_row.shape[0], slot_row.shape[0] * 2)
        small = slot_row.shape[0] < 128 and neg_row.shape[0] <= 128 and slot_row.shape[1] <= 40
        small = small and shards <= 16 and feature_table.shape[0] in (width, 2 * width)
        whole = width == 128 and reps == 4 and small and all(size % 64 == 0 for size in parts)
        form = column_split if whole else on_device
        return form(feature_table, projection, slot_owner, slot_row, visits, neg_row)

    return jax.shard_map(
        body,
        mesh=mesh,
        in_specs=(
            P("shard", None),
            P(),
            P(("shard", "rep"), None, None),
            P(("shard", "rep"), None),
            P(("shard", "rep"), None),
            P("shard"),
        ),
        out_specs=P("shard", None),
        check_vma=False,
    )
```

```python
import functools

import jax
import jax.numpy as jnp
from jax import lax
from jax.experimental import pallas as pl
from jax.experimental.pallas import tpu as pltpu
from jax.sharding import PartitionSpec as P

MESH = pl.DeviceIdType.MESH

score_scale = 8.0
margin_value = 0.1
epsilon = 1e-06


def unit_rows(values):
    norms = jnp.sqrt(jnp.sum(values * values, axis=-1, keepdims=True) + epsilon)
    return (values / norms, norms)


def unit_back(grads, unit, norms):
    return (grads - unit * jnp.sum(unit * grads, axis=-1, keepdims=True)) / norms


def silu_slope(preact):
    gate_value = jax.nn.sigmoid(preact)
    return gate_value * (1.0 + preact * (1.0 - gate_value))


def times_back(left, projection):
    return jnp.einsum("re,fe->rf", left, projection, preferred_element_type=jnp.float32)


def on_device(feature_table, projection, slot_owner, slot_row, visits, neg_row):
    shard_count = lax.axis_size("shard")
    query_count, slot_count = slot_row.shape
    row_count = query_count * slot_count
    capacity = 2 * row_count // shard_count
    feat_width = projection.shape[0]
    embed_width = projection.shape[1]
    owners = slot_owner.reshape(row_count)
    one_hot = (owners[:, None] == jnp.arange(shard_count, dtype=jnp.int32)[None, :]).astype(
        jnp.int32
    )
    earlier = jnp.cumsum(one_hot, axis=0) - one_hot
    slot_rank = jnp.sum(earlier * one_hot, axis=1)
    position = owners * capacity + slot_rank
    send_ids = (
        jnp.zeros((shard_count * capacity,), jnp.int32)
        .at[position]
        .set(slot_row.reshape(row_count))
    )
    send_ids = send_ids.reshape(shard_count, capacity)
    asked = lax.all_to_all(send_ids, "shard", split_axis=0, concat_axis=0, tiled=True)
    picked = feature_table[asked]
    fetched = lax.all_to_all(picked, "shard", split_axis=0, concat_axis=0, tiled=True)
    gathered = fetched.reshape(shard_count * capacity, feat_width)[position]
    neg_pre = jnp.dot(feature_table[neg_row], projection, preferred_element_type=jnp.float32)
    neg_unit, neg_norms = unit_rows(jax.nn.silu(neg_pre))
    neg_embed = lax.all_gather(neg_unit.astype(jnp.bfloat16), "shard", axis=0, tiled=True)
    visit_float = visits.astype(jnp.float32)
    coefs = visit_float / jnp.sum(visit_float, axis=1, keepdims=True)
    preact = jnp.dot(gathered, projection, preferred_element_type=jnp.float32).reshape(
        query_count, slot_count, embed_width
    )
    active = jax.nn.silu(preact)
    hood = active[:, 0] + jnp.einsum("bk,bke->be", coefs, active[:, 3:])
    query_unit, query_norms = unit_rows(hood)
    query_embed = query_unit.astype(jnp.bfloat16)
    item_unit, item_norms = unit_rows(active[:, 1:3])
    item_embed = item_unit.astype(jnp.bfloat16)
    query_float = query_embed.astype(jnp.float32)
    item_float = item_embed.astype(jnp.float32)
    neg_scores = jnp.einsum("be,ne->bn", query_embed, neg_embed, preferred_element_type=jnp.float32)
    pair_scores = jnp.sum(query_float[:, None, :] * item_float, axis=2)
    positive = pair_scores[:, 0:1]
    neg_weight = (
        score_scale * jax.nn.sigmoid(score_scale * (neg_scores - positive + margin_value))
    ).astype(jnp.bfloat16)
    hard_weight = (
        score_scale * jax.nn.sigmoid(score_scale * (pair_scores[:, 1:2] - positive + margin_value))
    ).astype(jnp.bfloat16)
    hard_float = hard_weight.astype(jnp.float32)
    total_weight = jnp.sum(neg_weight.astype(jnp.float32), axis=1, keepdims=True) + hard_float
    query_grad = (
        jnp.dot(neg_weight, neg_embed, preferred_element_type=jnp.float32)
        + hard_float * item_float[:, 1]
        - total_weight * item_float[:, 0]
    )
    item_grad = jnp.stack([-total_weight * query_float, hard_float * query_float], axis=1)
    neg_partial = jnp.einsum(
        "bn,be->ne", neg_weight, query_embed, preferred_element_type=jnp.float32
    )
    hood_grad = unit_back(query_grad, query_unit, query_norms)
    item_back = unit_back(item_grad, item_unit, item_norms)
    active_grad = jnp.concatenate(
        [hood_grad[:, None], item_back, coefs[:, :, None] * hood_grad[:, None]], axis=1
    )
    preact_grad = (
        (active_grad * silu_slope(preact)).astype(jnp.bfloat16).reshape(row_count, embed_width)
    )
    outgoing = (
        jnp.zeros((shard_count * capacity, embed_width), jnp.bfloat16).at[position].set(preact_grad)
    )
    incoming = lax.all_to_all(
        outgoing.reshape(shard_count, capacity, embed_width),
        "shard",
        split_axis=0,
        concat_axis=0,
        tiled=True,
    )
    contrib = times_back(incoming.reshape(shard_count * capacity, embed_width), projection)
    neg_sum = lax.psum_scatter(neg_partial, "shard", scatter_dimension=0, tiled=True)
    grad_local = (
        jnp.zeros((feature_table.shape[0], feat_width), jnp.float32)
        .at[asked.reshape(-1)]
        .add(contrib)
    )
    grad_local, neg_total = lax.psum((grad_local, neg_sum), "rep")
    neg_back = unit_back(neg_total, neg_unit, neg_norms)
    neg_pre_grad = (neg_back * silu_slope(neg_pre)).astype(jnp.bfloat16)
    neg_rows = times_back(neg_pre_grad, projection)
    return grad_local.at[neg_row].add(neg_rows)


def dot(left, right, left_dim=1, right_dim=0):
    return lax.dot_general(
        left, right, (((left_dim,), (right_dim,)), ((), ())), preferred_element_type=jnp.float32
    )


def lanes_of(columns, width):
    rows = columns[0].shape[0]
    lane = lax.broadcasted_iota(jnp.int32, (rows, width), 1)
    result = jnp.zeros((rows, width), jnp.float32)
    for place, column in enumerate(columns):
        result = jnp.where(lane == place, column, result)
    return result


def pack_lines(tile, start, count):
    each = 128 // count
    lines = []
    for i in range(0, 8, each):
        pieces = [tile[i + j : i + j + 1, start : start + count] for j in range(each)]
        lines.append(jnp.concatenate(pieces, axis=1))
    return jnp.concatenate(lines, axis=0)


def unpack_lines(packed, count):
    each = 128 // count
    pieces = [
        packed[i // each : i // each + 1, i % each * count : (i % each + 1) * count]
        for i in range(8)
    ]
    lines = jnp.concatenate(pieces, axis=0)
    return jnp.concatenate([lines, jnp.zeros((8, 128 - count), jnp.float32)], axis=1)


def loss_weights(dots, stats):
    inverse = lax.rsqrt(stats[:, 0:3] + epsilon)
    inv_q, inv_p, inv_h = inverse[:, 0:1], inverse[:, 1:2], inverse[:, 2:3]
    scores = dots * inv_q
    positive = stats[:, 3:4] * inv_q * inv_p
    hard = stats[:, 4:5] * inv_q * inv_h
    weight = score_scale * jax.nn.sigmoid(score_scale * (scores - positive + margin_value))
    weight = weight.astype(jnp.bfloat16)
    wide = weight.astype(jnp.float32)
    hard_weight = score_scale * jax.nn.sigmoid(score_scale * (hard - positive + margin_value))
    hard_weight = hard_weight.astype(jnp.bfloat16).astype(jnp.float32)
    total = jnp.sum(wide, axis=1, keepdims=True) + hard_weight
    along = jnp.sum(wide * scores, axis=1, keepdims=True) + hard_weight * hard - total * positive
    return weight, [inv_q, inv_p, inv_h, hard_weight, total, along, positive, hard]


def item_side(hood, pos, hard, scalars):
    f32, bf16 = jnp.float32, jnp.bfloat16
    inv_q, inv_p, inv_h, hard_weight, total, along, pos_score, hard_score = [
        scalars[:, i : i + 1] for i in range(8)
    ]
    query_unit, pos_unit, hard_unit = hood * inv_q, pos * inv_p, hard * inv_h
    query_float = query_unit.astype(bf16).astype(f32)
    known_grad = hard_weight * hard_unit.astype(bf16).astype(
        f32
    ) - total * pos_unit.astype(bf16).astype(f32)
    pos_grad = -total * (query_float - pos_unit * pos_score) * inv_p
    hard_grad = hard_weight * (query_float - hard_unit * hard_score) * inv_h
    return query_unit, query_float, known_grad, pos_grad, hard_grad


def kernel(
    sizes,
    table_hbm,
    projection_hbm,
    owner_line,
    row_line,
    visit_line,
    neg_line,
    out,
    table,
    projection,
    lines,
    info,
    info_in,
    slope,
    early,
    norms,
    norms_all,
    own_scalars,
    scalars_in,
    neg_all,
    feats,
    pre,
    act,
    info_all,
    rows,
    slices,
    picks,
    picked,
    partial,
    parts,
    stats,
    stats_all,
    weight_all,
    scalar_all,
    flipped,
    back,
    core_in,
    across,
    across_in,
    turned,
    landed,
    pre_grad,
    send_sem,
    recv_sem,
    local_sem,
):
    shards, slot_count, node_count, neg_count, query_count = sizes
    f32, bf16 = jnp.float32, jnp.bfloat16
    width = slices.shape[3]
    embed_width = projection_hbm.shape[1]
    node_part, neg_part = node_count // 4, neg_count // 4
    part = node_part + neg_part
    group = query_count * shards
    me, rep = lax.axis_index("shard"), lax.axis_index("rep")
    x, core = rep // 2, rep % 2
    mine, half = 2 * core + x, 2 * core
    crossed = 2 * core + 1 - x
    x_peer = (me, (1 - x) * 2 + core)
    core_peer = (me, x * 2 + 1 - core)
    peers = [lax.rem(me + k, shards) for k in range(shards)]
    sources = [lax.rem(me + shards - k, shards) for k in range(shards)]
    sent = []
    tile = 2 * width
    tiles = embed_width // tile
    loads = [pltpu.make_async_copy(table_hbm, table, local_sem.at[tiles])]
    for t in range(tiles):
        columns = pl.ds(t * tile, tile)
        loads.append(
            pltpu.make_async_copy(
                projection_hbm.at[:, columns], projection.at[t], local_sem.at[t]
            )
        )
    for load in loads:
        load.start()

    def send(source, target, device):
        sem = len(sent)
        copy = pltpu.make_async_remote_copy(
            src_ref=source,
            dst_ref=target,
            send_sem=send_sem.at[sem],
            recv_sem=recv_sem.at[sem],
            device_id=device,
            device_id_type=MESH,
        )
        copy.start()
        sent.append(copy)
        return copy

    drained = [0]

    def drain(count):
        for copy in sent[drained[0] : count]:
            copy.wait_send()
        drained[0] = count

    barrier = pltpu.get_barrier_semaphore()
    for k in range(1, shards):
        pl.semaphore_signal(barrier, inc=1, device_id=(peers[k], rep), device_id_type=MESH)
    for device in (x_peer, core_peer):
        pl.semaphore_signal(barrier, inc=1, device_id=device, device_id_type=MESH)

    gap = jnp.zeros((3, query_count), f32)
    pieces = [
        owner_line[...].astype(f32),
        row_line[...].astype(f32),
        jnp.concatenate([visit_line[...].astype(f32), gap], axis=0),
        jnp.zeros((slot_count, 128 - 3 * query_count), f32),
    ]
    info[...] = jnp.concatenate(pieces, axis=1).astype(bf16)
    lines[...] = jnp.zeros(lines.shape, f32)
    lines[0:1, 0:neg_count] = neg_line[...].astype(f32)
    neg_column = jnp.transpose(lines[...])[0:neg_count, 0:1].astype(jnp.int32)
    neg_pick = (
        lax.broadcasted_iota(jnp.int32, (neg_count, node_count), 1) == neg_column
    ).astype(bf16)
    loads[0].wait()
    neg_feat = dot(neg_pick, table[...]).astype(bf16)
    for b in range(4):
        feats[b * part : b * part + node_part] = table[b * node_part : (b + 1) * node_part]
        feats[b * part + node_part : (b + 1) * part] = neg_feat[b * neg_part : (b + 1) * neg_part]
    pl.semaphore_wait(barrier, shards + 1)

    own_rows = pl.ds(pl.multiple_of(me * query_count, query_count), query_count)
    info_copies = [
        send(info, info_in.at[me], (peers[k], rep)) for k in range(1, shards)
    ]
    info_in[me] = info[...]
    base = shards
    squares = jnp.zeros((4 * part, 1), f32)
    for load in loads[1:]:
        load.wait()
    slice_copies = []
    for k in list(range(1, shards)) + [0]:
        columns = pl.ds(pl.multiple_of(peers[k] * width, width), width)
        within = pl.ds(pl.multiple_of(peers[k] % 2 * width, width), width)
        values = dot(feats[...], projection[peers[k] // 2, :, within])
        pre[:, :, columns] = values.reshape(4, part, width)
        values = values * jax.nn.sigmoid(values)
        squares = squares + jnp.sum(values * values, axis=1, keepdims=True)
        values = values.reshape(4, part, width)
        act[:, :, columns] = values
        if k:
            rows[k] = values.astype(bf16)
            slice_copies.append(send(rows.at[k, mine], slices.at[me, mine], (peers[k], rep)))
        else:
            slices[me] = values.astype(bf16)
    inverse = lax.rsqrt(squares.reshape(4, part, 1)[:, node_part:] + epsilon)
    inverse = inverse.reshape(neg_count, 1)
    if neg_count < 128:
        inverse = jnp.concatenate([inverse, jnp.zeros((128 - neg_count, 1), f32)], axis=0)
    inverse = jnp.transpose(jnp.broadcast_to(inverse, (128, 128)))
    norms[...] = inverse[0:1]
    norms_all[me] = inverse[0:1]
    norm_copies = [send(norms, norms_all.at[me], (peers[k], rep)) for k in range(1, shards)]

    for copy in info_copies:
        copy.wait_recv()
    turn = [info_in[s].astype(f32) for s in range(shards)]
    if shards * slot_count < 128:
        turn.append(jnp.zeros((128 - shards * slot_count, 128), f32))
    turn = jnp.transpose(jnp.concatenate(turn, axis=0))
    for s in range(shards):
        pieces = [
            turn[j * query_count : (j + 1) * query_count, s * slot_count : (s + 1) * slot_count]
            for j in range(3)
        ]
        pieces.append(jnp.zeros((query_count, width - 3 * slot_count), f32))
        info_all[s * query_count : (s + 1) * query_count] = jnp.concatenate(pieces, axis=1)
    block = 16

    chunks = node_count // width
    zero = jnp.zeros((block, width), bf16)
    lane = lax.broadcasted_iota(jnp.int32, (block, width), 1)
    lanes = [(lane + c * width).astype(f32).astype(bf16) for c in range(chunks)]

    def pick_rows(step, carry):
        here = pl.ds(pl.multiple_of(step * block, block), block)
        ids = info_all[here]

        def wide(column):
            return jnp.broadcast_to(ids[:, column : column + 1], (block, width)).astype(bf16)

        def hits(slot, amount):
            owner, row = wide(slot), wide(slot_count + slot)
            found = [row == place for place in lanes]
            for shard in range(shards):
                held = jnp.where(owner == jnp.asarray(shard, bf16), amount, zero)
                for c in range(chunks):
                    yield shard * chunks + c, jnp.where(found[c], held, zero)

        for slot in range(3):
            for place, value in hits(slot, jnp.ones((block, width), bf16)):
                picks[slot, here, place * width : (place + 1) * width] = value
        spread = [zero] * (shards * chunks)
        for slot in range(3, slot_count):
            for place, value in hits(slot, wide(2 * slot_count + slot - 3)):
                spread[place] = spread[place] + value
        for place, value in enumerate(spread):
            picks[3, here, place * width : (place + 1) * width] = value
        return carry

    over_x, over_core, twice = {}, {}, {}

    def pass_on(k):
        slice_copies[k - 1].wait_recv()
        piece = slices.at[sources[k], mine]
        over_x[k] = send(piece, piece, x_peer)
        over_core[k] = send(piece, piece, core_peer)

    def pass_twice(k):
        over_x[k].wait_recv()
        piece = slices.at[sources[k], crossed]
        twice[k] = send(piece, piece, core_peer)

    def gather_from(k):
        source = sources[k]
        if k:
            over_core[k].wait_recv()
            twice[k].wait_recv()
        columns = pl.ds(pl.multiple_of(source * node_count, node_count), node_count)
        values = slices[source, :, :node_part].reshape(node_count, width)
        for kind in range(4):
            part_sum = dot(picks[kind, :, columns], values)
            picked[kind] = picked[kind] + part_sum if k else part_sum

    steps = group // block
    last = shards - 1
    lax.fori_loop(0, steps // 2, pick_rows, 0)
    for k in range(1, shards // 2):
        pass_on(k)
    lax.fori_loop(steps // 2, steps - steps // 4, pick_rows, 0)
    for k in range(shards // 2, shards):
        pass_on(k)
        pass_twice(k - shards // 2 + 1)
    lax.fori_loop(steps - steps // 4, steps, pick_rows, 0)
    for k in range(shards):
        if k + shards // 2 < last:
            pass_twice(k + shards // 2 + 1)
        gather_from(k)
    for copy in norm_copies:
        copy.wait_recv()
    inverse = [norms_all[s] for s in range(shards)]
    inverse = jnp.transpose(
        jnp.concatenate(inverse + [jnp.zeros((128 - shards, 128), f32)], axis=0)
    )
    for s in range(shards):
        values = slices[s, :, node_part:].reshape(neg_count, width).astype(f32)
        values = values * inverse[0:neg_count, s : s + 1]
        neg_all[s * neg_count : (s + 1) * neg_count] = values.astype(bf16)
    neg_slice = neg_all[...]
    counts = info_all[:, 2 * slot_count : 3 * slot_count - 3]
    visit_total = jnp.sum(counts, axis=1, keepdims=True)
    hood = picked[0] + picked[3] / visit_total
    pos, hard = picked[1], picked[2]
    partial[...] = dot(hood.astype(bf16), neg_slice, 1, 1).astype(bf16)
    pairs = ((hood, hood), (pos, pos), (hard, hard), (hood, pos), (hood, hard))
    part_rows = query_count // 2

    def half_rows(owner, h):
        start = owner * query_count + h * part_rows
        return pl.ds(pl.multiple_of(start, part_rows), part_rows)

    def send_half(h):
        there = pl.ds(h * part_rows, part_rows)
        return [
            send(partial.at[half_rows(peers[k], h)], parts.at[k, there], (peers[k], rep))
            for k in range(1, shards)
        ]

    score_copies = [send_half(0)]
    flat = jnp.transpose(
        lanes_of([jnp.sum(a * b, axis=1, keepdims=True) for a, b in pairs], width)
    )
    for s in range(shards):
        stats[s] = pack_lines(flat, s * query_count, query_count)
    stat_copies = []
    for k in range(1, shards):
        stat_copies.append(send(stats.at[peers[k]], stats_all.at[k], (peers[k], rep)))
    score_copies.append(send_half(1))
    slope[...] = silu_slope(pre[mine])
    neg_unit = act[mine, node_part:]
    inverse = lax.rsqrt(jnp.sum(neg_unit * neg_unit, axis=1, keepdims=True) + epsilon)
    neg_unit = neg_unit * inverse
    drain(len(sent) - 3 * (shards - 1))
    sums = stats[me]
    for copy in stat_copies:
        copy.wait_recv()
    for k in range(1, shards):
        sums = sums + stats_all[k]
    sums = unpack_lines(sums, query_count)
    sums = jnp.transpose(jnp.concatenate([sums, jnp.zeros((120, 128), f32)], axis=0))
    weight_copies, copies, halves = [], [], []
    for h in range(2):
        there = half_rows(me, h)
        dots = partial[there].astype(f32)
        for copy in score_copies[h]:
            copy.wait_recv()
        held = slice(h * part_rows, (h + 1) * part_rows)
        for k in range(1, shards):
            dots = dots + parts[k, held].astype(f32)
        weight, scalars = loss_weights(dots, sums[held])
        weight_all[there] = weight
        halves.append(lanes_of(scalars, 128))
        if h:
            rest = jnp.zeros((128 - query_count, 128), f32)
            flat = jnp.transpose(jnp.concatenate(halves + [rest], axis=0))
            own_scalars[...] = pack_lines(flat, 0, query_count)
            scalars_in[me] = pack_lines(flat, 0, query_count)
            copies = [
                send(own_scalars, scalars_in.at[me], (peers[k], rep)) for k in range(1, shards)
            ]
        for k in range(1, shards):
            weight_copies.append(
                send(weight_all.at[there], weight_all.at[there], (peers[k], rep))
            )
    for copy in copies:
        copy.wait_recv()
    flat = [unpack_lines(scalars_in[s], query_count) for s in range(shards)]
    if shards < 16:
        flat.append(jnp.zeros((128 - 8 * shards, 128), f32))
    flat = jnp.transpose(jnp.concatenate(flat, axis=0))
    for s in range(shards):
        scalar_all[s * query_count : (s + 1) * query_count, 0:8] = flat[
            0:query_count, s * 8 : (s + 1) * 8
        ]
    scalars = scalar_all[:, 0:8]
    side = item_side(hood, pos, hard, scalars)
    query_unit, query_float, known_grad, pos_grad, hard_grad = side
    flipped[:, 0:group] = jnp.transpose(pos_grad).astype(bf16)
    flipped[:, group : 2 * group] = jnp.transpose(hard_grad).astype(bf16)
    query_flipped = jnp.transpose(query_float).astype(bf16)

    def early_block(s, carry):
        columns = pl.ds(pl.multiple_of(s * node_count, node_count), node_count)
        early[s] = dot(flipped[:, 0:group], picks[1, :, columns]) + dot(
            flipped[:, group : 2 * group], picks[2, :, columns]
        )
        return carry

    lax.fori_loop(0, shards, early_block, 0)
    drain(len(sent) - 3 * (shards - 1))
    for copy in weight_copies:
        copy.wait_recv()

    weight = weight_all[...]
    along, inv_q = scalars[:, 5:6], scalars[:, 0:1]
    hood_grad = (dot(weight, neg_slice) + known_grad - query_unit * along) * inv_q
    flipped[:, 2 * group : 3 * group] = jnp.transpose(hood_grad).astype(bf16)
    flipped[:, 3 * group :] = jnp.transpose(hood_grad / visit_total).astype(bf16)
    neg_grad = jnp.transpose(dot(query_flipped, weight))
    back[:, :, node_part:] = neg_grad.reshape(shards, 4, neg_part, width)
    other = pl.ds(2 - half, 2)
    order = list(range(1, shards)) + [0]
    core_copies, x_copies, row_copies = {}, {}, {}

    def to_core(k):
        s = peers[k]
        columns = pl.ds(pl.multiple_of(s * node_count, node_count), node_count)
        total = early[s] + dot(flipped[:, 2 * group : 3 * group], picks[0, :, columns])
        total = total + dot(flipped[:, 3 * group :], picks[3, :, columns])
        back[s, :, :node_part] = jnp.transpose(total).reshape(4, node_part, width)
        core_copies[k] = send(back.at[s, other], core_in.at[s], core_peer)

    def to_x(k):
        s = peers[k]
        core_copies[k].wait_recv()
        across[s] = (back[s, crossed] + core_in[s, 1 - x]).astype(bf16)
        x_copies[k] = send(across.at[s], across_in.at[s], x_peer)

    def to_holder(k):
        s = peers[k]
        x_copies[k].wait_recv()
        total = back[s, mine] + core_in[s, x] + across_in[s].astype(f32)
        if k:
            turned[k] = total.astype(bf16)
            row_copies[k] = send(turned.at[k], landed.at[me], (s, rep))
        else:
            landed[me] = total.astype(bf16)

    lag = 3
    for step in range(shards + lag):
        if step < shards:
            to_core(order[step])
        if step >= lag:
            to_x(order[step - lag])
    for k in order:
        to_holder(k)

    home = [0] + list(range(1, shards))
    to_x_peer, to_core_peer, passed = [], [], []
    for k in home:
        if k:
            row_copies[k].wait_recv()
        s = sources[k]
        columns = pl.ds(pl.multiple_of(s * width, width), width)
        values = landed[s, :node_part].astype(f32) * slope[:node_part, columns]
        pre_grad[s, mine, :node_part] = values.astype(bf16)
        piece = pre_grad.at[s, mine, pl.ds(0, node_part)]
        to_x_peer.append(send(piece, piece, x_peer))
        to_core_peer.append(send(piece, piece, core_peer))
    neg_back = jnp.concatenate(
        [landed[s, node_part:].astype(f32) for s in range(shards)], axis=1
    )
    neg_back = neg_back - neg_unit * jnp.sum(neg_unit * neg_back, axis=1, keepdims=True)
    neg_back = (neg_back * inverse * slope[node_part:]).astype(bf16)
    for s in range(shards):
        pre_grad[s, mine, node_part:] = neg_back[:, s * width : (s + 1) * width]
    piece = pre_grad.at[:, mine, pl.ds(node_part, neg_part)]
    to_x_peer.append(send(piece, piece, x_peer))
    to_core_peer.append(send(piece, piece, core_peer))
    for k in home:
        to_x_peer[k].wait_recv()
        piece = pre_grad.at[sources[k], crossed, pl.ds(0, node_part)]
        passed.append(send(piece, piece, core_peer))
    to_x_peer[shards].wait_recv()
    piece = pre_grad.at[:, crossed, pl.ds(node_part, neg_part)]
    passed.append(send(piece, piece, core_peer))
    drain(len(sent) - len(to_x_peer + to_core_peer + passed))
    placed = (
        lax.broadcasted_iota(jnp.int32, (node_count, neg_count), 0) == neg_line[...]
    ).astype(bf16)
    for copy in to_core_peer + passed:
        copy.wait_recv()
    node_grad = jnp.concatenate(
        [pre_grad[s, :, :node_part].reshape(node_count, width) for s in range(shards)], axis=1
    )
    neg_grad = jnp.concatenate(
        [pre_grad[s, :, node_part:].reshape(neg_count, width) for s in range(shards)], axis=1
    )
    out[...] = (node_grad.astype(f32) + dot(placed, neg_grad)).astype(bf16)
    drain(len(sent))


def column_split(feature_table, projection, slot_owner, slot_row, visits, neg_row):
    shards = lax.axis_size("shard")
    query_count, slot_count = slot_row.shape
    node_count, feat_width = feature_table.shape
    neg_count = neg_row.shape[0]
    embed_width = projection.shape[1]
    width = embed_width // shards
    group = query_count * shards
    part = (node_count + neg_count) // 4
    f32, bf16 = jnp.float32, jnp.bfloat16
    owner_line = jnp.transpose(slot_owner, (1, 2, 0)).reshape(slot_count, query_count)
    sizes = (shards, slot_count, node_count, neg_count, query_count)
    sems = 19 * shards
    tiles = embed_width // (2 * width)
    hbm = pl.BlockSpec(memory_space=pl.ANY)
    vmem = pl.BlockSpec(memory_space=pltpu.VMEM)
    pre_grad = pl.pallas_call(
        functools.partial(kernel, sizes),
        out_shape=jax.ShapeDtypeStruct((node_count, embed_width), bf16),
        in_specs=[hbm] * 2 + [vmem] * 4,
        out_specs=vmem,
        scratch_shapes=[
            pltpu.VMEM((node_count, feat_width), bf16),
            pltpu.VMEM((tiles, feat_width, 2 * width), bf16),
            pltpu.VMEM((128, 128), f32),
            pltpu.VMEM((slot_count, 128), bf16),
            pltpu.VMEM((shards, slot_count, 128), bf16),
            pltpu.VMEM((part, embed_width), f32),
            pltpu.VMEM((shards, width, node_count), f32),
            pltpu.VMEM((1, 128), f32),
            pltpu.VMEM((shards, 1, 128), f32),
            pltpu.VMEM((8 * query_count // 128, 128), f32),
            pltpu.VMEM((shards, 8 * query_count // 128, 128), f32),
            pltpu.VMEM((shards * neg_count, width), bf16),
            pltpu.VMEM((4 * part, feat_width), bf16),
            pltpu.VMEM((4, part, embed_width), f32),
            pltpu.VMEM((4, part, embed_width), f32),
            pltpu.VMEM((group, width), f32),
            pltpu.VMEM((shards, 4, part, width), bf16),
            pltpu.VMEM((shards, 4, part, width), bf16),
            pltpu.VMEM((4, group, shards * node_count), bf16),
            pltpu.VMEM((4, group, width), f32),
            pltpu.VMEM((group, shards * neg_count), bf16),
            pltpu.VMEM((shards, query_count, shards * neg_count), bf16),
            pltpu.VMEM((shards, 8 * query_count // 128, 128), f32),
            pltpu.VMEM((shards, 8 * query_count // 128, 128), f32),
            pltpu.VMEM((group, shards * neg_count), bf16),
            pltpu.VMEM((group, width), f32),
            pltpu.VMEM((width, 4 * group), bf16),
            pltpu.VMEM((shards, 4, part, width), f32),
            pltpu.VMEM((shards, 2, part, width), f32),
            pltpu.VMEM((shards, part, width), bf16),
            pltpu.VMEM((shards, part, width), bf16),
            pltpu.VMEM((shards, part, width), bf16),
            pltpu.VMEM((shards, part, width), bf16),
            pltpu.VMEM((shards, 4, part, width), bf16),
            pltpu.SemaphoreType.DMA((sems,)),
            pltpu.SemaphoreType.DMA((sems,)),
            pltpu.SemaphoreType.DMA((tiles + 1,)),
        ],
        compiler_params=pltpu.CompilerParams(
            collective_id=0, has_side_effects=True, vmem_limit_bytes=56 * 1024 * 1024
        ),
    )(
        feature_table,
        projection,
        owner_line,
        jnp.transpose(slot_row),
        jnp.transpose(visits),
        neg_row.reshape(1, neg_count),
    )
    return times_back(pre_grad, projection)


def solution(mesh):
    shards, reps = mesh.shape["shard"], mesh.shape["rep"]

    def body(feature_table, projection, slot_owner, slot_row, visits, neg_row):
        width = projection.shape[1] // shards
        parts = (feature_table.shape[0], neg_row.shape[0], slot_row.shape[0] * 2)
        small = slot_row.shape[0] < 128 and neg_row.shape[0] <= 128 and slot_row.shape[1] == 16
        small = small and shards <= 8 and 4 * slot_row.shape[0] == 128 and feature_table.shape[0] in (width, 2 * width)
        whole = width == 128 and reps == 4 and small and all(size % 64 == 0 for size in parts)
        form = column_split if whole else on_device
        return form(feature_table, projection, slot_owner, slot_row, visits, neg_row)

    return jax.shard_map(
        body,
        mesh=mesh,
        in_specs=(
            P("shard", None),
            P(),
            P(("shard", "rep"), None, None),
            P(("shard", "rep"), None),
            P(("shard", "rep"), None),
            P("shard"),
        ),
        out_specs=P("shard", None),
        check_vma=False,
    )
```
